32 devices in a mesh: dp: 16 (over z, y, x), mp: 2 (over core).
Axes of the slice: x: 2, y: 2, z: 4, core: 2. Of those that a mesh axis runs over, the one named last changes fastest.
Arguments:
- tokens: bfloat16 [36864, 768], P(('dp', 'mp')), may hold values from -6 to 6
- short_lengths: int32 [32], P(('dp', 'mp')), may hold values from 64 to 128, as said below
- long_lengths: int32 [32], P(('dp', 'mp')), may hold values from 512 to 1024, as said below
- cotangent: bfloat16 [36864, 768], P(('dp', 'mp')), may hold values from -6 to 6
- norm1_gain: float32 [768], replicated, may hold values from 0.5 to 1.5
- norm1_bias: float32 [768], replicated, may hold values from -2 to 2
- mixin_one: bfloat16 [4, 192, 4, 48], replicated, may hold values from -0.4375 to 0.4375
- mixin_two: bfloat16 [4, 48, 4, 576], replicated, may hold values from -0.4375 to 0.4375
- conv_taps: float32 [3, 2304], replicated, may hold values from -3 to 3
- skip_gain: float32 [768], replicated, may hold values from -4 to 4
- pos_in: float32 [5, 128], replicated, may hold values from -2.5 to 2.5
- pos_bias: float32 [128], replicated, may hold values from -3.140625 to 3.140625
- pos_out: float32 [128, 768], replicated, may hold values from -0.0625 to 0.0625
- mixout_one: bfloat16 [4, 192, 4, 48], replicated, may hold values from -0.4375 to 0.4375
- mixout_two: bfloat16 [4, 48, 4, 192], replicated, may hold values from -0.4375 to 0.4375
- norm2_gain: float32 [768], replicated, may hold values from 0.5 to 1.5
- norm2_bias: float32 [768], replicated, may hold values from -2 to 2
- gate_one: bfloat16 [4, 192, 4, 48], P(None, None, 'mp'), may hold values from -0.4375 to 0.4375
- gate_two: bfloat16 [4, 48, 4, 768], P('mp'), may hold values from -0.4375 to 0.4375
- up_one: bfloat16 [4, 192, 4, 48], P(None, None, 'mp'), may hold values from -0.4375 to 0.4375
- up_two: bfloat16 [4, 48, 4, 768], P('mp'), may hold values from -0.4375 to 0.4375
- down_one: bfloat16 [4, 768, 4, 48], P('mp'), may hold values from -0.21875 to 0.21875
- down_two: bfloat16 [4, 48, 4, 192], P(None, None, 'mp'), may hold values from -0.4375 to 0.4375
Outputs:
- result: bfloat16 [36864, 768], P(('dp', 'mp'))
- tokens_grad: bfloat16 [36864, 768], P(('dp', 'mp'))
- norm1_gain_grad: float32 [768], P('mp')
- norm1_bias_grad: float32 [768], P('mp')
- mixin_one_grad: float32 [4, 192, 4, 48], P('mp')
- mixin_two_grad: float32 [4, 48, 4, 576], P('mp')
- conv_taps_grad: float32 [3, 2304], P(None, 'mp')
- skip_gain_grad: float32 [768], P('mp')
- pos_in_grad: float32 [5, 128], P(None, 'mp')
- pos_bias_grad: float32 [128], P('mp')
- pos_out_grad: float32 [128, 768], P(None, 'mp')
- mixout_one_grad: float32 [4, 192, 4, 48], P('mp')
- mixout_two_grad: float32 [4, 48, 4, 192], P('mp')
- norm2_gain_grad: float32 [768], P('mp')
- norm2_bias_grad: float32 [768], P('mp')
- gate_one_grad: float32 [4, 192, 4, 48], P(None, None, 'mp')
- gate_two_grad: float32 [4, 48, 4, 768], P('mp')
- up_one_grad: float32 [4, 192, 4, 48], P(None, None, 'mp')
- up_two_grad: float32 [4, 48, 4, 768], P('mp')
- down_one_grad: float32 [4, 768, 4, 48], P('mp')
- down_two_grad: float32 [4, 48, 4, 192], P(None, None, 'mp')
The draws below stay inside these ranges and needn't reach their ends.
Inputs may be any that keep to these rules, and one draw needn't show every extreme that they name: `short_lengths`: on every draw some short sequence fills its whole slot. `long_lengths`: on every draw some long sequence fills its whole slot.
All inputs are finite; a program needn't handle non-finite values.
Results may differ from the reference program's by a relative error of at most 0.015.
Values may be sent and summed in bfloat16 or wider, within the bound.
No kernel may reach another device: no remote copies, remote signals or barrier semaphores. Data moves between devices by JAX's collectives and lax.ppermute only.
A program may use at most 384 MiB of HBM per device.

```python
import math
import jax
import jax.numpy as jnp
from jax import lax

D = 768
HIDDEN_SIZE = 3072
ORDER = 128
MONARCH = 4
INNER = 192
POS = 5
SHORT = 128
LONG = 1024
SHORT_DEV = 1
TOKENS = 36864
SHORT_SEQS = 32
LONG_SEQS = 32
N_DP = 16
N_MP = 2


def draw_short_lengths(key, part):
    key = jax.random.fold_in(key, 11)
    first_key, second_key = jax.random.split(key)
    drawn_lens = jax.random.randint(first_key, (SHORT_SEQS,), SHORT // 2, SHORT + 1)
    chosen = jax.random.randint(second_key, (), 0, SHORT_SEQS)
    return jnp.where(jnp.arange(SHORT_SEQS) == chosen, SHORT, drawn_lens).astype(jnp.int32)


def draw_long_lengths(key, part):
    key = jax.random.fold_in(key, 23)
    first_key, second_key = jax.random.split(key)
    drawn_lens = jax.random.randint(first_key, (LONG_SEQS,), LONG // 2, LONG + 1)
    chosen = jax.random.randint(second_key, (), 0, LONG_SEQS)
    return jnp.where(jnp.arange(LONG_SEQS) == chosen, LONG, drawn_lens).astype(jnp.int32)


def levels(rng, extent, shards, smallest, high):
    def one(position, shards_of):
        draws = jax.random.uniform(jax.random.fold_in(jax.random.fold_in(rng, 6), position), (shards_of,), jnp.float32, smallest / len(shards), high / len(shards))
        return jnp.repeat(jnp.exp(draws), extent[position] // shards_of).reshape((-1,) + (1,) * (len(extent) - position - 1))

    level = one(*shards[0])
    for cut in shards[1:]:
        level = level * one(*cut)
    return level


def bell_draw(rng, shape, width, reach, pieces=(), dtype=jnp.bfloat16):
    level = levels(rng, shape, pieces, -0.22, 0.18) if pieces else 1.0
    entries = jax.random.normal(rng, shape, jnp.float32) * width * level
    return jnp.minimum(jnp.maximum(entries, -reach), reach).astype(dtype)


def setup_inputs(seed: int = 0) -> dict:
    splits = jax.random.split(jax.random.key(seed), 24)
    tokens = bell_draw(splits[0], (TOKENS, D), 1.0, 6.0, ((0, 32),))
    short_lengths = draw_short_lengths(jax.random.fold_in(splits[23], 71), 0)
    long_lengths = draw_long_lengths(jax.random.fold_in(splits[23], 71), 0)
    cotangent = bell_draw(splits[3], (TOKENS, D), 1.0, 6.0, ((0, 32),))
    norm1_gain = jnp.clip(1.0 + 0.1 * jax.random.normal(splits[4], (D,), jnp.float32), 0.5, 1.5)
    norm1_bias = bell_draw(splits[5], (D,), 0.3, 2.0, (), jnp.float32)
    mixin_one = bell_draw(splits[6], (MONARCH, D // MONARCH, MONARCH, INNER // MONARCH), (D // MONARCH) ** -0.5, 0.4375)
    mixin_two = bell_draw(splits[7], (MONARCH, INNER // MONARCH, MONARCH, 3 * D // MONARCH), INNER ** -0.5, 0.4375)
    conv_taps = bell_draw(splits[8], (3, 3 * D), 0.6, 3.0, (), jnp.float32)
    skip_gain = bell_draw(splits[9], (D,), 1.0, 4.0, (), jnp.float32)
    pos_in = bell_draw(splits[10], (POS, ORDER), POS ** -0.5, 2.5, (), jnp.float32)
    pos_bias = jnp.clip(jax.random.uniform(splits[11], (ORDER,), jnp.float32, -3.140625, 3.140625), -3.140625, 3.140625)
    pos_out = bell_draw(splits[12], (ORDER, D), (ORDER * 64) ** -0.5, 0.0625, (), jnp.float32)
    mixout_one = bell_draw(splits[13], (MONARCH, D // MONARCH, MONARCH, INNER // MONARCH), (D // MONARCH) ** -0.5, 0.4375)
    mixout_two = bell_draw(splits[14], (MONARCH, INNER // MONARCH, MONARCH, D // MONARCH), INNER ** -0.5, 0.4375)
    norm2_gain = jnp.clip(1.0 + 0.1 * jax.random.normal(splits[15], (D,), jnp.float32), 0.5, 1.5)
    norm2_bias = bell_draw(splits[16], (D,), 0.3, 2.0, (), jnp.float32)
    gate_one = bell_draw(splits[17], (MONARCH, D // MONARCH, MONARCH, INNER // MONARCH), (D // MONARCH) ** -0.5, 0.4375, ((2, 2),))
    gate_two = bell_draw(splits[18], (MONARCH, INNER // MONARCH, MONARCH, HIDDEN_SIZE // MONARCH), INNER ** -0.5, 0.4375, ((0, 2),))
    up_one = bell_draw(splits[19], (MONARCH, D // MONARCH, MONARCH, INNER // MONARCH), (D // MONARCH) ** -0.5, 0.4375, ((2, 2),))
    up_two = bell_draw(splits[20], (MONARCH, INNER // MONARCH, MONARCH, HIDDEN_SIZE // MONARCH), INNER ** -0.5, 0.4375, ((0, 2),))
    down_one = bell_draw(splits[21], (MONARCH, HIDDEN_SIZE // MONARCH, MONARCH, INNER // MONARCH), (HIDDEN_SIZE // MONARCH) ** -0.5, 0.21875, ((0, 2),))
    down_two = bell_draw(splits[22], (MONARCH, INNER // MONARCH, MONARCH, D // MONARCH), INNER ** -0.5, 0.4375, ((2, 2),))
    return {"tokens": tokens, "short_lengths": short_lengths, "long_lengths": long_lengths, "cotangent": cotangent, "norm1_gain": norm1_gain, "norm1_bias": norm1_bias, "mixin_one": mixin_one, "mixin_two": mixin_two, "conv_taps": conv_taps, "skip_gain": skip_gain, "pos_in": pos_in, "pos_bias": pos_bias, "pos_out": pos_out, "mixout_one": mixout_one, "mixout_two": mixout_two, "norm2_gain": norm2_gain, "norm2_bias": norm2_bias, "gate_one": gate_one, "gate_two": gate_two, "up_one": up_one, "up_two": up_two, "down_one": down_one, "down_two": down_two}


@jax.custom_vjp
def low(v):
    return lax.optimization_barrier(v.astype(jnp.bfloat16)).astype(jnp.float32)

@jax.custom_vjp
def low_back(v):
    return v

def low_keep(v):
    return (low(v), None)

def low_pass(kept, grad):
    return (grad,)

def back_keep(v):
    return (v, None)

def back_low(kept, grad):
    return (low(grad),)
low.defvjp(low_keep, low_pass)
low_back.defvjp(back_keep, back_low)
epsilon = 1e-05
precise = lax.Precision.HIGHEST
slowest = math.log(100.0) / 1.5
fastest = math.log(100.0) / 0.3

def layer_norm(values, norm_gain, norm_shift):
    centred = values - lax.optimization_barrier(jnp.mean(values, axis=-1, keepdims=True))
    spread = lax.optimization_barrier(jnp.mean(centred * centred, axis=-1, keepdims=True))
    return centred * lax.rsqrt(spread + epsilon) * norm_gain + norm_shift

def make_filter(length, pos_in, pos_bias, pos_out):
    fraction = jnp.arange(length).astype(jnp.float32) / length
    band_index = jnp.arange(1, pos_in.shape[0] // 2 + 1).astype(jnp.float32)
    angles = 2.0 * math.pi * fraction[:, None] * band_index[None, :]
    features = jnp.concatenate([fraction[:, None], jnp.cos(angles), jnp.sin(angles)], axis=1)
    hidden_order = jnp.sin(jnp.dot(features, pos_in, precision=precise) + pos_bias)
    shaped = jnp.dot(hidden_order, pos_out, precision=precise)
    channels = pos_out.shape[1]
    decay_rates = slowest + (fastest - slowest) * jnp.arange(channels).astype(jnp.float32) / (channels - 1)
    return shaped * jnp.exp(-fraction[:, None] * decay_rates[None, :])

def make_filters(pos_in, pos_bias, pos_out):
    return (make_filter(SHORT, pos_in, pos_bias, pos_out), make_filter(LONG, pos_in, pos_bias, pos_out))

def fft_conv(signal, kernel):
    length = signal.shape[1]
    spectrum = jnp.fft.rfft(signal, n=2 * length, axis=1) * jnp.fft.rfft(kernel, n=2 * length, axis=0)[None]
    return jnp.fft.irfft(spectrum, n=2 * length, axis=1)[:, :length]

def mix_group(signal, conv_taps, skip_gain, kernel):
    padded = jnp.pad(signal, ((0, 0), (1, 1), (0, 0)))
    shorted = conv_taps[0] * padded[:, :-2] + conv_taps[1] * padded[:, 1:-1] + conv_taps[2] * padded[:, 2:]
    channels = skip_gain.shape[0]
    first_gate = shorted[..., :channels]
    second_gate = shorted[..., channels:2 * channels]
    value_part = shorted[..., 2 * channels:]
    product = first_gate * value_part
    spread_out = fft_conv(product, kernel) + skip_gain * product
    return (spread_out * second_gate).reshape(-1, channels)

def mix_all(signal, conv_taps, skip_gain, kernels):
    short_kernel, long_kernel = kernels
    split_at = SHORT_DEV * SHORT
    head = mix_group(signal[:split_at].reshape(SHORT_DEV, SHORT, -1), conv_taps, skip_gain, short_kernel)
    tail = mix_group(signal[split_at:].reshape(1, LONG, -1), conv_taps, skip_gain, long_kernel)
    return jnp.concatenate([head, tail], axis=0)

def valid_rows(short_block, long_block):
    short_ok = jnp.arange(SHORT)[None, :] < short_block[:, None]
    long_ok = jnp.arange(LONG) < long_block[0]
    return jnp.concatenate([short_ok.reshape(-1), long_ok]).astype(jnp.float32)[:, None]

def monarch(source, section_one, section_two):
    amount = source.shape[0]
    blocks_in = source.reshape(amount, section_one.shape[0], section_one.shape[1])
    sectioned = low(low_back(jnp.einsum('tka,kamq->tkmq', blocks_in, section_one, precision=precise)))
    mapped = jnp.einsum('tkmq,mqke->tme', sectioned, section_two, precision=precise)
    return low_back(mapped).reshape(amount, -1)

def block_forward(params, kernels, token_vals, short_block, long_block):
    norm1_gain, norm1_bias, mixin_one, mixin_two, conv_taps, skip_gain, mixout_one, mixout_two, norm2_gain, norm2_bias, gate_one, gate_two, up_one, up_two, down_one, down_two = params
    validity = valid_rows(short_block, long_block)
    normed = layer_norm(token_vals, norm1_gain, norm1_bias)
    mixed = monarch(low(normed), mixin_one, mixin_two) * validity
    gated_vals = mix_all(mixed, conv_taps, skip_gain, kernels)
    middle = token_vals + monarch(low(gated_vals), mixout_one, mixout_two)
    normed_two = low(layer_norm(middle, norm2_gain, norm2_bias))
    gate_vals = monarch(normed_two, gate_one, gate_two)
    up_vals = monarch(normed_two, up_one, up_two)
    hidden_low = low(jax.nn.silu(gate_vals) * up_vals)
    return middle + monarch(hidden_low, down_one, down_two)

def reference(tokens, short_lengths, long_lengths, cotangent, norm1_gain, norm1_bias, mixin_one, mixin_two, conv_taps, skip_gain, pos_in, pos_bias, pos_out, mixout_one, mixout_two, norm2_gain, norm2_bias, gate_one, gate_two, up_one, up_two, down_one, down_two):
    params = tuple((member.astype(jnp.float32) for member in (norm1_gain, norm1_bias, mixin_one, mixin_two, conv_taps, skip_gain, mixout_one, mixout_two, norm2_gain, norm2_bias, gate_one, gate_two, up_one, up_two, down_one, down_two)))
    kernels, kernel_back = jax.vjp(make_filters, pos_in.astype(jnp.float32), pos_bias.astype(jnp.float32), pos_out.astype(jnp.float32))
    block_count = N_DP * N_MP
    row_blocks = tokens.reshape(block_count, -1, D)
    cot_blocks = cotangent.reshape(block_count, -1, D)
    short_sets = short_lengths.reshape(block_count, -1)
    long_sets = long_lengths.reshape(block_count, 1)

    def advance(carry, member):
        param_sum, kernel_sum = carry
        block_rows, block_cot, short_block, long_block = member

        def forward(weights, filters, inputs):
            return block_forward(weights, filters, inputs, short_block, long_block)
        outputs, back_fn = jax.vjp(forward, params, kernels, block_rows.astype(jnp.float32))
        grad_params, grad_kernels, grad_inputs = back_fn(block_cot.astype(jnp.float32))
        param_sum = jax.tree.map(jnp.add, param_sum, grad_params)
        kernel_sum = jax.tree.map(jnp.add, kernel_sum, grad_kernels)
        return ((param_sum, kernel_sum), (outputs.astype(jnp.bfloat16), grad_inputs.astype(jnp.bfloat16)))
    initial = (jax.tree.map(jnp.zeros_like, params), jax.tree.map(jnp.zeros_like, kernels))
    (param_sum, kernel_sum), (outputs, grad_inputs) = lax.scan(advance, initial, (row_blocks, cot_blocks, short_sets, long_sets))
    pos_in_grad, pos_bias_grad, pos_out_grad = kernel_back(kernel_sum)
    grads = param_sum
    return (outputs.reshape(-1, D), grad_inputs.reshape(-1, D), grads[0], grads[1], grads[2], grads[3], grads[4], grads[5], pos_in_grad, pos_bias_grad, pos_out_grad, grads[6], grads[7], grads[8], grads[9], grads[10], grads[11], grads[12], grads[13], grads[14], grads[15])
```

```python
import functools
import math

import jax
import jax.numpy as jnp
import numpy as np
from jax import lax
from jax.experimental import pallas as pl
from jax.experimental.pallas import tpu as pltpu
from jax.sharding import PartitionSpec as P

BF, F32 = jnp.bfloat16, jnp.float32
SHORT, LONG = 128, 1024
ROWS = SHORT + LONG
D = 768
INNER = 192
EPS = 1e-05
SLOWEST = math.log(100.0) / 1.5
FASTEST = math.log(100.0) / 0.3
TILE = 384
CHUNK = 256


def nn(a, b):
    return jnp.dot(a, b, preferred_element_type=F32)


def tn(a, b):
    return lax.dot_general(a, b, (((0,), (0,)), ((), ())), preferred_element_type=F32)


def nt(a, b):
    return lax.dot_general(a, b, (((1,), (1,)), ((), ())), preferred_element_type=F32)


def iota(shape, dim):
    return lax.broadcasted_iota(jnp.int32, shape, dim)


def block_of(index, width, count):
    out = jnp.zeros_like(index)
    for i in range(1, count):
        out = out + (index >= width * i).astype(jnp.int32)
    return out


def ones_where(cond):
    return jnp.where(cond, 1.0, 0.0).astype(BF)


def dense_one(w, base, cols):
    rows, width = w.shape
    col = iota((width, cols), 1)
    sel = ones_where((iota((width, cols), 0) == base + (col >> 2)) & (col < INNER))
    keep = block_of(iota((rows, cols), 0), rows // 4, 4) == (iota((rows, cols), 1) & 3)
    return jnp.where(keep, nn(w, sel), 0.0).astype(BF)


def compact_one(grad, outer):
    rows, cols = grad.shape
    keep = (iota((rows, cols), 0) & 3) == block_of(iota((rows, cols), 1), cols // 4, 4)
    kept = jnp.where(keep, grad, 0.0).astype(BF)
    stride = rows // outer
    row = iota((48 * outer, rows), 0)
    member = block_of(row, 48, outer)
    target = member * stride + (row - 48 * member) * 4
    col = iota((48 * outer, rows), 1)
    sel = ones_where((col >= target) & (col < target + 4))
    return nn(sel, kept)


def norm_parts(x):
    centred = x - jnp.mean(x, axis=-1, keepdims=True)
    rstd = lax.rsqrt(jnp.mean(centred * centred, axis=-1, keepdims=True) + EPS)
    return centred * rstd, rstd


def norm_back(grad, xhat, rstd, gain):
    scaled = grad * gain
    first = jnp.mean(scaled, axis=-1, keepdims=True)
    second = jnp.mean(scaled * xhat, axis=-1, keepdims=True)
    return rstd * (scaled - first - xhat * second)


def params(**kw):
    return pltpu.CompilerParams(vmem_limit_bytes=56 * 1024 * 1024, **kw)


def whole(shape):
    return pl.BlockSpec(shape, lambda *a: (0,) * len(shape))


def smem():
    return pl.BlockSpec(memory_space=pltpu.SMEM)


def sds(shape, dtype):
    return jax.ShapeDtypeStruct(shape, dtype)


def tables():
    def pair(n):
        idx = 2 * np.arange(n, dtype=np.int64) + 1
        phase = (idx[:, None] * idx[None, :]) % (8 * n)
        angle = phase.astype(np.float64) * (math.pi / (4 * n))
        return np.cos(angle), np.sin(angle)

    short, long = pair(SHORT), pair(LONG)
    fraction = np.concatenate([np.arange(SHORT) / SHORT, np.arange(LONG) / LONG])
    half = np.concatenate(
        [(2 * np.arange(n) + 1) * (math.pi / (4 * n)) for n in (SHORT, LONG)]
    )
    aux = np.zeros((ROWS, 8), np.float32)
    aux[:, 0] = fraction
    for i, band in enumerate((1, 2)):
        aux[:, 1 + i] = np.cos(2.0 * math.pi * band * fraction)
        aux[:, 3 + i] = np.sin(2.0 * math.pi * band * fraction)
    aux[:, 5] = np.cos(half)
    aux[:, 6] = np.sin(half)
    rates = SLOWEST + (FASTEST - SLOWEST) * np.arange(D) / (D - 1)
    tabs = [jnp.asarray(t.astype(np.float32), BF) for t in (*short, *long)]
    return (*tabs, jnp.asarray(aux), jnp.asarray(rates[None].astype(np.float32)))


def scale_rows(shape):
    return jnp.where(iota(shape, 0) < SHORT, 1.0 / SHORT, 1.0 / LONG)


def transform(v, tabs):
    cs, ss, cl, sl = tabs
    head, tail = v[:SHORT], v[SHORT:]
    real = jnp.concatenate([nn(cs[...], head), nn(cl[...], tail)], axis=0)
    imag = jnp.concatenate([nn(ss[...], head), nn(sl[...], tail)], axis=0)
    return real, imag


def restore(real, imag, tabs):
    cs, ss, cl, sl = tabs
    head = nn(cs[...], real[:SHORT]) + nn(ss[...], imag[:SHORT])
    tail = nn(cl[...], real[SHORT:]) + nn(sl[...], imag[SHORT:])
    return jnp.concatenate([head, tail], axis=0)


def filter_kernel(aux, pos_in, pos_bias, pos_out, rates, cs, ss, cl, sl, sin_o, cos_o, kr_o, ks_o):
    @pl.when(pl.program_id(0) == 0)
    def _():
        pre = jnp.broadcast_to(pos_bias[...], (ROWS, 128))
        for i in range(5):
            pre = pre + aux[:, i : i + 1] * pos_in[i : i + 1, :]
        sin_o[...] = jnp.sin(pre)
        cos_o[...] = jnp.cos(pre)

    hidden = sin_o[...]
    high = hidden.astype(BF)
    low = (hidden - high.astype(F32)).astype(BF)
    w = pos_out[...]
    w_high = w.astype(BF)
    w_low = (w - w_high.astype(F32)).astype(BF)
    shaped = nn(high, w_high) + nn(high, w_low) + nn(low, w_high)
    kern = (shaped * jnp.exp(-aux[:, 0:1] * rates[...])).astype(BF)
    a, b = transform(kern, (cs, ss, cl, sl))
    cos_h, sin_h = aux[:, 5:6], aux[:, 6:7]
    scale = scale_rows((ROWS, 1))
    kr_o[...] = (cos_h * a + sin_h * b) * scale
    ks_o[...] = (cos_h * b - sin_h * a) * scale


def make_filter(const, pos_in, pos_bias, pos_out):
    cs, ss, cl, sl, aux, rates = const
    col = lambda rows: pl.BlockSpec((rows, CHUNK), lambda c: (0, c))
    return pl.pallas_call(
        filter_kernel,
        grid=(D // CHUNK,),
        in_specs=[whole((ROWS, 8)), whole((5, 128)), whole((1, 128)), col(128), col(1)]
        + [whole((SHORT, SHORT))] * 2
        + [whole((LONG, LONG))] * 2,
        out_specs=[whole((ROWS, 128))] * 2 + [col(ROWS)] * 2,
        out_shape=[sds((ROWS, 128), F32)] * 2 + [sds((ROWS, D), F32)] * 2,
        compiler_params=params(),
        name="filters",
    )(aux, pos_in, pos_bias, pos_out, rates, cs, ss, cl, sl)


def row_valid(short_len, long_len, start, rows):
    row = iota((rows, 1), 0) + start
    limit = jnp.where(row < SHORT, short_len[0], long_len[0] + SHORT)
    return row < limit


def mixin_kernel(short_len, long_len, tokens, gain, bias, w1, w2, mixed_o, sect_o, w1d, w2p):
    step = pl.program_id(0)

    @pl.when(step == 0)
    def _():
        for m in range(4):
            w1d[:, m * 256 : (m + 1) * 256] = dense_one(w1[...], m * 48, 256)
            shift = iota((576, 640), 1) == iota((576, 640), 0) + 64 * (m % 2)
            w2p[m, :INNER] = nn(w2[m], ones_where(shift)).astype(BF)
            w2p[m, INNER:] = jnp.zeros((64, 640), BF)

    xhat, _ = norm_parts(tokens[...].astype(F32))
    normed = (xhat * gain[...] + bias[...]).astype(BF)
    sect = nn(normed, w1d[...]).astype(BF)
    sect_o[...] = sect
    valid = row_valid(short_len, long_len, step * TILE, TILE)
    pieces = []
    for p in range(2):
        a = nn(sect[:, 512 * p : 512 * p + 256], w2p[2 * p])
        b = nn(sect[:, 512 * p + 256 : 512 * p + 512], w2p[2 * p + 1])
        pieces += [a[:, :512], a[:, 512:] + b[:, :128], b[:, 128:]]
    full = jnp.where(valid, jnp.concatenate(pieces, axis=1), 0.0).astype(BF)
    for j in range(3):
        mixed_o[j] = full[:, j * D : (j + 1) * D]


def rows_spec(width):
    return pl.BlockSpec((TILE, width), lambda i: (i, 0))


def mixin_forward(short_len, long_len, tokens, gain, bias, w1, w2):
    return pl.pallas_call(
        mixin_kernel,
        grid=(ROWS // TILE,),
        in_specs=[smem(), smem(), rows_spec(D), whole((1, D)), whole((1, D)), whole((D, INNER)), whole((4, INNER, 576))],
        out_specs=[
            pl.BlockSpec((3, TILE, D), lambda i: (0, i, 0)),
            rows_spec(1024),
            whole((D, 1024)),
            whole((4, 256, 640)),
        ],
        out_shape=[sds((3, ROWS, D), BF), sds((ROWS, 1024), BF), sds((D, 1024), BF), sds((4, 256, 640), BF)],
        compiler_params=params(),
        name="mixer_input",
    )(short_len, long_len, tokens, gain, bias, w1, w2)


def edges(shape):
    row = iota(shape, 0)
    first = (row == 0) | (row == SHORT)
    last = (row == SHORT - 1) | (row == ROWS - 1)
    return first, last


def before(v, first):
    return jnp.where(first, 0.0, pltpu.roll(v, 1, 0))


def after(v, last):
    return jnp.where(last, 0.0, pltpu.roll(v, ROWS - 1, 0))


def conv_forward_kernel(mixed, t0, t1, t2, skip, kr, ks, cs, ss, cl, sl, gated_o, spread_o, xr_o, xs_o):
    first, last = edges((ROWS, CHUNK))
    parts = []
    for j, taps in enumerate((t0, t1, t2)):
        m = mixed[j].astype(F32)
        parts.append(taps[0:1] * before(m, first) + taps[1:2] * m + taps[2:3] * after(m, last))
    product = parts[0] * parts[2]
    tabs = (cs, ss, cl, sl)
    real, imag = transform(product.astype(BF), tabs)
    xr_o[...] = real.astype(BF)
    xs_o[...] = imag.astype(BF)
    a, b = kr[...], ks[...]
    out_real = (real * a - imag * b).astype(BF)
    out_imag = (real * b + imag * a).astype(BF)
    spread = restore(out_real, out_imag, tabs) + skip[...] * product
    spread_o[...] = spread.astype(BF)
    gated_o[...] = (spread * parts[1]).astype(BF)


def chunk_spec(rows):
    return pl.BlockSpec((rows, CHUNK), lambda c: (0, c))


def tap_spec(j):
    return pl.BlockSpec((3, CHUNK), lambda c, j=j: (0, c + j * (D // CHUNK)))


def table_specs():
    return [whole((SHORT, SHORT))] * 2 + [whole((LONG, LONG))] * 2


def conv_forward(const, mixed, taps, skip, kr, ks):
    parts = pl.BlockSpec((3, ROWS, CHUNK), lambda c: (0, 0, c))
    return pl.pallas_call(
        conv_forward_kernel,
        grid=(D // CHUNK,),
        in_specs=[parts, tap_spec(0), tap_spec(1), tap_spec(2), chunk_spec(1), chunk_spec(ROWS), chunk_spec(ROWS)]
        + table_specs(),
        out_specs=[chunk_spec(ROWS)] * 4,
        out_shape=[sds((ROWS, D), BF)] * 4,
        compiler_params=params(),
        name="conv_forward",
    )(mixed, taps, taps, taps, skip, kr, ks, *const[:4])


def conv_back_kernel(
    short_len, long_len, mixed, t0, t1, t2, skip, kr, ks, xr, xs, spread, grad_gated, sin_h, cos_h, aux, pos_out, rates,
    cs, ss, cl, sl, grad_o, small_o, pos_out_o, pos_o, hidden_grad
):
    step = pl.program_id(0)
    tabs = (cs, ss, cl, sl)
    first, last = edges((ROWS, CHUNK))
    taps = (t0, t1, t2)
    parts = []
    for j in range(3):
        m = mixed[j].astype(F32)
        parts.append(taps[j][0:1] * before(m, first) + taps[j][1:2] * m + taps[j][2:3] * after(m, last))
    product = parts[0] * parts[2]
    gg = grad_gated[...].astype(F32)
    grad_spread = gg * parts[1]
    real, imag = transform(grad_spread.astype(BF), tabs)
    a, b = kr[...], ks[...]
    grad_product = restore((a * real + b * imag).astype(BF), (a * imag - b * real).astype(BF), tabs)
    grad_product = grad_product + skip[...] * grad_spread
    x_real, x_imag = xr[...].astype(F32), xs[...].astype(F32)
    z_real = x_real * real + x_imag * imag
    z_imag = x_real * imag - x_imag * real
    cos_p, sin_p = aux[:, 5:6], aux[:, 6:7]
    grad_kernel = restore(
        (cos_p * z_real - sin_p * z_imag).astype(BF), (cos_p * z_imag + sin_p * z_real).astype(BF), tabs
    )
    shaped_grad = (grad_kernel * (scale_rows((ROWS, 1)) * jnp.exp(-aux[:, 0:1] * rates[...]))).astype(BF)
    pos_out_o[...] = tn(sin_h[...].astype(BF), shaped_grad)
    piece = nt(shaped_grad, pos_out[...].astype(BF))

    @pl.when(step == 0)
    def _():
        hidden_grad[...] = piece

    @pl.when(step > 0)
    def _():
        hidden_grad[...] += piece

    @pl.when(step == pl.num_programs(0) - 1)
    def _():
        pre = hidden_grad[...] * cos_h[...]
        rows = [jnp.sum(aux[:, i : i + 1] * pre, axis=0, keepdims=True) for i in range(5)]
        rows.append(jnp.sum(pre, axis=0, keepdims=True))
        rows.append(jnp.zeros((2, 128), F32))
        pos_o[...] = jnp.concatenate(rows, axis=0)

    grads = (grad_product * parts[2], gg * spread[...].astype(F32), grad_product * parts[0])
    valid = row_valid(short_len, long_len, 0, ROWS)
    small = []
    for j in range(3):
        m = mixed[j].astype(F32)
        g = grads[j]
        small += [
            jnp.sum(g * before(m, first), axis=0, keepdims=True),
            jnp.sum(g * m, axis=0, keepdims=True),
            jnp.sum(g * after(m, last), axis=0, keepdims=True),
        ]
        back = taps[j][0:1] * after(g, last) + taps[j][1:2] * g + taps[j][2:3] * before(g, first)
        grad_o[j] = jnp.where(valid, back, 0.0).astype(BF)
    small.append(jnp.sum(grad_spread * product, axis=0, keepdims=True))
    small.append(jnp.zeros((6, CHUNK), F32))
    small_o[...] = jnp.concatenate(small, axis=0)


def conv_back(const, short_len, long_len, mixed, taps, skip, kr, ks, xr, xs, spread, grad_gated, sin_h, cos_h, pos_out):
    aux, rates = const[4:]
    parts = pl.BlockSpec((3, ROWS, CHUNK), lambda c: (0, 0, c))
    return pl.pallas_call(
        conv_back_kernel,
        grid=(D // CHUNK,),
        in_specs=[smem(), smem(), parts, tap_spec(0), tap_spec(1), tap_spec(2), chunk_spec(1)]
        + [chunk_spec(ROWS)] * 6
        + [whole((ROWS, 128))] * 2
        + [whole((ROWS, 8)), chunk_spec(128), chunk_spec(1)]
        + table_specs(),
        out_specs=[parts, chunk_spec(16), chunk_spec(128), whole((8, 128))],
        out_shape=[sds((3, ROWS, D), BF), sds((16, D), F32), sds((128, D), F32), sds((8, 128), F32)],
        scratch_shapes=[pltpu.VMEM((ROWS, 128), F32)],
        compiler_params=params(),
        name="conv_back",
    )(short_len, long_len, mixed, taps, taps, taps, skip, kr, ks, xr, xs, spread, grad_gated, sin_h, cos_h, aux, pos_out,
      rates, *const[:4])


def mixout_kernel(tokens, gated, w1, w2, gain, bias, middle_o, normed_o, sect_o, w1d, w2p):
    @pl.when(pl.program_id(0) == 0)
    def _():
        for m in range(4):
            w1d[:, m * 256 : (m + 1) * 256] = dense_one(w1[...], m * 48, 256)
            shift = iota((INNER, 256), 1) == iota((INNER, 256), 0) + 64 * (m % 2)
            w2p[m, :INNER] = nn(w2[m], ones_where(shift)).astype(BF)
            w2p[m, INNER:] = jnp.zeros((64, 256), BF)

    sect = nn(gated[...], w1d[...]).astype(BF)
    sect_o[...] = sect
    pieces = []
    for p in range(2):
        a = nn(sect[:, 512 * p : 512 * p + 256], w2p[2 * p])
        b = nn(sect[:, 512 * p + 256 : 512 * p + 512], w2p[2 * p + 1])
        pieces += [a[:, :128], a[:, 128:] + b[:, :128], b[:, 128:]]
    middle = tokens[...].astype(F32) + jnp.concatenate(pieces, axis=1)
    middle_o[...] = middle
    xhat, _ = norm_parts(middle)
    normed_o[...] = (xhat * gain[...] + bias[...]).astype(BF)


def mixout_forward(tokens, gated, w1, w2, gain, bias):
    return pl.pallas_call(
        mixout_kernel,
        grid=(ROWS // TILE,),
        in_specs=[rows_spec(D), rows_spec(D), whole((D, INNER)), whole((4, INNER, INNER)), whole((1, D)), whole((1, D))],
        out_specs=[rows_spec(D), rows_spec(D), rows_spec(1024), whole((D, 1024)), whole((4, 256, 256))],
        out_shape=[sds((ROWS, D), F32), sds((ROWS, D), BF), sds((ROWS, 1024), BF), sds((D, 1024), BF), sds((4, 256, 256), BF)],
        compiler_params=params(),
        name="mixer_output",
    )(tokens, gated, w1, w2, gain, bias)


def glu_kernel(h, normed, cot, g1, g2, u1, u2, d1, d2, sect_o, grad_g_o, grad_u_o, grads_o, g1d, u1d, d2d, acc):
    step = pl.program_id(0)

    @pl.when(step == 0)
    def _():
        g1d[...] = dense_one(g1[...], h * 48, INNER)
        u1d[...] = dense_one(u1[...], h * 48, INNER)
        col = iota((INNER, D), 1)
        tile = ones_where(col - INNER * block_of(col, INNER, 4) == iota((INNER, D), 0))
        keep = block_of(iota((INNER, D), 0), 48, 4) == block_of(col, INNER, 4)
        d2d[...] = jnp.where(keep, nn(d2[...], tile), 0.0).astype(BF)

    rows = normed[...]
    gate_sect = nn(rows, g1d[...]).astype(BF)
    up_sect = nn(rows, u1d[...]).astype(BF)
    gate = nn(gate_sect, g2[...])
    up = nn(up_sect, u2[...])
    sig = jax.nn.sigmoid(gate)
    act = gate * sig
    hidden = (act * up).astype(BF)
    sect_o[...] = nn(hidden, d1[...]).astype(BF)
    grad_sect = nt(cot[...], d2d[...]).astype(BF)
    grad_hidden = nt(grad_sect, d1[...])
    grad_gate = (grad_hidden * up * (sig * (1.0 + gate * (1.0 - sig)))).astype(BF)
    grad_up = (grad_hidden * act).astype(BF)
    grad_g_o[...] = nt(grad_gate, g2[...]).astype(BF)
    grad_u_o[...] = nt(grad_up, u2[...]).astype(BF)
    terms = (tn(grad_sect, hidden), tn(gate_sect, grad_gate), tn(up_sect, grad_up))

    @pl.when(step == 0)
    def _():
        for i, term in enumerate(terms):
            acc[i] = term

    @pl.when(step > 0)
    def _():
        for i, term in enumerate(terms):
            acc[i] += term

    @pl.when(step == pl.num_programs(0) - 1)
    def _():
        for i in range(3):
            for c in range(6):
                grads_o[i * 6 + c] = acc[i, :, c * 128 : (c + 1) * 128].astype(BF)


def glu_block(h, normed, cot, g1, g2, u1, u2, d1, d2):
    pick = lambda shape: pl.BlockSpec((None,) + shape, lambda i: (h, 0, 0))
    return pl.pallas_call(
        functools.partial(glu_kernel, h),
        grid=(ROWS // TILE,),
        in_specs=[
            rows_spec(D), rows_spec(D), whole((D, 96)), pick((INNER, D)), whole((D, 96)), pick((INNER, D)),
            pick((D, INNER)), pick((INNER, INNER)),
        ],
        out_specs=[rows_spec(INNER)] * 3 + [whole((18, INNER, 128))] + [whole((D, INNER))] * 2 + [whole((INNER, D))],
        out_shape=[sds((ROWS, INNER), BF)] * 3
        + [sds((18, INNER, 128), BF)]
        + [sds((D, INNER), BF)] * 2
        + [sds((INNER, D), BF)],
        scratch_shapes=[pltpu.VMEM((3, INNER, D), F32)],
        compiler_params=params(),
        name="feed_forward",
    )(normed, cot, g1, g2, u1, u2, d1, d2)


def outer_kernel(normed, cot, s0, s1, gg0, gg1, gu0, gu1, out, acc):
    step = pl.program_id(0)
    terms = (
        tn(gg0[...], normed[...]), tn(gg1[...], normed[...]), tn(gu0[...], normed[...]), tn(gu1[...], normed[...]),
        tn(s0[...], cot[...]), tn(s1[...], cot[...]),
    )

    @pl.when(step == 0)
    def _():
        for i, term in enumerate(terms):
            acc[i] = term

    @pl.when(step > 0)
    def _():
        for i, term in enumerate(terms):
            acc[i] += term

    @pl.when(step == pl.num_programs(0) - 1)
    def _():
        for w in range(2):
            for i in range(2):
                one = compact_one(acc[2 * w + i], 1).astype(BF)
                start = 96 * w + 48 * i
                for c in range(6):
                    out[3 + c, start : start + 48] = one[:, c * 128 : (c + 1) * 128]
        total = jnp.zeros((INNER, 384), F32)
        for i in range(2):
            col = iota((INNER, D), 1)
            keep = block_of(iota((INNER, D), 0), 48, 4) == block_of(col, INNER, 4)
            kept = jnp.where(keep, acc[4 + i], 0.0).astype(BF)
            row = iota((D, 384), 0)
            sel = ones_where(row - INNER * block_of(row, INNER, 4) + INNER * i == iota((D, 384), 1))
            total = total + nn(kept, sel)
        for c in range(3):
            out[c] = total[:, c * 128 : (c + 1) * 128].astype(BF)


def outer_grads(normed, cot, parts):
    return pl.pallas_call(
        outer_kernel,
        grid=(ROWS // TILE,),
        in_specs=[rows_spec(D)] * 2 + [rows_spec(INNER)] * 6,
        out_specs=whole((9, INNER, 128)),
        out_shape=sds((9, INNER, 128), BF),
        scratch_shapes=[pltpu.VMEM((6, INNER, D), F32)],
        compiler_params=params(),
        name="outer_grads",
    )(normed, cot, *parts)


def accumulate(step, acc, terms):
    @pl.when(step == 0)
    def _():
        for ref, term in zip(acc, terms):
            ref[...] = term

    @pl.when(step > 0)
    def _():
        for ref, term in zip(acc, terms):
            ref[...] += term


def column_sums(pair):
    rows = [jnp.sum(v, axis=0, keepdims=True) for v in pair]
    return jnp.concatenate(rows + [jnp.zeros((6, D), F32)], axis=0)


def slot_of(mp, half):
    return jnp.where(mp[0] == half, 0, 1)


def middle_back_kernel(
    mp, middle, cot, gated, sect, s0, s1, s2, s3, e0, e1, e2, e3, f0, f1, f2, f3, d0, d1, d2, d3, g0, g1, g2, g3,
    u0, u1, u2, u3, gain, w1d, w2p, result_o, grad_middle_o, grad_gated_o, grads_o, small_o, acc1, acc2
):
    step = pl.program_id(0)
    mid = middle[...]
    out = mid
    grad = jnp.zeros((TILE, D), F32)
    for s, d in zip((s0, s1, s2, s3), (d0, d1, d2, d3)):
        out = out + nn(s[...], d[...])
    result_o[...] = out.astype(BF)
    for e, g in zip((e0, e1, e2, e3, f0, f1, f2, f3), (g0, g1, g2, g3, u0, u1, u2, u3)):
        grad = grad + nt(e[...], g[...])
    xhat, rstd = norm_parts(mid)
    sums = column_sums((grad * xhat, grad))
    grad_middle = cot[...].astype(F32) + norm_back(grad, xhat, rstd, gain[...])
    grad_middle_o[...] = grad_middle
    branch = grad_middle.astype(BF)
    sections, terms = [], []
    for m in range(4):
        start = 384 * (m // 2) + 128 * (m % 2)
        window = branch[:, start : start + 256]
        sections.append(nt(window, w2p[m]).astype(BF))
        terms.append(tn(sect[:, m * 256 : (m + 1) * 256], window))
    grad_sect = jnp.concatenate(sections, axis=1)
    grad_gated_o[...] = nt(grad_sect, w1d[...]).astype(BF)
    accumulate(step, [small_o, acc1] + [acc2.at[m] for m in range(4)], [sums, tn(grad_sect, gated[...])] + terms)

    @pl.when(step == pl.num_programs(0) - 1)
    def _():
        one = compact_one(acc1[...], 4).astype(BF)
        lane = iota((INNER, 128), 1)
        for half in range(2):
            slot = slot_of(mp, half)
            for c in range(3):
                grads_o[slot, c] = one[:, half * 384 + c * 128 : half * 384 + (c + 1) * 128]
            a, b = acc2[2 * half, :INNER], acc2[2 * half + 1, :INNER]
            both = jnp.where(lane < 64, a[:, 128:], b[:, :128])
            for c, piece in enumerate((a[:, :128], both, b[:, 128:])):
                grads_o[slot, 3 + c] = piece.astype(BF)


def middle_back(mp, middle, cot, gated, sect, parts, dense, gain, w1d, w2p):
    return pl.pallas_call(
        middle_back_kernel,
        grid=(ROWS // TILE,),
        in_specs=[smem(), rows_spec(D), rows_spec(D), rows_spec(D), rows_spec(1024)]
        + [rows_spec(INNER)] * 12
        + [whole((INNER, D))] * 4
        + [whole((D, INNER))] * 8
        + [whole((1, D)), whole((D, 1024)), whole((4, 256, 256))],
        out_specs=[rows_spec(D)] * 3 + [whole((2, 6, INNER, 128)), whole((8, D))],
        out_shape=[sds((ROWS, D), BF), sds((ROWS, D), F32), sds((ROWS, D), BF), sds((2, 6, INNER, 128), BF), sds((8, D), F32)],
        scratch_shapes=[pltpu.VMEM((1024, D), F32), pltpu.VMEM((4, 256, 256), F32)],
        compiler_params=params(),
        name="middle_back",
    )(mp, middle, cot, gated, sect, *parts, *dense, gain, w1d, w2p)


def mixin_back_kernel(mp, tokens, grad_mixed, sect, grad_middle, gain, bias, w1d, w2p, tokens_o, grads_o, small_o, acc1, acc2):
    step = pl.program_id(0)
    xhat, rstd = norm_parts(tokens[...].astype(F32))
    normed = (xhat * gain[...] + bias[...]).astype(BF)
    full = jnp.concatenate([grad_mixed[j] for j in range(3)], axis=1)
    sections, terms = [], []
    for m in range(4):
        start = 1152 * (m // 2) + 512 * (m % 2)
        window = full[:, start : start + 640]
        sections.append(nt(window, w2p[m]).astype(BF))
        terms.append(tn(sect[:, m * 256 : (m + 1) * 256], window))
    grad_sect = jnp.concatenate(sections, axis=1)
    grad = nt(grad_sect, w1d[...])
    sums = column_sums((grad * xhat, grad))
    tokens_o[...] = (grad_middle[...] + norm_back(grad, xhat, rstd, gain[...])).astype(BF)
    accumulate(step, [small_o, acc1] + [acc2.at[m] for m in range(4)], [sums, tn(grad_sect, normed)] + terms)

    @pl.when(step == pl.num_programs(0) - 1)
    def _():
        one = compact_one(acc1[...], 4).astype(BF)
        lane = iota((INNER, 128), 1)
        for half in range(2):
            slot = slot_of(mp, half)
            for c in range(3):
                grads_o[slot, c] = one[:, half * 384 + c * 128 : half * 384 + (c + 1) * 128]
            a, b = acc2[2 * half, :INNER], acc2[2 * half + 1, :INNER]
            pieces = [a[:, c * 128 : (c + 1) * 128] for c in range(4)]
            pieces.append(jnp.where(lane < 64, a[:, 512:], b[:, :128]))
            pieces += [b[:, c * 128 : (c + 1) * 128] for c in range(1, 5)]
            for c, piece in enumerate(pieces):
                grads_o[slot, 3 + c] = piece.astype(BF)


def mixin_back(mp, tokens, grad_mixed, sect, grad_middle, gain, bias, w1d, w2p):
    return pl.pallas_call(
        mixin_back_kernel,
        grid=(ROWS // TILE,),
        in_specs=[smem(), rows_spec(D), pl.BlockSpec((3, TILE, D), lambda i: (0, i, 0)), rows_spec(1024), rows_spec(D)]
        + [whole((1, D)), whole((1, D)), whole((D, 1024)), whole((4, 256, 640))],
        out_specs=[rows_spec(D), whole((2, 12, INNER, 128)), whole((8, D))],
        out_shape=[sds((ROWS, D), BF), sds((2, 12, INNER, 128), BF), sds((8, D), F32)],
        scratch_shapes=[pltpu.VMEM((1024, D), F32), pltpu.VMEM((4, 256, 640), F32)],
        compiler_params=params(),
        name="mixer_input_back",
    )(mp, tokens, grad_mixed, sect, grad_middle, gain, bias, w1d, w2p)


def swap_pair(v):
    n = lax.axis_size("mp")
    return lax.ppermute(v, "mp", [(i, (i + 1) % n) for i in range(n)])


def swap_bit(v, bit):
    n = lax.axis_size("dp")
    return lax.ppermute(v, "dp", [(i, i ^ (1 << bit)) for i in range(n)])


def add(a, b):
    return (a.astype(F32) + b.astype(F32)).astype(BF)


def sum_dp(buf):
    rows = buf.shape[0]
    bits = (lax.axis_size("dp") - 1).bit_length()
    cut = min(3, bits)
    unit = 16 << cut
    padded = -(-rows // unit) * unit
    buf = jnp.pad(buf, ((0, padded - rows), (0, 0)))
    units = padded // unit
    sizes = [(units + 2 - i) // 3 * unit for i in range(3)]
    groups, start = [], 0
    for size in sizes:
        groups.append(buf[start : start + size])
        start += size
    index = lax.axis_index("dp")
    for s in range(cut):
        for i in range(3):
            bit = (i + s) % cut
            mine = (index >> bit) & 1
            half = groups[i].shape[0] // 2
            send = lax.dynamic_slice_in_dim(groups[i], (1 - mine) * half, half, 0)
            keep = lax.dynamic_slice_in_dim(groups[i], mine * half, half, 0)
            groups[i] = add(keep, swap_bit(send, bit))
    for bit in range(cut, bits):
        groups = [add(g, swap_bit(g, bit)) for g in groups]
    for s in reversed(range(cut)):
        for i in range(3):
            bit = (i + s) % cut
            mine = (index >> bit) & 1
            got = swap_bit(groups[i], bit)
            groups[i] = jnp.where(
                mine == 0, jnp.concatenate([groups[i], got], 0), jnp.concatenate([got, groups[i]], 0)
            )
    return jnp.concatenate(groups, axis=0)[:rows]


def unslab(v, count):
    return v.reshape(count, INNER, 128).transpose(1, 0, 2).reshape(INNER, count * 128)


def local(
    tokens, short_lengths, long_lengths, cotangent, norm1_gain, norm1_bias, mixin_one, mixin_two, conv_taps, skip_gain,
    pos_in, pos_bias, pos_out, mixout_one, mixout_two, norm2_gain, norm2_bias, gate_one, gate_two, up_one, up_two,
    down_one, down_two,
):
    mp_index = lax.axis_index("mp")
    mp = mp_index.astype(jnp.int32).reshape(1)
    const = tables()
    row = lambda v: v.reshape(1, -1)
    glu_own = (
        gate_one.reshape(D, 96),
        gate_two.reshape(2, INNER, D),
        up_one.reshape(D, 96),
        up_two.reshape(2, INNER, D),
        down_one.reshape(2, D, INNER),
        down_two.transpose(2, 0, 1, 3).reshape(2, INNER, INNER),
    )
    glu_other = tuple(swap_pair(w) for w in glu_own)

    sin_h, cos_h, kr, ks = make_filter(const, pos_in, row(pos_bias), pos_out)
    mixed, sect_in, w1d_in, w2p_in = mixin_forward(
        short_lengths, long_lengths, tokens, row(norm1_gain), row(norm1_bias), mixin_one.reshape(D, INNER),
        mixin_two.reshape(4, INNER, 576),
    )
    gated, spread, xr, xs = conv_forward(const, mixed, conv_taps, row(skip_gain), kr, ks)
    middle, normed_two, sect_out, w1d_out, w2p_out = mixout_forward(
        tokens, gated, mixout_one.reshape(D, INNER), mixout_two.reshape(4, INNER, INNER), row(norm2_gain), row(norm2_bias)
    )
    blocks = []
    for h, weights in ((0, glu_other), (0, glu_own), (1, glu_other), (1, glu_own)):
        blocks.append(glu_block(h, normed_two, cotangent, *weights))
    sects, grads_g, grads_u, grads_two, g1d, u1d, d2d = zip(*blocks)
    outer = [
        outer_grads(normed_two, cotangent, (sects[i], sects[i + 2], grads_g[i], grads_g[i + 2], grads_u[i], grads_u[i + 2]))
        for i in range(2)
    ]
    glu_sums = []
    for i in range(2):
        glu_sums.append(sum_dp(add(grads_two[2 * i + 1], swap_pair(grads_two[2 * i])).reshape(-1, 128)))
    glu_sums.append(sum_dp(add(outer[1], swap_pair(outer[0])).reshape(-1, 128)))

    result, grad_middle, grad_gated, mixout_grads, norm2_small = middle_back(
        mp, middle, cotangent, gated, sect_out, sects + grads_g + grads_u, d2d + g1d + u1d, row(norm2_gain), w1d_out, w2p_out
    )
    grad_mixed, conv_small, pos_out_grad, pos_small = conv_back(
        const, short_lengths, long_lengths, mixed, conv_taps, row(skip_gain), kr, ks, xr, xs, spread, grad_gated, sin_h,
        cos_h, pos_out,
    )
    tokens_grad, mixin_grads, norm1_small = mixin_back(
        mp, tokens, grad_mixed, sect_in, grad_middle, row(norm1_gain), row(norm1_bias), w1d_in, w2p_in
    )
    taps_grad = conv_small[:9].reshape(3, 3, D).transpose(1, 0, 2).reshape(3, 3 * D)
    halves = lambda v: v.reshape(v.shape[0], 2, -1).transpose(1, 0, 2).reshape(2, -1)
    small = jnp.concatenate(
        [halves(v) for v in (norm1_small[:2], norm2_small[:2], conv_small[9:10], taps_grad, pos_small[:6], pos_out_grad)],
        axis=1,
    ).astype(BF).reshape(2, -1, 128)
    pick = lambda v, slot: lax.dynamic_index_in_dim(v, slot, 0, keepdims=False)
    own = jnp.concatenate(
        [mixout_grads[0].reshape(-1, 128), mixin_grads[0].reshape(-1, 128), pick(small, mp_index)], axis=0
    )
    other = jnp.concatenate(
        [mixout_grads[1].reshape(-1, 128), mixin_grads[1].reshape(-1, 128), pick(small, 1 - mp_index)], axis=0
    )
    mixer_sum = sum_dp(add(own, swap_pair(other))).astype(F32)

    def one_half(v):
        return unslab(v, 3).reshape(4, 48, 2, 192).transpose(2, 3, 0, 1)

    def two_half(v, count):
        return unslab(v, count).reshape(48, 4, 2, -1).transpose(2, 0, 1, 3)

    mixout_one_grad = one_half(mixer_sum[:576])
    mixout_two_grad = two_half(mixer_sum[576:1152], 3)
    mixin_one_grad = one_half(mixer_sum[1152:1728])
    mixin_two_grad = two_half(mixer_sum[1728:3456], 9)
    flat = mixer_sum[3456:].reshape(-1)
    pieces, start = [], 0
    for rows_n, width in ((2, 384), (2, 384), (1, 384), (3, 1152), (6, 64), (128, 384)):
        pieces.append(flat[start : start + rows_n * width].reshape(rows_n, width))
        start += rows_n * width
    n1, n2, sk, taps_out, pos_s, pos_o = pieces

    down_one_grads, gate_two_grads, up_two_grads = [], [], []
    for i in range(2):
        v = glu_sums[i].astype(F32).reshape(3, 6 * INNER, 128)
        down_one_grads.append(unslab(v[0], 6).T.reshape(D, 4, 48))
        gate_two_grads.append(unslab(v[1], 6).reshape(48, 4, D))
        up_two_grads.append(unslab(v[2], 6).reshape(48, 4, D))
    ones = glu_sums[2].astype(F32)
    down_two_grad = unslab(ones[:576], 3).reshape(4, 48, 2, 192)
    outer_one = unslab(ones[576:], 6).reshape(2, 2, 48, 4, 192).transpose(0, 3, 4, 1, 2)
    return (
        result, tokens_grad, n1[0], n1[1], mixin_one_grad, mixin_two_grad, taps_out, sk[0], pos_s[:5], pos_s[5], pos_o,
        mixout_one_grad, mixout_two_grad, n2[0], n2[1], outer_one[0], jnp.stack(gate_two_grads), outer_one[1],
        jnp.stack(up_two_grads), jnp.stack(down_one_grads), down_two_grad,
    )


def solution(mesh):
    return jax.shard_map(
        local,
        mesh=mesh,
        in_specs=(
            P(("dp", "mp"), None),
            P(("dp", "mp")),
            P(("dp", "mp")),
            P(("dp", "mp"), None),
            *[P()] * 13,
            P(None, None, "mp", None),
            P("mp", None, None, None),
            P(None, None, "mp", None),
            P("mp", None, None, None),
            P("mp", None, None, None),
            P(None, None, "mp", None),
        ),
        out_specs=(
            P(("dp", "mp"), None),
            P(("dp", "mp"), None),
            P("mp"),
            P("mp"),
            P("mp", None, None, None),
            P("mp", None, None, None),
            P(None, "mp"),
            P("mp"),
            P(None, "mp"),
            P("mp"),
            P(None, "mp"),
            P("mp", None, None, None),
            P("mp", None, None, None),
            P("mp"),
            P("mp"),
            P(None, None, "mp", None),
            P("mp", None, None, None),
            P(None, None, "mp", None),
            P("mp", None, None, None),
            P("mp", None, None, None),
            P(None, None, "mp", None),
        ),
        check_vma=False,
    )
```

```python
import functools
import math

import jax
import jax.numpy as jnp
import numpy as np
from jax import lax
from jax.experimental import pallas as pl
from jax.experimental.pallas import tpu as pltpu
from jax.sharding import PartitionSpec as P

BF, F32 = jnp.bfloat16, jnp.float32
SHORT, LONG = 128, 1024
ROWS = SHORT + LONG
D = 768
INNER = 192
EPS = 1e-05
SLOWEST = math.log(100.0) / 1.5
FASTEST = math.log(100.0) / 0.3
TILE = 384
CHUNK = 256
MIB = 1024 * 1024
GLU_ONE, GLU_TWO, GLU_ROWS = 18 * INNER, 21 * INNER, 4352
MIX_IN, MIX_SMALL, MIX_POS, MIX_OUT, MIX_ROWS = 6 * INNER, 18 * INNER, 18 * INNER + 48, 18 * INNER + 64, 4096


def nn(a, b):
    return jnp.dot(a, b, preferred_element_type=F32)


def tn(a, b):
    return lax.dot_general(a, b, (((0,), (0,)), ((), ())), preferred_element_type=F32)


def nt(a, b):
    return lax.dot_general(a, b, (((1,), (1,)), ((), ())), preferred_element_type=F32)


def iota(shape, dim):
    return lax.broadcasted_iota(jnp.int32, shape, dim)


def block_of(index, width, count):
    out = jnp.zeros_like(index)
    for i in range(1, count):
        out = out + (index >= width * i).astype(jnp.int32)
    return out


def ones_where(cond):
    return jnp.where(cond, 1.0, 0.0).astype(BF)


def dense_rows(joined, base, rows):
    width, cols = joined.shape
    row = iota((rows, width), 0)
    sel = ones_where((iota((rows, width), 1) == base + (row >> 2)) & (row < INNER))
    keep = (iota((rows, cols), 0) & 3) == block_of(iota((rows, cols), 1), cols // 4, 4)
    return jnp.where(keep, nn(sel, joined), 0.0).astype(BF)


def joined_one(w1):
    return jnp.concatenate([w1[k] for k in range(4)], axis=1)


def compact_one(grad, outer):
    rows, cols = grad.shape
    keep = (iota((rows, cols), 0) & 3) == block_of(iota((rows, cols), 1), cols // 4, 4)
    kept = jnp.where(keep, grad, 0.0).astype(BF)
    stride = rows // outer
    row = iota((48 * outer, rows), 0)
    member = block_of(row, 48, outer)
    target = member * stride + (row - 48 * member) * 4
    col = iota((48 * outer, rows), 1)
    sel = ones_where((col >= target) & (col < target + 4))
    return nn(sel, kept)


def norm_parts(x):
    centred = x - jnp.mean(x, axis=-1, keepdims=True)
    rstd = lax.rsqrt(jnp.mean(centred * centred, axis=-1, keepdims=True) + EPS)
    return centred * rstd, rstd


def norm_back(grad, xhat, rstd, gain):
    scaled = grad * gain
    first = jnp.mean(scaled, axis=-1, keepdims=True)
    second = jnp.mean(scaled * xhat, axis=-1, keepdims=True)
    return rstd * (scaled - first - xhat * second)


WHOLE, PINNED, FAR = "whole", "pinned", "far"


def by_rows(*shape):
    dim = len(shape) - 2
    block = shape[:dim] + (TILE,) + shape[dim + 1 :]
    return pl.BlockSpec(block, lambda i: (0,) * dim + (i, 0))


def by_columns(*shape):
    lead = len(shape) - 1
    return pl.BlockSpec(shape[:-1] + (CHUNK,), lambda i: (0,) * lead + (i,))


def call(kernel, name, outs, scratch, limit, us, *args, grid=None, aliases=None, after=()):
    inner = kernel
    count, skip = len(args), len(after)
    if skip:
        kernel = lambda *refs: inner(*refs[:count], *refs[count + skip :])
    in_specs, operands, out_specs, out_shape = [], [], [], []
    for arg in args:
        arg, mode = arg if isinstance(arg, tuple) else (arg, WHOLE)
        if arg.dtype == jnp.int32:
            in_specs.append(pl.BlockSpec(memory_space=pltpu.SMEM))
        elif mode == FAR:
            arg = pltpu.with_memory_space_constraint(arg, pltpu.HBM)
            in_specs.append(pl.BlockSpec(memory_space=pl.ANY))
        elif isinstance(mode, pl.BlockSpec):
            arg = pltpu.with_memory_space_constraint(arg, pltpu.HBM)
            in_specs.append(mode)
        else:
            if mode == PINNED:
                arg = pltpu.with_memory_space_constraint(arg, pltpu.VMEM)
            in_specs.append(pl.BlockSpec(memory_space=pltpu.VMEM))
        operands.append(arg)
    for arg in after:
        in_specs.append(pl.BlockSpec(memory_space=pl.ANY))
        operands.append(arg)
    for shape, dtype, *mode in outs:
        mode = mode[0] if mode else WHOLE
        if isinstance(mode, pl.BlockSpec):
            out_specs.append(mode)
            out_shape.append(pltpu.HBM(shape, dtype))
        else:
            out_specs.append(pl.BlockSpec(memory_space=pltpu.VMEM))
            out_shape.append(pltpu.VMEM(shape, dtype) if mode == PINNED else jax.ShapeDtypeStruct(shape, dtype))
    return pl.pallas_call(
        kernel,
        out_shape=out_shape,
        in_specs=in_specs,
        out_specs=out_specs,
        grid=(grid,) if grid else (),
        scratch_shapes=[pltpu.VMEM(*v) if isinstance(v, tuple) else v for v in scratch],
        input_output_aliases=aliases or {},
        cost_estimate=pl.CostEstimate(flops=int(us * 1.0e9), bytes_accessed=0, transcendentals=0),
        compiler_params=pltpu.CompilerParams(vmem_limit_bytes=limit * MIB),
        name=name,
    )(*operands)


def first_step(body):
    pl.when(pl.program_id(0) == 0)(body)


def last_step(body):
    pl.when(pl.program_id(0) == pl.num_programs(0) - 1)(body)


def grid_part(size):
    start = pl.multiple_of(pl.program_id(0) * size, size)
    return pl.ds(start, size), start


def tables():
    def pair(n):
        idx = 2 * np.arange(n, dtype=np.int64) + 1
        phase = (idx[:, None] * idx[None, :]) % (8 * n)
        angle = phase.astype(np.float64) * (math.pi / (4 * n))
        return np.concatenate([np.cos(angle), np.sin(angle)], axis=1)

    fraction = np.concatenate([np.arange(SHORT) / SHORT, np.arange(LONG) / LONG])
    half = np.concatenate(
        [(2 * np.arange(n) + 1) * (math.pi / (4 * n)) for n in (SHORT, LONG)]
    )
    aux = np.zeros((ROWS, 8), np.float32)
    aux[:, 0] = fraction
    for i, band in enumerate((1, 2)):
        aux[:, 1 + i] = np.cos(2.0 * math.pi * band * fraction)
        aux[:, 3 + i] = np.sin(2.0 * math.pi * band * fraction)
    aux[:, 5] = np.cos(half)
    aux[:, 6] = np.sin(half)
    rates = SLOWEST + (FASTEST - SLOWEST) * np.arange(D) / (D - 1)
    return (
        jnp.asarray(pair(SHORT).astype(np.float32), BF),
        jnp.asarray(pair(LONG).astype(np.float32), BF),
        jnp.asarray(aux),
        jnp.asarray(rates[None].astype(np.float32)),
    )


def scale_rows(shape):
    return jnp.where(iota(shape, 0) < SHORT, 1.0 / SHORT, 1.0 / LONG)


def transform(v, ts, tl):
    head, tail = v[:SHORT], v[SHORT:]
    real = jnp.concatenate([nn(ts[:, :SHORT], head), nn(tl[:, :LONG], tail)], axis=0)
    imag = jnp.concatenate([nn(ts[:, SHORT:], head), nn(tl[:, LONG:], tail)], axis=0)
    return real, imag


def restore(real, imag, ts, tl):
    head = nn(ts[...], jnp.concatenate([real[:SHORT], imag[:SHORT]], axis=0))
    tail = nn(tl[...], jnp.concatenate([real[SHORT:], imag[SHORT:]], axis=0))
    return jnp.concatenate([head, tail], axis=0)


def chunks(body):
    def step(c, carry):
        body(pl.ds(pl.multiple_of(c * CHUNK, CHUNK), CHUNK))
        return carry

    lax.fori_loop(0, D // CHUNK, step, 0)


def tiles(body, rows=ROWS, tile=TILE):
    def step(i, carry):
        body(pl.ds(pl.multiple_of(i * tile, tile), tile), i * tile)
        return carry

    lax.fori_loop(0, rows // tile, step, 0)


def filter_kernel(aux, pos_in, pos_bias, pos_out, rates, ts, tl, sin_o, cos_o, kr_o, ks_o):
    pre = jnp.broadcast_to(pos_bias[...], (ROWS, 128))
    for i in range(5):
        pre = pre + aux[:, i : i + 1] * pos_in[i : i + 1, :]
    sin_o[...] = jnp.sin(pre)
    cos_o[...] = jnp.cos(pre)

    def body(cols):
        hidden = sin_o[...]
        high = hidden.astype(BF)
        low = (hidden - high.astype(F32)).astype(BF)
        w = pos_out[:, cols]
        w_high = w.astype(BF)
        w_low = (w - w_high.astype(F32)).astype(BF)
        shaped = nn(high, w_high) + nn(high, w_low) + nn(low, w_high)
        kern = (shaped * jnp.exp(-aux[:, 0:1] * rates[:, cols])).astype(BF)
        a, b = transform(kern, ts, tl)
        cos_h, sin_h = aux[:, 5:6], aux[:, 6:7]
        scale = scale_rows((ROWS, 1))
        kr_o[:, cols] = ((cos_h * a + sin_h * b) * scale).astype(BF)
        ks_o[:, cols] = ((cos_h * b - sin_h * a) * scale).astype(BF)

    chunks(body)


def make_filter(const, pos_in, pos_bias, pos_out):
    ts, tl, aux, rates = const
    return call(
        filter_kernel, "filters", [((ROWS, 128), F32, PINNED)] * 2 + [((ROWS, D), BF, PINNED)] * 2, [], 10, 8,
        aux, pos_in, pos_bias, pos_out, rates, ts, tl,
    )


def row_valid(short_len, long_len, start, rows):
    row = iota((rows, 1), 0) + start
    limit = jnp.where(row < SHORT, short_len[0], long_len[0] + SHORT)
    return row < limit


def mixin_kernel(short_len, long_len, tokens, vecs, w1, w2, mixed_o, saved_o, sect_o, w1d_o, w2p_o, w1d, w2p):
    @first_step
    def _():
        joined = joined_one(w1)
        for m in range(4):
            w1d[m * 256 : (m + 1) * 256] = dense_rows(joined, m * 48, 256)
            shift = iota((576, 640), 1) == iota((576, 640), 0) + 64 * (m % 2)
            w2p[m, :INNER] = nn(w2[m].reshape(INNER, 576), ones_where(shift)).astype(BF)
            w2p[m, INNER:] = jnp.zeros((64, 640), BF)
        w1d_o[...] = w1d[...]
        w2p_o[...] = w2p[...]

    rows, start = grid_part(TILE)
    xhat, _ = norm_parts(tokens[...].astype(F32))
    normed = (xhat * vecs[0:1] + vecs[1:2]).astype(BF)
    sect = nt(normed, w1d[...]).astype(BF)
    sect_o[...] = sect
    valid = row_valid(short_len, long_len, start, TILE)
    pieces = []
    for p in range(2):
        a = nn(sect[:, 512 * p : 512 * p + 256], w2p[2 * p])
        b = nn(sect[:, 512 * p + 256 : 512 * p + 512], w2p[2 * p + 1])
        pieces += [a[:, :512], a[:, 512:] + b[:, :128], b[:, 128:]]
    full = jnp.where(valid, jnp.concatenate(pieces, axis=1), 0.0).astype(BF)
    for j in range(3):
        part = full[:, j * D : (j + 1) * D]
        mixed_o[j, rows] = part
        saved_o[j] = part


def mixin_forward(short_len, long_len, tokens, vecs, w1, w2):
    once = lambda *shape: pl.BlockSpec(shape, lambda i: (0,) * len(shape))
    return call(
        mixin_kernel, "mixer_input",
        [
            ((3, ROWS, D), BF, PINNED), ((3, ROWS, D), BF, by_rows(3, ROWS, D)), ((ROWS, 1024), BF, by_rows(ROWS, 1024)),
            ((1024, D), BF, once(1024, D)), ((4, 256, 640), BF, once(4, 256, 640)),
        ],
        [((1024, D), BF), ((4, 256, 640), BF)], 28, 8,
        short_len, long_len, (tokens, by_rows(ROWS, D)), vecs, w1, w2, grid=ROWS // TILE,
    )


def edges(shape):
    row = iota(shape, 0)
    first = (row == 0) | (row == SHORT)
    last = (row == SHORT - 1) | (row == ROWS - 1)
    return first, last


def before(v, first):
    return jnp.where(first, 0.0, pltpu.roll(v, 1, 0))


def after(v, last):
    return jnp.where(last, 0.0, pltpu.roll(v, ROWS - 1, 0))


def tap_rows(taps, cols, j):
    return [taps[3 * j + i : 3 * j + i + 1, cols] for i in range(3)]


def conv_forward_kernel(mixed, taps, vecs, kr, ks, ts, tl, gated_o, spread_o, xr_o, xs_o, parts_o):
    cols, _ = grid_part(CHUNK)
    first, last = edges((ROWS, CHUNK))
    parts = []
    for j in range(3):
        m = mixed[j, :, cols].astype(F32)
        t0, t1, t2 = tap_rows(taps, cols, j)
        parts.append(t0 * before(m, first) + t1 * m + t2 * after(m, last))
        parts_o[j] = parts[j].astype(BF)
    product = parts[0] * parts[2]
    real, imag = transform(product.astype(BF), ts, tl)
    xr_o[...] = real.astype(BF)
    xs_o[...] = imag.astype(BF)
    a, b = kr[:, cols].astype(F32), ks[:, cols].astype(F32)
    spread = restore((real * a - imag * b).astype(BF), (real * b + imag * a).astype(BF), ts, tl)
    spread = spread + vecs[4:5, cols] * product
    spread_o[...] = spread.astype(BF)
    gated_o[:, cols] = (spread * parts[1]).astype(BF)


def conv_forward(const, mixed, taps, vecs, kr, ks):
    column = ((ROWS, D), BF, by_columns(ROWS, D))
    return call(
        conv_forward_kernel, "conv_forward",
        [((ROWS, D), BF, PINNED), column, column, column, ((3, ROWS, D), BF, by_columns(3, ROWS, D))], [], 26, 14,
        (mixed, PINNED), taps, vecs, (kr, PINNED), (ks, PINNED), const[0], const[1], grid=D // CHUNK,
    )


def conv_back_kernel(
    c, short_len, long_len, mixed_h, parts_h, taps, vecs, kr, ks, xr_h, xs_h, spread_h, grad_gated, sin_h, cos_h, aux, pos_out,
    rates, ts, tl, *rest
):
    *earlier, grad_o, small_o, pos_out_o, hidden_o, mixed, parts, xr, xs, spread, sems = rest
    cols = slice(c * CHUNK, (c + 1) * CHUNK)
    copies = [
        pltpu.make_async_copy(far.at[..., cols], near, sems.at[i])
        for i, (far, near) in enumerate(((parts_h, parts), (xr_h, xr), (xs_h, xs), (spread_h, spread), (mixed_h, mixed)))
    ]
    for copy in copies:
        copy.start()
    first, last = edges((ROWS, CHUNK))
    gg = grad_gated[:, cols].astype(F32)
    copies[0].wait()
    grad_spread = gg * parts[1].astype(F32)
    real, imag = transform(grad_spread.astype(BF), ts, tl)
    a, b = kr[:, cols].astype(F32), ks[:, cols].astype(F32)
    grad_product = restore((a * real + b * imag).astype(BF), (a * imag - b * real).astype(BF), ts, tl)
    grad_product = grad_product + vecs[4:5, cols] * grad_spread
    copies[1].wait()
    copies[2].wait()
    x_real, x_imag = xr[...].astype(F32), xs[...].astype(F32)
    z_real = x_real * real + x_imag * imag
    z_imag = x_real * imag - x_imag * real
    cos_p, sin_p = aux[:, 5:6], aux[:, 6:7]
    grad_kernel = restore(
        (cos_p * z_real - sin_p * z_imag).astype(BF), (cos_p * z_imag + sin_p * z_real).astype(BF), ts, tl
    )
    shaped_grad = (grad_kernel * (scale_rows((ROWS, 1)) * jnp.exp(-aux[:, 0:1] * rates[:, cols]))).astype(BF)
    pos_out_o[...] = tn(sin_h[...].astype(BF), shaped_grad)
    hidden = nt(shaped_grad, pos_out[:, cols].astype(BF))
    copies[3].wait()
    copies[4].wait()
    front = parts[0].astype(F32)
    value = parts[2].astype(F32)
    grads = (grad_product * value, gg * spread[...].astype(F32), grad_product * front)
    valid = row_valid(short_len, long_len, 0, ROWS)
    small = []
    for j in range(3):
        m = mixed[j].astype(F32)
        g = grads[j]
        up, down = after(g, last), before(g, first)
        t0, t1, t2 = tap_rows(taps, cols, j)
        small += [jnp.sum(v * m, axis=0, keepdims=True) for v in (up, g, down)]
        grad_o[j] = jnp.where(valid, t0 * up + t1 * g + t2 * down, 0.0).astype(BF)
    small.append(jnp.sum(grad_spread * front * value, axis=0, keepdims=True))
    small.append(jnp.zeros((6, CHUNK), F32))
    small_o[...] = jnp.concatenate(small, axis=0)
    if not earlier:
        hidden_o[...] = hidden
    else:
        pre = (hidden + earlier[0][...] + earlier[1][...]) * cos_h[...]
        rows = [jnp.sum(aux[:, i : i + 1] * pre, axis=0, keepdims=True) for i in range(5)]
        rows.append(jnp.sum(pre, axis=0, keepdims=True))
        rows.append(jnp.zeros((2, 128), F32))
        hidden_o[...] = jnp.concatenate(rows, axis=0)


def conv_back(c, const, short_len, long_len, saved, taps, vecs, kr, ks, grad_gated, sin_h, cos_h, pos_out, earlier, after):
    ts, tl, aux, rates = const
    mixed, parts, xr, xs, spread = saved
    final = len(earlier) > 0
    one = ((ROWS, CHUNK), BF)
    three = ((3, ROWS, CHUNK), BF)
    return call(
        functools.partial(conv_back_kernel, c), "conv_back",
        [(*three, PINNED), ((16, CHUNK), F32), ((128, CHUNK), F32)] + ([((8, 128), F32)] if final else [((ROWS, 128), F32, PINNED)]),
        [three, three, one, one, one, pltpu.SemaphoreType.DMA((5,))], 30, 8,
        short_len, long_len, (mixed, FAR), (parts, FAR), taps, vecs, (kr, PINNED), (ks, PINNED), (xr, FAR), (xs, FAR),
        (spread, FAR), (grad_gated, PINNED), (sin_h, PINNED), (cos_h, PINNED), aux, pos_out, rates, ts, tl,
        *[(v, PINNED) for v in earlier], after=after,
    )


def mixout_kernel(tokens, gated, vecs, w1, w2, middle_o, out_o, normed_o, sect_o, w1d, w2p):
    @first_step
    def _():
        joined = joined_one(w1)
        for m in range(4):
            w1d[m * 256 : (m + 1) * 256] = dense_rows(joined, m * 48, 256)
            shift = iota((INNER, 256), 1) == iota((INNER, 256), 0) + 64 * (m % 2)
            w2p[m, :INNER] = nn(w2[m].reshape(INNER, INNER), ones_where(shift)).astype(BF)
            w2p[m, INNER:] = jnp.zeros((64, 256), BF)

    rows, _ = grid_part(TILE)
    sect = nt(gated[rows], w1d[...]).astype(BF)
    sect_o[rows] = sect
    pieces = []
    for p in range(2):
        a = nn(sect[:, 512 * p : 512 * p + 256], w2p[2 * p])
        b = nn(sect[:, 512 * p + 256 : 512 * p + 512], w2p[2 * p + 1])
        pieces += [a[:, :128], a[:, 128:] + b[:, :128], b[:, 128:]]
    middle = tokens[...].astype(F32) + jnp.concatenate(pieces, axis=1)
    middle_o[...] = middle
    out_o[rows] = middle
    xhat, _ = norm_parts(middle)
    normed_o[rows] = (xhat * vecs[2:3] + vecs[3:4]).astype(BF)


def mixout_forward(tokens, gated, vecs, w1, w2):
    tile = by_rows(ROWS, D)
    return call(
        mixout_kernel, "mixer_output",
        [
            ((ROWS, D), F32, tile), ((ROWS, D), F32, PINNED), ((ROWS, D), BF, PINNED), ((ROWS, 1024), BF, PINNED),
            ((1024, D), BF, PINNED), ((4, 256, 256), BF, PINNED),
        ],
        [], 18, 5, (tokens, tile), (gated, PINNED), vecs, w1, w2, grid=ROWS // TILE,
    )


def glu_kernel(
    h, normed, cot, out_in, grad_in, g1, g2, u1, u2, d1, d2, out_o, grad_o, grads_o,
    g1d, u1d, d2d, hidden_s, gate_s, up_s, sect_s, gsect_s, usect_s, grad_sect_s, ggs_s, gus_s
):
    g1d[...] = dense_rows(joined_one(g1), h * 48, INNER)
    u1d[...] = dense_rows(joined_one(u1), h * 48, INNER)
    col = iota((INNER, D), 1)
    keep = block_of(iota((INNER, D), 0), 48, 4) == block_of(col, INNER, 4)
    tile = ones_where(col - INNER * block_of(col, INNER, 4) == iota((INNER, D), 0))
    d2_rows = jnp.concatenate([d2[m, :, h, :] for m in range(4)], axis=0)
    d2d[...] = jnp.where(keep, nn(d2_rows, tile), 0.0).astype(BF)
    g2r = g2[h].reshape(INNER, D)
    u2r = u2[h].reshape(INNER, D)
    d1r = d1[h]

    def body(rows, start):
        x = normed[rows]
        gate_sect = nt(x, g1d[...]).astype(BF)
        up_sect = nt(x, u1d[...]).astype(BF)
        gate = nn(gate_sect, g2r)
        up = nn(up_sect, u2r)
        sig = jax.nn.sigmoid(gate)
        act = gate * sig
        hidden = (act * up).astype(BF)
        sect = nt(hidden, d1r).astype(BF)
        out_o[rows] = out_in[rows] + nn(sect, d2d[...])
        grad_sect = nt(cot[rows], d2d[...]).astype(BF)
        grad_hidden = nn(grad_sect, d1r)
        grad_gate = (grad_hidden * up * (sig * (1.0 + gate * (1.0 - sig)))).astype(BF)
        grad_up = (grad_hidden * act).astype(BF)
        ggs = nt(grad_gate, g2r).astype(BF)
        gus = nt(grad_up, u2r).astype(BF)
        piece = nn(ggs, g1d[...]) + nn(gus, u1d[...])
        grad_o[rows] = piece if grad_in is None else grad_in[rows] + piece
        hidden_s[rows] = hidden
        gate_s[rows] = grad_gate
        up_s[rows] = grad_up
        sect_s[rows] = sect
        gsect_s[rows] = gate_sect
        usect_s[rows] = up_sect
        grad_sect_s[rows] = grad_sect
        ggs_s[rows] = ggs
        gus_s[rows] = gus

    tiles(body)
    for i, (a, b) in enumerate(((grad_sect_s, hidden_s), (gsect_s, gate_s), (usect_s, up_s))):
        term = tn(a[...], b[...]).astype(BF)
        for c in range(6):
            start = (i * 6 + c) * INNER
            grads_o[start : start + INNER] = term[:, c * 128 : (c + 1) * 128]
    for i, a in enumerate((ggs_s, gus_s)):
        one = compact_one(tn(a[...], normed[...]), 1).astype(BF)
        for c in range(6):
            start = GLU_ONE + 96 * c + 48 * i
            grads_o[start : start + 48] = one[:, c * 128 : (c + 1) * 128]
    kept = jnp.where(keep, tn(sect_s[...], cot[...]), 0.0).astype(BF)
    row = iota((D, 256), 0)
    two = nn(kept, ones_where(row - INNER * block_of(row, INNER, 4) == iota((D, 256), 1)))
    grads_o[GLU_TWO : GLU_TWO + INNER] = two[:, :128].astype(BF)
    rest = two[:96, 128:] + pltpu.roll(two[96:, 128:], 64, 1)
    grads_o[GLU_TWO + INNER : GLU_TWO + INNER + 96] = rest.astype(BF)
    grads_o[GLU_TWO + INNER + 96 :] = jnp.zeros((32, 128), BF)


def glu_block(h, normed, cot, out, grad, weights, after=()):
    kernel = functools.partial(glu_kernel, h)
    args = [(normed, PINNED), cot, (out, PINNED), (grad, PINNED), *weights]
    if grad is None:
        del args[3]
        kernel = lambda a, b, c, *rest: glu_kernel(h, a, b, c, None, *rest)
    rows = ((ROWS, INNER), BF)
    return call(
        kernel, "feed_forward",
        [((ROWS, D), F32, PINNED)] * 2 + [((GLU_ROWS, 128), BF)],
        [((INNER, D), BF)] * 3 + [((ROWS, D), BF)] * 3 + [rows] * 6, 26, 12, *args,
        aliases={2: 0} if grad is None else {2: 0, 3: 1}, after=after,
    )


def column_sums(pair):
    rows = [jnp.sum(v, axis=0, keepdims=True) for v in pair]
    return jnp.concatenate(rows + [jnp.zeros((6, D), F32)], axis=0)


def slot_of(mp, half):
    return jnp.where(mp[0] == half, 0, 1)


def window_starts(e):
    pair = 2 * e
    return [pair * (m // 2) + (e // 128 * 128) * (m % 2) for m in range(4)]


def middle_back_kernel(
    mp, middle, out, grad_in, cot, gated, sect, vecs, w1d, w2p, result_o, grad_middle_o, grad_gated_o, grads_o, small_o,
    branch_s, grad_sect_s
):
    @first_step
    def _():
        small_o[...] = jnp.zeros((8, D), F32)

    rows, _ = grid_part(TILE)
    result_o[...] = out[rows].astype(BF)
    grad = grad_in[rows]
    xhat, rstd = norm_parts(middle[...])
    small_o[...] += column_sums((grad * xhat, grad))
    grad_middle = cot[rows].astype(F32) + norm_back(grad, xhat, rstd, vecs[2:3])
    grad_middle_o[...] = grad_middle
    branch = grad_middle.astype(BF)
    branch_s[rows] = branch
    pieces = [nt(branch[:, s : s + 256], w2p[m]).astype(BF) for m, s in enumerate(window_starts(INNER))]
    grad_sect = jnp.concatenate(pieces, axis=1)
    grad_sect_s[rows] = grad_sect
    grad_gated_o[rows] = nn(grad_sect, w1d[...]).astype(BF)

    @last_step
    def _():
        one = compact_one(tn(grad_sect_s[...], gated[...]), 4).astype(BF)
        lane = iota((INNER, 128), 1)
        two = []
        for m, s in enumerate(window_starts(INNER)):
            two.append(tn(sect[:, m * 256 : (m + 1) * 256], branch_s[:, s : s + 256])[:INNER])
        for half in range(2):
            slot = slot_of(mp, half)
            pieces = [one[:, half * 384 + c * 128 : half * 384 + (c + 1) * 128] for c in range(3)]
            a, b = two[2 * half], two[2 * half + 1]
            pieces += [a[:, :128], jnp.where(lane < 64, a[:, 128:], b[:, :128]), b[:, 128:]]
            for c, piece in enumerate(pieces):
                grads_o[slot, c * INNER : (c + 1) * INNER] = piece.astype(BF)


def middle_back(mp, middle, out, grad, cot, gated, sect, vecs, w1d, w2p, after):
    tile = by_rows(ROWS, D)
    return call(
        middle_back_kernel, "middle_back",
        [((ROWS, D), BF, tile), ((ROWS, D), F32, tile), ((ROWS, D), BF, PINNED), ((2, 6 * INNER, 128), BF), ((8, D), F32)],
        [((ROWS, D), BF), ((ROWS, 1024), BF)], 26, 10, mp, (middle, tile), (out, PINNED), (grad, PINNED), cot, (gated, PINNED),
        (sect, PINNED), vecs, (w1d, PINNED), (w2p, PINNED), grid=ROWS // TILE, after=after,
    )


def mixin_back_kernel(
    mp, tokens, m0, m1, m2, sect, grad_middle, vecs, w1d, w2p, mixout_grads, norm2, c0, c1, c2, p0, p1, p2, pos,
    tokens_o, own_o, other_o, norm1, normed_s, grad_sect_s
):
    @first_step
    def _():
        norm1[...] = jnp.zeros((8, D), F32)

    def pieces_of(start, width, rows):
        out = []
        while width:
            j, at = start // D, start % D
            c, at = at // CHUNK, at % CHUNK
            n = min(width, CHUNK - at)
            out.append((m0, m1, m2)[c][j, rows, at : at + n])
            start, width = start + n, width - n
        return jnp.concatenate(out, axis=1)

    rows, _ = grid_part(TILE)
    xhat, rstd = norm_parts(tokens[...].astype(F32))
    normed_s[rows] = (xhat * vecs[0:1] + vecs[1:2]).astype(BF)
    pieces = [nt(pieces_of(s, 640, rows), w2p[m]).astype(BF) for m, s in enumerate(window_starts(576))]
    grad_sect = jnp.concatenate(pieces, axis=1)
    grad_sect_s[rows] = grad_sect
    grad = nn(grad_sect, w1d[...])
    norm1[...] += column_sums((grad * xhat, grad))
    tokens_o[...] = (grad_middle[...] + norm_back(grad, xhat, rstd, vecs[0:1])).astype(BF)

    @last_step
    def _():
        one = compact_one(tn(grad_sect_s[...], normed_s[...]), 4).astype(BF)
        lane = iota((INNER, 128), 1)
        own = mp[0]
        blocks = []
        for half in range(2):
            block = [(0, mixout_grads[half])]
            a, b = [
                tn(sect[:, m * 256 : (m + 1) * 256], pieces_of(window_starts(576)[m], 640, slice(None)))[:INNER]
                for m in (2 * half, 2 * half + 1)
            ]
            pieces = [one[:, half * 384 + c * 128 : half * 384 + (c + 1) * 128] for c in range(3)]
            pieces += [a[:, c * 128 : (c + 1) * 128] for c in range(4)]
            pieces.append(jnp.where(lane < 64, a[:, 512:], b[:, :128]))
            pieces += [b[:, c * 128 : (c + 1) * 128] for c in range(1, 5)]
            block += [(MIX_IN + c * INNER, piece.astype(BF)) for c, piece in enumerate(pieces)]
            cut = lambda v, r, col: v[r : r + 1, col : col + 128]
            conv = lambda r, col: (c0, c1, c2)[col // CHUNK][r : r + 1, col % CHUNK : col % CHUNK + 128]
            small = []
            for v, r in ((norm1, 0), (norm1, 1), (norm2, 0), (norm2, 1)):
                small += [cut(v, r, half * 384 + 128 * i) for i in range(3)]
            small += [conv(9, half * 384 + 128 * i) for i in range(3)]
            for tap in range(3):
                for i in range(9):
                    col = half * 1152 + 128 * i
                    small.append(conv(3 * (col // D) + tap, col % D))
            small.append(jnp.zeros((6, 128), F32))
            block.append((MIX_SMALL, jnp.concatenate(small, axis=0).astype(BF)))
            block.append((MIX_POS, jnp.concatenate([pos[...], jnp.zeros((8, 128), F32)], axis=0).astype(BF)))
            for i in range(3):
                col = half * 384 + 128 * i
                part = (p0, p1, p2)[col // CHUNK][:, col % CHUNK : col % CHUNK + 128]
                block.append((MIX_OUT + 128 * i, part.astype(BF)))
            block.append((MIX_OUT + 384, jnp.zeros((MIX_ROWS - MIX_OUT - 384, 128), BF)))
            blocks.append(block)
        for half in range(2):
            block = blocks[half]

            @pl.when(own == half)
            def _():
                for at, piece in block[1:]:
                    own_o[at : at + piece.shape[0]] = piece

            @pl.when(own != half)
            def _():
                for at, piece in block[1:]:
                    other_o[at : at + piece.shape[0]] = piece

        own_o[:MIX_IN] = mixout_grads[0]
        other_o[:MIX_IN] = mixout_grads[1]


def mixin_back(mp, tokens, grads, sect, grad_middle, vecs, w1d, w2p, extra, after):
    tile = by_rows(ROWS, D)
    return call(
        mixin_back_kernel, "mixer_input_back", [((ROWS, D), BF, tile), ((MIX_ROWS, 128), BF), ((MIX_ROWS, 128), BF)],
        [((8, D), F32), ((ROWS, D), BF), ((ROWS, 1024), BF)], 26, 12, mp, (tokens, tile), *[(g, PINNED) for g in grads], sect,
        (grad_middle, tile), vecs, w1d, w2p, *extra, grid=ROWS // TILE, after=after,
    )


def swap_pair(v):
    n = lax.axis_size("mp")
    return lax.ppermute(v, "mp", [(i, (i + 1) % n) for i in range(n)])


def swap_bit(v, bit):
    n = lax.axis_size("dp")
    return lax.ppermute(v, "dp", [(i, i ^ (1 << bit)) for i in range(n)])


def sum_of(a, b):
    return (a.astype(F32) + b.astype(F32)).astype(BF)


def part_of(ref, bit, half):
    return ref[pl.ds(pl.multiple_of(bit * half, 16), half)]


def split_kernel(n, bits, *refs):
    for i in range(n):
        keep, got = refs[2 * i], refs[2 * i + 1]
        send_o, keep_o = refs[2 * n + 2 * i], refs[2 * n + 2 * i + 1]
        half, bit = send_o.shape[0], bits[i]
        send_o[...] = sum_of(part_of(keep, 1 - bit, half), part_of(got, 1 - bit, half))
        keep_o[...] = sum_of(part_of(keep, bit, half), part_of(got, bit, half))


def split(bits, pairs, after=()):
    outs = [((p[0].shape[0] // 2, 128), BF) for p in pairs for _ in range(2)]
    flat = [v for p in pairs for v in p]
    got = call(functools.partial(split_kernel, len(pairs)), "split", outs, [], 8, 1, bits, *flat, after=after)
    return [(got[2 * i], got[2 * i + 1]) for i in range(len(pairs))]


def sum_kernel(n, *refs):
    for i in range(n):
        refs[2 * n + i][...] = sum_of(refs[2 * i][...], refs[2 * i + 1][...])


def sums(pairs, after=()):
    outs = [(p[0].shape, BF) for p in pairs]
    return call(functools.partial(sum_kernel, len(pairs)), "sum", outs, [], 8, 1, *[v for p in pairs for v in p], after=after)


def merge_kernel(n, bits, *refs):
    for i in range(n):
        mine, got, out = refs[2 * i], refs[2 * i + 1], refs[2 * n + i]
        half = mine.shape[0]
        out[pl.ds(pl.multiple_of(bits[i] * half, 16), half)] = mine[...]
        out[pl.ds(pl.multiple_of((1 - bits[i]) * half, 16), half)] = got[...]


def merge(bits, pairs, after=()):
    outs = [((2 * p[0].shape[0], 128), BF) for p in pairs]
    flat = [v for p in pairs for v in p]
    return call(functools.partial(merge_kernel, len(pairs)), "merge", outs, [], 8, 1, bits, *flat, after=after)


class Sum:
    def __init__(self, index, pairs, orders, total_bits):
        self.index, self.orders, self.n = index, orders, len(pairs)
        self.rest = [b for b in range(total_bits) if b not in orders[0]]
        self.pairs = pairs
        self.level = 0

    def bits(self, level):
        mine = [(self.index >> order[level]) & 1 for order in self.orders]
        return jnp.stack(mine).astype(jnp.int32)

    def steps(self):
        depth = len(self.orders[0])
        plan = [("split", i) for i in range(depth)]
        plan += [("sum", b) for b in [None] + self.rest]
        plan += [("merge", i) for i in reversed(range(1, depth))]
        return plan

    def step(self, after=()):
        plan = self.steps()
        kind, what = plan[self.level]
        following = plan[self.level + 1] if self.level + 1 < len(plan) else ("end", 0)
        depth = len(self.orders[0])
        if kind == "split":
            halves = split(self.bits(what), self.pairs, after)
            self.pairs = [(k, swap_bit(s, o[what])) for (s, k), o in zip(halves, self.orders)]
            self.token = halves[0][1]
        else:
            out = sums(self.pairs, after) if kind == "sum" else merge(self.bits(what), self.pairs, after)
            self.token = out[0]
            if following[0] == "sum":
                self.pairs = [(v, swap_bit(v, following[1])) for v in out]
            else:
                back = following[1] if following[0] == "merge" else 0
                if not depth:
                    self.pairs = [(v, v) for v in out]
                else:
                    self.pairs = [(v, swap_bit(v, o[back])) for v, o in zip(out, self.orders)]
        self.level += 1
        return self.token

    @property
    def done(self):
        return self.level == len(self.steps())

    def last_bits(self):
        return self.bits(0)


def rows_at(mine, got, bit, start, count):
    half = mine.shape[0]
    out, at = [], start
    while at < start + count:
        n = min(count - (at - start), half - at % half)
        local, lower = at % half, at < half
        a, b = mine[local : local + n], got[local : local + n]
        first = bit == 0 if lower else bit == 1
        out.append(jnp.where(first, a, b))
        at += n
    return out[0] if len(out) == 1 else jnp.concatenate(out, axis=0)


def unpack_glu_kernel(bits, a0, b0, a1, b1, down_one, gate_two, up_two, gate_one, up_one, down_two):
    for h, (mine, got) in enumerate(((a0, b0), (a1, b1))):
        take = lambda start, count: rows_at(mine, got, bits[h], start, count).astype(F32)
        wide = lambda start, rows: jnp.concatenate([take(start + c * rows, rows) for c in range(6)], axis=1)
        down_one[h] = wide(0, INNER)
        gate_two[h] = wide(6 * INNER, INNER).reshape(48, 4, D)
        up_two[h] = wide(12 * INNER, INNER).reshape(48, 4, D)
        ones = wide(GLU_ONE, 96)
        for k in range(4):
            gate_one[k, h] = ones[:48, k * INNER : (k + 1) * INNER]
            up_one[k, h] = ones[48:, k * INNER : (k + 1) * INNER]
        rest = take(GLU_TWO + INNER, 96)
        right = jnp.concatenate([rest, pltpu.roll(rest, 64, 1)], axis=0)
        two = jnp.concatenate([take(GLU_TWO, INNER), right[:, :64]], axis=1)
        for m in range(4):
            down_two[m, :, h, :] = two[48 * m : 48 * m + 48]


def unpack_glu(bits, parts, after=()):
    outs = [
        ((2, INNER, D), F32), ((2, 48, 4, D), F32), ((2, 48, 4, D), F32), ((4, 2, 48, INNER), F32), ((4, 2, 48, INNER), F32),
        ((4, 48, 2, INNER), F32),
    ]
    return call(unpack_glu_kernel, "unpack_feed_forward", outs, [], 24, 8, bits, *parts, after=after)


def unpack_mixer_kernel(bits, a0, b0, a1, b1, mixout_one, mixout_two, mixin_one, mixin_two, vecs, taps, pos, pos_out):
    size = MIX_ROWS // 2

    def take(start, count):
        out, at = [], start
        while at < start + count:
            g = at // size
            n = min(start + count, (g + 1) * size) - at
            mine, got = ((a0, b0), (a1, b1))[g]
            out.append(rows_at(mine, got, bits[g], at - g * size, n).astype(F32))
            at += n
        return out[0] if len(out) == 1 else jnp.concatenate(out, axis=0)

    wide = lambda start, rows, n: jnp.concatenate([take(start + c * rows, rows) for c in range(n)], axis=1)
    for base, one, two, e in ((0, mixout_one, mixout_two, INNER), (MIX_IN, mixin_one, mixin_two, 576)):
        ones = wide(base, INNER, 3)
        twos = wide(base + 3 * INNER, INNER, 2 * e // 128)
        for i in range(2):
            one[i] = ones[:, i * INNER : (i + 1) * INNER]
            two[i] = twos[:, i * e : (i + 1) * e].reshape(48, 4, e)
    small = take(MIX_SMALL, 48)
    for i in range(5):
        vecs[i : i + 1] = jnp.concatenate([small[3 * i + c : 3 * i + c + 1] for c in range(3)], axis=1)
    for i in range(3):
        taps[i : i + 1] = jnp.concatenate([small[15 + 9 * i + c : 16 + 9 * i + c] for c in range(9)], axis=1)
    pos[...] = take(MIX_POS, 16)[:8]
    pos_out[...] = wide(MIX_OUT, 128, 3)


def unpack_mixer(bits, parts):
    outs = [
        ((2, INNER, INNER), F32), ((2, 48, 4, INNER), F32), ((2, INNER, INNER), F32), ((2, 48, 4, 576), F32), ((5, 384), F32),
        ((3, 1152), F32), ((8, 128), F32), ((128, 384), F32),
    ]
    return call(unpack_mixer_kernel, "unpack_mixer", outs, [], 24, 5, bits, *parts)


def local(
    tokens, short_lengths, long_lengths, cotangent, norm1_gain, norm1_bias, mixin_one, mixin_two, conv_taps, skip_gain,
    pos_in, pos_bias, pos_out, mixout_one, mixout_two, norm2_gain, norm2_bias, gate_one, gate_two, up_one, up_two,
    down_one, down_two,
):
    mp_index = lax.axis_index("mp")
    mp = mp_index.astype(jnp.int32).reshape(1)
    dp_index = lax.axis_index("dp")
    total_bits = (lax.axis_size("dp") - 1).bit_length()
    const = tables()
    vecs = jnp.stack([norm1_gain, norm1_bias, norm2_gain, norm2_bias, skip_gain])
    taps = conv_taps.reshape(3, 3, D).transpose(1, 0, 2).reshape(9, D)
    rows_first = lambda w: w.transpose(0, 2, 3, 1).reshape(w.shape[0], -1, w.shape[1])
    glu_own = (rows_first(gate_one), gate_two, rows_first(up_one), up_two, rows_first(down_one), down_two)
    glu_other = tuple(swap_pair(w) for w in glu_own)

    mixed, mixed_saved, sect_in, w1d_in, w2p_in = mixin_forward(
        short_lengths, long_lengths, tokens, vecs, rows_first(mixin_one), mixin_two
    )
    sin_h, cos_h, kr, ks = make_filter(const, pos_in, pos_bias.reshape(1, -1), pos_out)
    gated, spread, xr, xs, parts = conv_forward(const, mixed, taps, vecs, kr, ks)
    middle, out, normed_two, sect_out, w1d_out, w2p_out = mixout_forward(
        tokens, gated, vecs, rows_first(mixout_one), mixout_two
    )
    cut = min(3, total_bits)
    first_order, second_order = tuple(range(cut)), (1, 0, 2)[:cut] if cut > 1 else tuple(range(cut))

    def block(h, weights, out, grad, after=()):
        return glu_block(h, normed_two, cotangent, out, grad, weights, after)

    out, grad, other = block(0, glu_other, out, None)
    out, grad, own = block(0, glu_own, out, grad)
    a = Sum(dp_index, [(own, swap_pair(other))], [first_order], total_bits)
    token = a.step()
    out, grad, other = block(1, glu_other, out, grad, (token,))
    token = a.step((other,))
    out, grad, own = block(1, glu_own, out, grad, (token,))
    b = Sum(dp_index, [(own, swap_pair(other))], [second_order], total_bits)
    tokens_ab = (a.step((own,)), b.step())
    result, grad_middle, grad_gated, mixout_grads, norm2_small = middle_back(
        mp, middle, out, grad, cotangent, gated, sect_out, vecs, w1d_out, w2p_out, tokens_ab
    )
    saved = (mixed_saved, parts, xr, xs, spread)
    last = (norm2_small,)
    grads, smalls, outs, hidden = [], [], [], []
    for c in range(D // CHUNK):
        tokens_ab = tuple(v.step(last) for v in (a, b) if not v.done)
        g, small, pos_o, hid = conv_back(
            c, const, short_lengths, long_lengths, saved, taps, vecs, kr, ks, grad_gated, sin_h, cos_h, pos_out,
            hidden if c == D // CHUNK - 1 else [], tokens_ab,
        )
        last = (small,)
        grads.append(g)
        smalls.append(small)
        outs.append(pos_o)
        hidden.append(hid)
    tokens_ab = tuple(v.step(last) for v in (a, b) if not v.done)
    tokens_grad, own, other = mixin_back(
        mp, tokens, grads, sect_in, grad_middle, vecs, w1d_in, w2p_in,
        (mixout_grads, norm2_small, *smalls, *outs, hidden[-1]), tokens_ab,
    )
    got = swap_pair(other)
    size = MIX_ROWS // 2
    t = Sum(dp_index, [(own[:size], got[:size]), (own[size:], got[size:])], [first_order, second_order], total_bits)
    glu = None
    while not t.done or glu is None:
        if not t.done:
            last = (t.step(),)
        for v in (a, b):
            if not v.done:
                v.step()
        if a.done and b.done and glu is None:
            bits = jnp.concatenate([a.last_bits(), b.last_bits()])
            glu = unpack_glu(bits, [*a.pairs[0], *b.pairs[0]], last)
    mix = unpack_mixer(t.last_bits(), [*t.pairs[0], *t.pairs[1]])

    natural = lambda v: v.transpose(0, 3, 1, 2)
    down_one_g, gate_two_g, up_two_g, gate_one_g, up_one_g, down_two_g = glu
    mixout_one_g, mixout_two_g, mixin_one_g, mixin_two_g, vecs_g, taps_g, pos_g, pos_out_g = mix
    pos_own = lax.dynamic_slice_in_dim(pos_g, mp_index * 64, 64, 1)
    one = lambda v: natural(v.reshape(2, 4, 48, INNER))
    return (
        result, tokens_grad, vecs_g[0], vecs_g[1], one(mixin_one_g), mixin_two_g, taps_g, vecs_g[4], pos_own[:5], pos_own[5],
        pos_out_g, one(mixout_one_g), mixout_two_g, vecs_g[2], vecs_g[3], natural(gate_one_g), gate_two_g, natural(up_one_g),
        up_two_g, natural(down_one_g.reshape(2, 4, 48, D)), down_two_g,
    )


def solution(mesh):
    return jax.shard_map(
        local,
        mesh=mesh,
        in_specs=(
            P(("dp", "mp"), None),
            P(("dp", "mp")),
            P(("dp", "mp")),
            P(("dp", "mp"), None),
            *[P()] * 13,
            P(None, None, "mp", None),
            P("mp", None, None, None),
            P(None, None, "mp", None),
            P("mp", None, None, None),
            P("mp", None, None, None),
            P(None, None, "mp", None),
        ),
        out_specs=(
            P(("dp", "mp"), None),
            P(("dp", "mp"), None),
            P("mp"),
            P("mp"),
            P("mp", None, None, None),
            P("mp", None, None, None),
            P(None, "mp"),
            P("mp"),
            P(None, "mp"),
            P("mp"),
            P(None, "mp"),
            P("mp", None, None, None),
            P("mp", None, None, None),
            P("mp"),
            P("mp"),
            P(None, None, "mp", None),
            P("mp", None, None, None),
            P(None, None, "mp", None),
            P("mp", None, None, None),
            P("mp", None, None, None),
            P(None, None, "mp", None),
        ),
        check_vma=False,
    )
```

```python
import functools
import math

import jax
import jax.numpy as jnp
import numpy as np
from jax import lax
from jax.experimental import pallas as pl
from jax.experimental.pallas import tpu as pltpu
from jax.sharding import PartitionSpec as P

BF, F32 = jnp.bfloat16, jnp.float32
SHORT, LONG = 128, 1024
ROWS = SHORT + LONG
D = 768
INNER = 192
EPS = 1e-05
SLOWEST = math.log(100.0) / 1.5
FASTEST = math.log(100.0) / 0.3
TILE = 384
CHUNK = 256
MIB = 1024 * 1024
GLU_ONE, GLU_TWO, GLU_ROWS = 18 * INNER, 21 * INNER, 4352
MIX_IN, MIX_SMALL, MIX_POS, MIX_OUT, MIX_ROWS = 6 * INNER, 18 * INNER, 18 * INNER + 48, 18 * INNER + 64, 4096


def nn(a, b):
    return jnp.dot(a, b, preferred_element_type=F32)


def tn(a, b):
    return lax.dot_general(a, b, (((0,), (0,)), ((), ())), preferred_element_type=F32)


def nt(a, b):
    return lax.dot_general(a, b, (((1,), (1,)), ((), ())), preferred_element_type=F32)


def iota(shape, dim):
    return lax.broadcasted_iota(jnp.int32, shape, dim)


def block_of(index, width, count):
    out = jnp.zeros_like(index)
    for i in range(1, count):
        out = out + (index >= width * i).astype(jnp.int32)
    return out


def ones_where(cond):
    return jnp.where(cond, 1.0, 0.0).astype(BF)


def dense_rows(joined, base, rows):
    width, cols = joined.shape
    row = iota((rows, width), 0)
    sel = ones_where((iota((rows, width), 1) == base + (row >> 2)) & (row < INNER))
    keep = (iota((rows, cols), 0) & 3) == block_of(iota((rows, cols), 1), cols // 4, 4)
    return jnp.where(keep, nn(sel, joined), 0.0).astype(BF)


def joined_one(w1):
    return jnp.concatenate([w1[k] for k in range(4)], axis=1)


def compact_one(grad, outer):
    rows, cols = grad.shape
    keep = (iota((rows, cols), 0) & 3) == block_of(iota((rows, cols), 1), cols // 4, 4)
    kept = jnp.where(keep, grad, 0.0).astype(BF)
    stride = rows // outer
    row = iota((48 * outer, rows), 0)
    member = block_of(row, 48, outer)
    target = member * stride + (row - 48 * member) * 4
    col = iota((48 * outer, rows), 1)
    sel = ones_where((col >= target) & (col < target + 4))
    return nn(sel, kept)


def window_starts(e):
    return [2 * e * (m // 2) + (e // 128 * 128) * (m % 2) for m in range(4)]


def pad_rows(width):
    row, col = iota((256, INNER), 0), iota((256, INNER), 1)
    a, q = row >> 6, row & 63
    return ones_where((col == (a * 48 + q if width == 48 else q * 4 + a)) & (q < 48))


def shift_columns(e, k):
    width = e + 64
    return ones_where(iota((e, width), 1) == iota((e, width), 0) + 64 * (k % 2))


def mixer_weights(w1, w2, w1p, w2p, e):
    for i in range(4):
        first = nn(pad_rows(48), w1[i]).astype(BF)
        w1p[i] = nn(first, shift_columns(INNER, i)).astype(BF)
        second = nn(pad_rows(4), w2[i].reshape(INNER, e)).astype(BF)
        w2p[i] = nn(second, shift_columns(e, i)).astype(BF)


def exchange(blocks):
    rows = blocks[0].shape[0]
    low = iota((rows, 128), 1) < 64
    parts = [[b[:, :128], b[:, 128:]] for b in blocks]
    turned = [[pltpu.roll(v, 64, 1) for v in p] for p in parts]
    out = []
    for m in range(4):
        v = m // 2
        pieces = []
        for p in (0, 2):
            if m % 2 == 0:
                pieces.append(jnp.where(low, parts[p][v], turned[p + 1][v]))
            else:
                pieces.append(jnp.where(low, turned[p][v], parts[p + 1][v]))
        out.append(jnp.concatenate(pieces, axis=1).astype(BF))
    return out


def join(windows):
    out = []
    for a, b in (windows[:2], windows[2:]):
        n = a.shape[1] - 128
        out += [a[:, :n], a[:, n:] + b[:, :128], b[:, 128:]]
    return jnp.concatenate(out, axis=1)


def sections(x, w1p):
    return exchange([nt(x[:, s : s + 256], w1p[k]) for k, s in enumerate(window_starts(INNER))])


def pair_columns(a, b):
    n = a.shape[1] - 128
    lane = iota((a.shape[0], 128), 1)
    return jnp.concatenate([a[:, :n], jnp.where(lane < 64, a[:, n:], b[:, :128]), b[:, 128:]], axis=1)


def block_grads(width, left, right):
    return tn(pad_rows(width), tn(left, right).astype(BF))


def norm_parts(x):
    centred = x - jnp.mean(x, axis=-1, keepdims=True)
    rstd = lax.rsqrt(jnp.mean(centred * centred, axis=-1, keepdims=True) + EPS)
    return centred * rstd, rstd


def norm_back(grad, xhat, rstd, gain):
    scaled = grad * gain
    first = jnp.mean(scaled, axis=-1, keepdims=True)
    second = jnp.mean(scaled * xhat, axis=-1, keepdims=True)
    return rstd * (scaled - first - xhat * second)


LIMITS = {"mixer_input": 20, "filters": 10, "conv_forward": 14, "mixer_output": 8, "feed_forward": 20, "middle_back": 18, "conv_back": 21, "mixer_input_back": 18, "mixer_input_grads": 20}
WHOLE, PINNED, FAR = "whole", "pinned", "far"


def by_rows(*shape):
    dim = len(shape) - 2
    block = shape[:dim] + (TILE,) + shape[dim + 1 :]
    return pl.BlockSpec(block, lambda i: (0,) * dim + (i, 0))


def by_columns(*shape):
    lead = len(shape) - 1
    return pl.BlockSpec(shape[:-1] + (CHUNK,), lambda i: (0,) * lead + (i,))


def call(kernel, name, outs, scratch, limit, us, *args, grid=None, aliases=None, after=()):
    inner = kernel
    count, skip = len(args), len(after)
    if skip:
        kernel = lambda *refs: inner(*refs[:count], *refs[count + skip :])
    in_specs, operands, out_specs, out_shape = [], [], [], []
    for arg in args:
        arg, mode = arg if isinstance(arg, tuple) else (arg, WHOLE)
        if arg.dtype == jnp.int32:
            in_specs.append(pl.BlockSpec(memory_space=pltpu.SMEM))
        elif mode == FAR:
            arg = pltpu.with_memory_space_constraint(arg, pltpu.HBM)
            in_specs.append(pl.BlockSpec(memory_space=pl.ANY))
        elif isinstance(mode, pl.BlockSpec):
            arg = pltpu.with_memory_space_constraint(arg, pltpu.HBM)
            in_specs.append(mode)
        else:
            if mode == PINNED:
                arg = pltpu.with_memory_space_constraint(arg, pltpu.VMEM)
            in_specs.append(pl.BlockSpec(memory_space=pltpu.VMEM))
        operands.append(arg)
    for arg in after:
        in_specs.append(pl.BlockSpec(memory_space=pl.ANY))
        operands.append(arg)
    for shape, dtype, *mode in outs:
        mode = mode[0] if mode else WHOLE
        if mode == FAR or isinstance(mode, pl.BlockSpec):
            out_specs.append(pl.BlockSpec(memory_space=pl.ANY) if mode == FAR else mode)
            out_shape.append(pltpu.HBM(shape, dtype))
        else:
            out_specs.append(pl.BlockSpec(memory_space=pltpu.VMEM))
            out_shape.append(pltpu.VMEM(shape, dtype) if mode == PINNED else jax.ShapeDtypeStruct(shape, dtype))
    return pl.pallas_call(
        kernel,
        out_shape=out_shape,
        in_specs=in_specs,
        out_specs=out_specs,
        grid=(grid,) if grid else (),
        scratch_shapes=[pltpu.VMEM(*v) if isinstance(v, tuple) else v for v in scratch],
        input_output_aliases=aliases or {},
        cost_estimate=pl.CostEstimate(flops=int(us * 1.0e9), bytes_accessed=0, transcendentals=0),
        compiler_params=pltpu.CompilerParams(vmem_limit_bytes=LIMITS.get(name, 6) * MIB),
        name=name,
    )(*operands)


def first_step(body):
    pl.when(pl.program_id(0) == 0)(body)


def last_step(body):
    pl.when(pl.program_id(0) == pl.num_programs(0) - 1)(body)


def grid_part(size):
    start = pl.multiple_of(pl.program_id(0) * size, size)
    return pl.ds(start, size), start


def tables():
    def phases(n, f, t):
        whole = ((2 * f[:, None] + 1) * (2 * t[None, :] + 1)) % (8 * n)
        angle = whole.astype(np.float64) * (math.pi / (4 * n))
        return np.cos(angle), np.sin(angle)

    half = LONG // 2
    low = np.arange(half, dtype=np.int64)
    short = np.concatenate(phases(SHORT, np.arange(SHORT), np.arange(SHORT)), axis=1)
    parts = [np.concatenate(phases(LONG, low, 2 * low + odd), axis=0) for odd in (0, 1)]
    fraction = np.concatenate([np.arange(SHORT) / SHORT, np.arange(LONG) / LONG])
    order = np.concatenate([low, LONG - 1 - low])
    shift = np.concatenate(
        [(2 * f + 1) * (math.pi / (4 * n)) for f, n in ((np.arange(SHORT), SHORT), (order, LONG))]
    )
    aux = np.zeros((ROWS, 8), np.float32)
    aux[:, 0] = fraction
    for i, band in enumerate((1, 2)):
        aux[:, 1 + i] = np.cos(2.0 * math.pi * band * fraction)
        aux[:, 3 + i] = np.sin(2.0 * math.pi * band * fraction)
    aux[:, 5] = np.cos(shift)
    aux[:, 6] = np.sin(shift)
    aux[:, 7] = 1.0
    rates = SLOWEST + (FASTEST - SLOWEST) * np.arange(D) / (D - 1)
    low_type = lambda t: jnp.asarray(t.astype(np.float32), BF)
    return (
        (low_type(short), *[low_type(p) for p in parts], *[low_type(np.ascontiguousarray(p.T)) for p in parts]),
        jnp.asarray(aux),
        jnp.asarray(rates[None].astype(np.float32)),
    )


def scale_rows(shape):
    return jnp.where(iota(shape, 0) < SHORT, 1.0 / SHORT, 1.0 / LONG)


def parity(odd):
    return pl.ds(odd, LONG // 2, stride=2)


LANES = [slice(i, i + 128) for i in range(0, CHUNK, 128)]


def transform(v, tabs, room):
    ts, fe, fo, _, _ = tabs
    head = v[:SHORT].astype(BF)
    for i, lanes in enumerate(LANES):
        room[i] = v[SHORT:, lanes]
    even, odd = [jnp.concatenate([room[i, parity(p)] for i in range(2)], axis=1).astype(BF) for p in (0, 1)]
    e, o = nn(fe[...], even), nn(fo[...], odd)
    h = LONG // 2
    real = jnp.concatenate([nn(ts[:, :SHORT], head), e[:h] + o[:h], e[h:] - o[h:]], axis=0)
    imag = jnp.concatenate([nn(ts[:, SHORT:], head), e[h:] + o[h:], e[:h] - o[:h]], axis=0)
    return real, imag


def restore(real, imag, tabs, room):
    ts, _, _, ie, io = tabs
    h = SHORT + LONG // 2
    head = nn(ts[...], jnp.concatenate([real[:SHORT], imag[:SHORT]], axis=0).astype(BF))
    r0, r1, i0, i1 = real[SHORT:h], real[h:], imag[SHORT:h], imag[h:]
    even = nn(ie[...], jnp.concatenate([r0 + i1, i0 + r1], axis=0).astype(BF))
    odd = nn(io[...], jnp.concatenate([r0 - i1, i0 - r1], axis=0).astype(BF))
    for i, lanes in enumerate(LANES):
        room[i, parity(0)] = even[:, lanes]
        room[i, parity(1)] = odd[:, lanes]
    return jnp.concatenate([head, jnp.concatenate([room[0], room[1]], axis=1)], axis=0)


ROOM = ((2, LONG, 128), F32)


def chunks(body):
    def step(c, carry):
        body(pl.ds(pl.multiple_of(c * CHUNK, CHUNK), CHUNK))
        return carry

    lax.fori_loop(0, D // CHUNK, step, 0)


def tiles(body, rows=ROWS, tile=TILE):
    def step(i, carry):
        body(pl.ds(pl.multiple_of(i * tile, tile), tile), i * tile)
        return carry

    lax.fori_loop(0, rows // tile, step, 0)


def small_kernel(*refs):
    far, (vecs_o, taps_o), near, sems = refs[:6], refs[6:8], refs[8:14], refs[14]
    copies = [pltpu.make_async_copy(f, n, sems.at[i]) for i, (f, n) in enumerate(zip(far, near))]
    for copy in copies:
        copy.start()
    for copy in copies:
        copy.wait()
    vecs_o[...] = jnp.concatenate([v[...].reshape(1, D) for v in near[:5]] + [jnp.zeros((3, D), F32)], axis=0)
    taps = [near[5][i : i + 1, j * D : (j + 1) * D] for j in range(3) for i in range(3)]
    taps_o[...] = jnp.concatenate(taps + [jnp.zeros((7, D), F32)], axis=0)


def small_params(*args):
    return call(
        small_kernel, "small_parameters", [((8, D), F32), ((16, D), F32)],
        [((D,), F32)] * 5 + [((3, 3 * D), F32), pltpu.SemaphoreType.DMA((6,))], 8, 1, *[(v, FAR) for v in args],
    )


def filter_kernel(aux, pos_in, pos_bias, pos_out, rates, *refs):
    *tabs, sin_o, cos_o, kr_o, ks_o, room = refs
    pre = jnp.broadcast_to(pos_bias[...], (ROWS, 128))
    for i in range(5):
        pre = pre + aux[:, i : i + 1] * pos_in[i : i + 1, :]
    sin_o[...] = jnp.sin(pre)
    cos_o[...] = jnp.cos(pre)

    def body(cols):
        hidden = sin_o[...]
        high = hidden.astype(BF)
        low = (hidden - high.astype(F32)).astype(BF)
        w = pos_out[:, cols]
        w_high = w.astype(BF)
        w_low = (w - w_high.astype(F32)).astype(BF)
        shaped = nn(high, w_high) + nn(high, w_low) + nn(low, w_high)
        kern = shaped * jnp.exp(-aux[:, 0:1] * rates[:, cols])
        a, b = transform(kern, tabs, room)
        cos_h, sin_h = aux[:, 5:6], aux[:, 6:7]
        scale = scale_rows((ROWS, 1))
        kr_o[:, cols] = ((cos_h * a + sin_h * b) * scale).astype(BF)
        ks_o[:, cols] = ((cos_h * b - sin_h * a) * scale).astype(BF)

    chunks(body)


def make_filter(const, pos_in, pos_bias, pos_out, after):
    tabs, aux, rates = const
    return call(
        filter_kernel, "filters", [((ROWS, 128), F32, PINNED)] * 2 + [((ROWS, D), BF, PINNED)] * 2, [ROOM], 10, 8,
        aux, pos_in, pos_bias, pos_out, rates, *tabs, after=after,
    )


def row_valid(short_len, long_len, start, rows):
    row = iota((rows, 1), 0) + start
    limit = jnp.where(row < SHORT, short_len[0], long_len[0] + SHORT)
    return row < limit


def mixin_kernel(short_len, long_len, tokens, vecs, w1, w2, mixed_o, sect_o, w1p, w2p):
    @first_step
    def _():
        mixer_weights(w1, w2, w1p, w2p, 576)

    rows, start = grid_part(TILE)
    xhat, _ = norm_parts(tokens[...].astype(F32))
    normed = (xhat * vecs[0:1] + vecs[1:2]).astype(BF)
    sect = sections(normed, w1p)
    for m in range(4):
        sect_o[:, m * 256 : (m + 1) * 256] = sect[m]
    valid = row_valid(short_len, long_len, start, TILE)
    full = jnp.where(valid, join([nn(sect[m], w2p[m]) for m in range(4)]), 0.0).astype(BF)
    for j in range(3):
        mixed_o[j, rows] = full[:, j * D : (j + 1) * D]


def mixin_forward(short_len, long_len, tokens, vecs, w1, w2, after):
    return call(
        mixin_kernel, "mixer_input", [((3, ROWS, D), BF, PINNED), ((ROWS, 1024), BF, by_rows(ROWS, 1024))],
        [((4, 256, 256), BF), ((4, 256, 640), BF)], 22, 7,
        short_len, long_len, (tokens, by_rows(ROWS, D)), vecs, w1, w2, grid=ROWS // TILE, after=after,
    )


def edges(shape):
    row = iota(shape, 0)
    first = (row == 0) | (row == SHORT)
    last = (row == SHORT - 1) | (row == ROWS - 1)
    return first, last


def before(v, first):
    return jnp.where(first, 0.0, pltpu.roll(v, 1, 0))


def after(v, last):
    return jnp.where(last, 0.0, pltpu.roll(v, ROWS - 1, 0))


def tap_rows(taps, cols, j):
    return [taps[3 * j + i : 3 * j + i + 1, cols] for i in range(3)]


def conv_forward_kernel(mixed, taps, vecs, kr, ks, *refs):
    *tabs, gated_o, spread_o, xr_o, xs_o, parts_o, saved_o, sem, room = refs
    save = pltpu.make_async_copy(mixed, saved_o, sem.at[0])
    first_step(save.start)
    last_step(save.wait)
    cols, _ = grid_part(CHUNK)
    first, last = edges((ROWS, CHUNK))
    parts = []
    for j in range(3):
        m = mixed[j, :, cols].astype(F32)
        t0, t1, t2 = tap_rows(taps, cols, j)
        parts.append(t0 * before(m, first) + t1 * m + t2 * after(m, last))
        parts_o[j] = parts[j].astype(BF)
    product = parts[0] * parts[2]
    real, imag = transform(product, tabs, room)
    xr_o[...] = real.astype(BF)
    xs_o[...] = imag.astype(BF)
    a, b = kr[:, cols].astype(F32), ks[:, cols].astype(F32)
    spread = restore(real * a - imag * b, real * b + imag * a, tabs, room)
    spread = spread + vecs[4:5, cols] * product
    spread_o[...] = spread.astype(BF)
    gated_o[:, cols] = (spread * parts[1]).astype(BF)


def conv_forward(const, mixed, taps, vecs, kr, ks):
    column = ((ROWS, D), BF, by_columns(ROWS, D))
    return call(
        conv_forward_kernel, "conv_forward",
        [((ROWS, D), BF, PINNED), column, column, column, ((3, ROWS, D), BF, by_columns(3, ROWS, D)),
         ((3, ROWS, D), BF, FAR)], [pltpu.SemaphoreType.DMA((1,)), ROOM], 22, 12,
        (mixed, PINNED), taps, vecs, (kr, PINNED), (ks, PINNED), *const[0], grid=D // CHUNK,
    )


def conv_back_kernel(
    c, short_len, long_len, mixed_h, parts_h, taps, vecs, kr, ks, xr_h, xs_h, spread_h, grad_gated, sin_h, cos_h, aux, pos_out,
    rates, *rest
):
    tabs = rest[:5]
    *earlier, grad_o, small_o, pos_out_o, hidden_o, mixed, parts, xr, xs, spread, sems, room = rest[5:]
    cols = slice(c * CHUNK, (c + 1) * CHUNK)
    copies = [
        pltpu.make_async_copy(far.at[..., cols], near, sems.at[i])
        for i, (far, near) in enumerate(((parts_h, parts), (xr_h, xr), (xs_h, xs), (spread_h, spread), (mixed_h, mixed)))
    ]
    for copy in copies:
        copy.start()
    first, last = edges((ROWS, CHUNK))
    gg = grad_gated[:, cols].astype(F32)
    copies[0].wait()
    grad_spread = gg * parts[1].astype(F32)
    real, imag = transform(grad_spread, tabs, room)
    a, b = kr[:, cols].astype(F32), ks[:, cols].astype(F32)
    grad_product = restore(a * real + b * imag, a * imag - b * real, tabs, room)
    grad_product = grad_product + vecs[4:5, cols] * grad_spread
    copies[1].wait()
    copies[2].wait()
    x_real, x_imag = xr[...].astype(F32), xs[...].astype(F32)
    z_real = x_real * real + x_imag * imag
    z_imag = x_real * imag - x_imag * real
    cos_p, sin_p = aux[:, 5:6], aux[:, 6:7]
    grad_kernel = restore(cos_p * z_real - sin_p * z_imag, cos_p * z_imag + sin_p * z_real, tabs, room)
    shaped_grad = (grad_kernel * (scale_rows((ROWS, 1)) * jnp.exp(-aux[:, 0:1] * rates[:, cols]))).astype(BF)
    pos_out_o[...] = tn(sin_h[...].astype(BF), shaped_grad)
    hidden = nt(shaped_grad, pos_out[:, cols].astype(BF))
    copies[3].wait()
    copies[4].wait()
    front = parts[0].astype(F32)
    value = parts[2].astype(F32)
    grads = (grad_product * value, gg * spread[...].astype(F32), grad_product * front)
    valid = row_valid(short_len, long_len, 0, ROWS)
    small = []
    for j in range(3):
        m = mixed[j].astype(F32)
        g = grads[j]
        up, down = after(g, last), before(g, first)
        t0, t1, t2 = tap_rows(taps, cols, j)
        small += [jnp.sum(v * m, axis=0, keepdims=True) for v in (up, g, down)]
        grad_o[j] = jnp.where(valid, t0 * up + t1 * g + t2 * down, 0.0).astype(BF)
    small.append(jnp.sum(grad_spread * front * value, axis=0, keepdims=True))
    small.append(jnp.zeros((6, CHUNK), F32))
    small_o[...] = jnp.concatenate(small, axis=0)
    if not earlier:
        hidden_o[...] = hidden
    else:
        pre = (hidden + earlier[0][...] + earlier[1][...]) * cos_h[...]
        hidden_o[...] = lax.dot_general(
            aux[...], pre, (((0,), (0,)), ((), ())), precision=lax.Precision.HIGHEST, preferred_element_type=F32
        )


def conv_back(c, const, short_len, long_len, saved, taps, vecs, kr, ks, grad_gated, sin_h, cos_h, pos_out, earlier, after):
    tabs, aux, rates = const
    mixed, parts, xr, xs, spread = saved
    final = len(earlier) > 0
    one = ((ROWS, CHUNK), BF)
    three = ((3, ROWS, CHUNK), BF)
    return call(
        functools.partial(conv_back_kernel, c), "conv_back",
        [(*three, PINNED), ((16, CHUNK), F32), ((128, CHUNK), F32)] + ([((8, 128), F32)] if final else [((ROWS, 128), F32, PINNED)]),
        [three, three, one, one, one, pltpu.SemaphoreType.DMA((5,)), ROOM], 30, 8,
        short_len, long_len, (mixed, FAR), (parts, FAR), taps, vecs, (kr, PINNED), (ks, PINNED), (xr, FAR), (xs, FAR),
        (spread, FAR), (grad_gated, PINNED), (sin_h, PINNED), (cos_h, PINNED), aux, pos_out, rates, *tabs,
        *[(v, PINNED) for v in earlier], after=after,
    )


def mixout_kernel(tokens, gated, vecs, w1, w2, middle_o, out_o, normed_o, sect_o, w1p, w2p):
    @first_step
    def _():
        mixer_weights(w1, w2, w1p, w2p, INNER)

    rows, _ = grid_part(TILE)
    sect = sections(gated[rows], w1p)
    for m in range(4):
        sect_o[rows, m * 256 : (m + 1) * 256] = sect[m]
    middle = tokens[...].astype(F32) + join([nn(sect[m], w2p[m]) for m in range(4)])
    middle_o[...] = middle
    out_o[rows] = middle
    xhat, _ = norm_parts(middle)
    normed_o[rows] = (xhat * vecs[2:3] + vecs[3:4]).astype(BF)


def mixout_forward(tokens, gated, vecs, w1, w2, after):
    tile = by_rows(ROWS, D)
    return call(
        mixout_kernel, "mixer_output",
        [
            ((ROWS, D), F32, tile), ((ROWS, D), F32, PINNED), ((ROWS, D), BF, PINNED), ((ROWS, 1024), BF, PINNED),
            ((4, 256, 256), BF, PINNED), ((4, 256, 256), BF, PINNED),
        ],
        [], 18, 6, (tokens, tile), (gated, PINNED), vecs, w1, w2, grid=ROWS // TILE, after=after,
    )


def glu_kernel(
    h, normed, cot, out_in, grad_in, g1, g2, u1, u2, d1, d2, out_o, grad_o, grads_o,
    g1d, u1d, d2d, hidden_s, gate_s, up_s, sect_s, gsect_s, usect_s, grad_sect_s, ggs_s, gus_s
):
    g1d[...] = dense_rows(joined_one(g1), h * 48, INNER)
    u1d[...] = dense_rows(joined_one(u1), h * 48, INNER)
    col = iota((INNER, D), 1)
    keep = block_of(iota((INNER, D), 0), 48, 4) == block_of(col, INNER, 4)
    tile = ones_where(col - INNER * block_of(col, INNER, 4) == iota((INNER, D), 0))
    d2_rows = jnp.concatenate([d2[m, :, h, :] for m in range(4)], axis=0)
    d2d[...] = jnp.where(keep, nn(d2_rows, tile), 0.0).astype(BF)
    g2r = g2[h].reshape(INNER, D)
    u2r = u2[h].reshape(INNER, D)
    d1r = d1[h]

    def body(rows, start):
        x = normed[rows]
        gate_sect = nt(x, g1d[...]).astype(BF)
        up_sect = nt(x, u1d[...]).astype(BF)
        gate = nn(gate_sect, g2r)
        up = nn(up_sect, u2r)
        sig = jax.nn.sigmoid(gate)
        act = gate * sig
        hidden = (act * up).astype(BF)
        sect = nt(hidden, d1r).astype(BF)
        out_o[rows] = out_in[rows] + nn(sect, d2d[...])
        grad_sect = nt(cot[rows], d2d[...]).astype(BF)
        grad_hidden = nn(grad_sect, d1r)
        grad_gate = (grad_hidden * up * (sig * (1.0 + gate * (1.0 - sig)))).astype(BF)
        grad_up = (grad_hidden * act).astype(BF)
        ggs = nt(grad_gate, g2r).astype(BF)
        gus = nt(grad_up, u2r).astype(BF)
        piece = nn(ggs, g1d[...]) + nn(gus, u1d[...])
        grad_o[rows] = piece if grad_in is None else grad_in[rows] + piece
        hidden_s[rows] = hidden
        gate_s[rows] = grad_gate
        up_s[rows] = grad_up
        sect_s[rows] = sect
        gsect_s[rows] = gate_sect
        usect_s[rows] = up_sect
        grad_sect_s[rows] = grad_sect
        ggs_s[rows] = ggs
        gus_s[rows] = gus

    tiles(body)
    for i, (a, b) in enumerate(((grad_sect_s, hidden_s), (gsect_s, gate_s), (usect_s, up_s))):
        term = tn(a[...], b[...]).astype(BF)
        for c in range(6):
            start = (i * 6 + c) * INNER
            grads_o[start : start + INNER] = term[:, c * 128 : (c + 1) * 128]
    for i, a in enumerate((ggs_s, gus_s)):
        one = compact_one(tn(a[...], normed[...]), 1).astype(BF)
        for c in range(6):
            start = GLU_ONE + 96 * c + 48 * i
            grads_o[start : start + 48] = one[:, c * 128 : (c + 1) * 128]
    kept = jnp.where(keep, tn(sect_s[...], cot[...]), 0.0).astype(BF)
    row = iota((D, 256), 0)
    two = nn(kept, ones_where(row - INNER * block_of(row, INNER, 4) == iota((D, 256), 1)))
    grads_o[GLU_TWO : GLU_TWO + INNER] = two[:, :128].astype(BF)
    rest = two[:96, 128:] + pltpu.roll(two[96:, 128:], 64, 1)
    grads_o[GLU_TWO + INNER : GLU_TWO + INNER + 96] = rest.astype(BF)
    grads_o[GLU_TWO + INNER + 96 :] = jnp.zeros((32, 128), BF)


def glu_block(h, normed, cot, out, grad, weights, after=()):
    kernel = functools.partial(glu_kernel, h)
    args = [(normed, PINNED), cot, (out, PINNED), (grad, PINNED), *weights]
    if grad is None:
        del args[3]
        kernel = lambda a, b, c, *rest: glu_kernel(h, a, b, c, None, *rest)
    rows = ((ROWS, INNER), BF)
    return call(
        kernel, "feed_forward",
        [((ROWS, D), F32, PINNED)] * 2 + [((GLU_ROWS, 128), BF)],
        [((INNER, D), BF)] * 3 + [((ROWS, D), BF)] * 3 + [rows] * 6, 26, 12, *args,
        aliases={2: 0} if grad is None else {2: 0, 3: 1}, after=after,
    )


def column_sums(pair):
    rows = [jnp.sum(v, axis=0, keepdims=True) for v in pair]
    return jnp.concatenate(rows + [jnp.zeros((6, D), F32)], axis=0)


def slot_of(mp, half):
    return jnp.where(mp[0] == half, 0, 1)


def middle_back_kernel(
    mp, middle, out, grad_in, cot, gated, sect, vecs, w1p, w2p, result_o, grad_middle_o, grad_gated_o, grads_o, small_o,
    branch_s, grad_sect_s
):
    @first_step
    def _():
        small_o[...] = jnp.zeros((8, D), F32)

    rows, _ = grid_part(TILE)
    result_o[...] = out[rows].astype(BF)
    grad = grad_in[rows]
    xhat, rstd = norm_parts(middle[...])
    small_o[...] += column_sums((grad * xhat, grad))
    grad_middle = cot[rows].astype(F32) + norm_back(grad, xhat, rstd, vecs[2:3])
    grad_middle_o[...] = grad_middle
    branch = grad_middle.astype(BF)
    branch_s[rows] = branch
    starts = window_starts(INNER)
    grad_sect = exchange([nt(branch[:, s : s + 256], w2p[m]) for m, s in enumerate(starts)])
    for k in range(4):
        grad_sect_s[rows, k * 256 : (k + 1) * 256] = grad_sect[k]
    grad_gated_o[rows] = join([nn(grad_sect[k], w1p[k]) for k in range(4)]).astype(BF)

    @last_step
    def _():
        part = lambda i: slice(i * 256, (i + 1) * 256)
        for half in range(2):
            slot = slot_of(mp, half)
            pair = (2 * half, 2 * half + 1)
            one = pair_columns(*[block_grads(48, grad_sect_s[:, part(k)], gated[:, starts[k] : starts[k] + 256]) for k in pair])
            two = pair_columns(*[block_grads(4, sect[:, part(m)], branch_s[:, starts[m] : starts[m] + 256]) for m in pair])
            for i, v in enumerate((one, two)):
                for c in range(3):
                    at = (3 * i + c) * INNER
                    grads_o[slot, at : at + INNER] = v[:, c * 128 : (c + 1) * 128].astype(BF)


def middle_back(mp, middle, out, grad, cot, gated, sect, vecs, w1p, w2p, after):
    tile = by_rows(ROWS, D)
    return call(
        middle_back_kernel, "middle_back",
        [((ROWS, D), BF, tile), ((ROWS, D), F32, tile), ((ROWS, D), BF, PINNED), ((2, 6 * INNER, 128), BF), ((8, D), F32)],
        [((ROWS, D), BF), ((ROWS, 1024), BF)], 26, 10, mp, (middle, tile), (out, PINNED), (grad, PINNED), cot, (gated, PINNED),
        (sect, PINNED), vecs, (w1p, PINNED), (w2p, PINNED), grid=ROWS // TILE, after=after,
    )


def mixed_window(grads, start, rows):
    out, width = [], 640
    while width:
        j, at = start // D, start % D
        c, at = at // CHUNK, at % CHUNK
        n = min(width, CHUNK - at)
        out.append(grads[c][j, rows, at : at + n])
        start, width = start + n, width - n
    return jnp.concatenate(out, axis=1)


def mixin_back_kernel(tokens, m0, m1, m2, grad_middle, vecs, w1, w2, tokens_o, norm1, normed_o, grad_sect_o, w1p, w2p):
    @first_step
    def _():
        mixer_weights(w1, w2, w1p, w2p, 576)
        norm1[...] = jnp.zeros((8, D), F32)

    rows, _ = grid_part(TILE)
    xhat, rstd = norm_parts(tokens[...].astype(F32))
    normed_o[rows] = (xhat * vecs[0:1] + vecs[1:2]).astype(BF)
    windows = [mixed_window((m0, m1, m2), s, rows) for s in window_starts(576)]
    grad_sect = exchange([nt(v, w2p[m]) for m, v in enumerate(windows)])
    for k in range(4):
        grad_sect_o[rows, k * 256 : (k + 1) * 256] = grad_sect[k]
    grad = join([nn(grad_sect[k], w1p[k]) for k in range(4)])
    norm1[...] += column_sums((grad * xhat, grad))
    tokens_o[...] = (grad_middle[...] + norm_back(grad, xhat, rstd, vecs[0:1])).astype(BF)


def mixin_back(tokens, grads, grad_middle, vecs, w1, w2, after):
    tile = by_rows(ROWS, D)
    return call(
        mixin_back_kernel, "mixer_input_back",
        [((ROWS, D), BF, tile), ((8, D), F32), ((ROWS, D), BF, PINNED), ((ROWS, 1024), BF, PINNED)],
        [((4, 256, 256), BF), ((4, 256, 640), BF)], 26, 9, (tokens, tile), *[(g, PINNED) for g in grads],
        (grad_middle, tile), vecs, w1, w2, grid=ROWS // TILE, after=after,
    )


def mixin_grads_kernel(
    mp, m0, m1, m2, sect, normed, grad_sect, mixout_grads, norm1, norm2, c0, c1, c2, p0, p1, p2, pos, own_o, other_o
):
    part = lambda i: slice(i * 256, (i + 1) * 256)
    blocks = []
    for half in range(2):
        block = []
        pair = (2 * half, 2 * half + 1)
        starts = window_starts(INNER)
        one = pair_columns(*[block_grads(48, grad_sect[:, part(k)], normed[:, starts[k] : starts[k] + 256]) for k in pair])
        starts = window_starts(576)
        two = pair_columns(
            *[block_grads(4, sect[:, part(m)], mixed_window((m0, m1, m2), starts[m], slice(None))) for m in pair]
        )
        for at, v in ((MIX_IN, one), (MIX_IN + 3 * INNER, two)):
            for c in range(v.shape[1] // 128):
                block.append((at + c * INNER, v[:, c * 128 : (c + 1) * 128].astype(BF)))
        cut = lambda v, r, col: v[r : r + 1, col : col + 128]
        conv = lambda r, col: (c0, c1, c2)[col // CHUNK][r : r + 1, col % CHUNK : col % CHUNK + 128]
        small = []
        for v, r in ((norm1, 0), (norm1, 1), (norm2, 0), (norm2, 1)):
            small += [cut(v, r, half * 384 + 128 * i) for i in range(3)]
        small += [conv(9, half * 384 + 128 * i) for i in range(3)]
        for tap in range(3):
            for i in range(9):
                col = half * 1152 + 128 * i
                small.append(conv(3 * (col // D) + tap, col % D))
        small.append(jnp.zeros((6, 128), F32))
        block.append((MIX_SMALL, jnp.concatenate(small, axis=0).astype(BF)))
        block.append((MIX_POS, jnp.concatenate([pos[...], jnp.zeros((8, 128), F32)], axis=0).astype(BF)))
        for i in range(3):
            col = half * 384 + 128 * i
            block.append((MIX_OUT + 128 * i, (p0, p1, p2)[col // CHUNK][:, col % CHUNK : col % CHUNK + 128].astype(BF)))
        block.append((MIX_OUT + 384, jnp.zeros((MIX_ROWS - MIX_OUT - 384, 128), BF)))
        blocks.append(block)
    for half in range(2):
        block = blocks[half]

        @pl.when(mp[0] == half)
        def _():
            for at, piece in block:
                own_o[at : at + piece.shape[0]] = piece

        @pl.when(mp[0] != half)
        def _():
            for at, piece in block:
                other_o[at : at + piece.shape[0]] = piece

    own_o[:MIX_IN] = mixout_grads[0]
    other_o[:MIX_IN] = mixout_grads[1]


def mixin_grads(mp, grads, sect, normed, grad_sect, extra, after):
    return call(
        mixin_grads_kernel, "mixer_input_grads", [((MIX_ROWS, 128), BF)] * 2, [], 20, 6, mp, *[(g, PINNED) for g in grads],
        sect, (normed, PINNED), (grad_sect, PINNED), *extra, after=after,
    )


def swap_pair(v):
    n = lax.axis_size("mp")
    return lax.ppermute(v, "mp", [(i, (i + 1) % n) for i in range(n)])


def swap_bit(v, bit):
    n = lax.axis_size("dp")
    return lax.ppermute(v, "dp", [(i, i ^ (1 << bit)) for i in range(n)])


def sum_of(a, b):
    return (a.astype(F32) + b.astype(F32)).astype(BF)


def part_of(ref, bit, half):
    return ref[pl.ds(pl.multiple_of(bit * half, 16), half)]


def split_kernel(bits, place, *refs):
    n = len(bits)
    for i in range(n):
        keep, got = refs[2 * i], refs[2 * i + 1]
        send_o, keep_o = refs[2 * n + 2 * i], refs[2 * n + 2 * i + 1]
        half, bit = send_o.shape[0], place[bits[i]]
        send_o[...] = sum_of(part_of(keep, 1 - bit, half), part_of(got, 1 - bit, half))
        keep_o[...] = sum_of(part_of(keep, bit, half), part_of(got, bit, half))


def split(place, bits, pairs, after=()):
    outs = [((p[0].shape[0] // 2, 128), BF) for p in pairs for _ in range(2)]
    flat = [v for p in pairs for v in p]
    got = call(functools.partial(split_kernel, bits), "split", outs, [], 8, 1, place, *flat, after=after)
    return [(got[2 * i], got[2 * i + 1]) for i in range(len(pairs))]


def sum_kernel(mine, got, out):
    out[...] = sum_of(mine[...], got[...])


def total(mine, got, after=()):
    return call(sum_kernel, "sum", [(mine.shape, BF)], [], 8, 1, mine, got, after=after)[0]


def merge_kernel(bits, place, *refs):
    n = len(bits)
    for i in range(n):
        mine, got, out = refs[2 * i], refs[2 * i + 1], refs[2 * n + i]
        half, bit = mine.shape[0], place[bits[i]]
        out[pl.ds(pl.multiple_of(bit * half, 16), half)] = mine[...]
        out[pl.ds(pl.multiple_of((1 - bit) * half, 16), half)] = got[...]


def merge(place, bits, pairs, after=()):
    outs = [((2 * p[0].shape[0], 128), BF) for p in pairs]
    flat = [v for p in pairs for v in p]
    return call(functools.partial(merge_kernel, bits), "merge", outs, [], 8, 1, place, *flat, after=after)


def sum_steps(place, own, got, order, rest):
    after = yield None
    pair = (own, got)
    for bit in order:
        ((send, keep),) = split(place, (bit,), [pair], after)
        pair = (keep, swap_bit(send, bit))
        after = yield keep, pair, False
    for i, bit in enumerate((*rest, None)):
        out = total(*pair, after)
        if bit is not None:
            pair = (out, swap_bit(out, bit))
            after = yield out, pair, False
    for bit in reversed(order):
        pair = (out, swap_bit(out, bit))
        after = yield out, pair, bit == order[0]
        if bit != order[0]:
            (out,) = merge(place, (bit,), [pair], after)


class Steps:
    def __init__(self, *args):
        self.run = sum_steps(*args)
        next(self.run)
        self.halves, self.done = None, False

    def step(self, after=()):
        token, self.halves, self.done = self.run.send(after)
        return token


def second_kernel(place, ka, ra, kb, rb, send_a, send_b, keep):
    for i, (mine, got, send, bit) in enumerate(((ka, ra, send_a, place[1]), (kb, rb, send_b, place[0]))):
        half = send.shape[0]
        send[...] = sum_of(part_of(mine, 1 - bit, half), part_of(got, 1 - bit, half))
        keep[i * half : (i + 1) * half] = sum_of(part_of(mine, bit, half), part_of(got, bit, half))


def third_kernel(place, keep, ra, rb, send_o, keep_o):
    size = ra.shape[0]
    half, bit = size // 2, place[2]
    for i, got in enumerate((ra, rb)):
        base = i * size
        for out, b in ((send_o, 1 - bit), (keep_o, bit)):
            rows = pl.ds(pl.multiple_of(base + b * half, 16), half)
            out[i * half : (i + 1) * half] = sum_of(keep[rows], part_of(got, b, half))


def fifth_kernel(place, mine, got, a, b):
    half, bit = mine.shape[0] // 2, place[2]
    for i, out in enumerate((a, b)):
        rows = slice(i * half, (i + 1) * half)
        out[pl.ds(pl.multiple_of(bit * half, 16), half)] = mine[rows]
        out[pl.ds(pl.multiple_of((1 - bit) * half, 16), half)] = got[rows]


def sum_mixer(place, own, got, rest, between, after):
    size = own.shape[0] // 2
    rows = lambda n: ((n, 128), BF)
    (sa, ka), (sb, kb) = split(place, (0, 1), [(own[:size], got[:size]), (own[size:], got[size:])], after)
    ra, rb = swap_bit(sa, 0), swap_bit(sb, 1)
    after = between(0, ka)
    sa, sb, keep = call(second_kernel, "second_split", [rows(size // 4)] * 2 + [rows(size // 2)], [], 8, 1, place, ka, ra, kb, rb, after=after)
    ra, rb = swap_bit(sa, 1), swap_bit(sb, 0)
    after = between(1, keep)
    send, keep = call(third_kernel, "third_split", [rows(size // 4)] * 2, [], 8, 1, place, keep, ra, rb, after=after)
    got = swap_bit(send, 2)
    out = total(keep, got, between(2, keep))
    for bit in rest:
        out = total(out, swap_bit(out, bit), between(3, out))
    got = swap_bit(out, 2)
    a, b = call(fifth_kernel, "first_merge", [rows(size // 4)] * 2, [], 8, 1, place, out, got, after=between(4, out))
    ra, rb = swap_bit(a, 1), swap_bit(b, 0)
    a, b = merge(place, (1, 0), [(a, ra), (b, rb)], between(5, a))
    ra, rb = swap_bit(a, 0), swap_bit(b, 1)
    between(6, a)
    return a, ra, b, rb


def rows_at(mine, got, bit, start, count):
    half = mine.shape[0]
    out, at = [], start
    while at < start + count:
        n = min(count - (at - start), half - at % half)
        local, lower = at % half, at < half
        a, b = mine[local : local + n], got[local : local + n]
        first = bit == 0 if lower else bit == 1
        out.append(jnp.where(first, a, b))
        at += n
    return out[0] if len(out) == 1 else jnp.concatenate(out, axis=0)


def unpack_glu_kernel(place, a0, b0, a1, b1, down_one, gate_two, up_two, gate_one, up_one, down_two):
    for h, (mine, got) in enumerate(((a0, b0), (a1, b1))):
        take = lambda start, count: rows_at(mine, got, place[h], start, count).astype(F32)
        wide = lambda start, rows: jnp.concatenate([take(start + c * rows, rows) for c in range(6)], axis=1)
        down_one[h] = wide(0, INNER)
        gate_two[h] = wide(6 * INNER, INNER).reshape(48, 4, D)
        up_two[h] = wide(12 * INNER, INNER).reshape(48, 4, D)
        ones = wide(GLU_ONE, 96)
        for k in range(4):
            gate_one[k, h] = ones[:48, k * INNER : (k + 1) * INNER]
            up_one[k, h] = ones[48:, k * INNER : (k + 1) * INNER]
        rest = take(GLU_TWO + INNER, 96)
        right = jnp.concatenate([rest, pltpu.roll(rest, 64, 1)], axis=0)
        two = jnp.concatenate([take(GLU_TWO, INNER), right[:, :64]], axis=1)
        for m in range(4):
            down_two[m, :, h, :] = two[48 * m : 48 * m + 48]


def unpack_glu(place, parts, after=()):
    outs = [
        ((2, INNER, D), F32), ((2, 48, 4, D), F32), ((2, 48, 4, D), F32), ((4, 2, 48, INNER), F32), ((4, 2, 48, INNER), F32),
        ((4, 48, 2, INNER), F32),
    ]
    return call(unpack_glu_kernel, "unpack_feed_forward", outs, [], 24, 4, place, *parts, after=after)


def unpack_mixer_kernel(place, a0, b0, a1, b1, mixout_one, mixout_two, mixin_one, mixin_two, vecs, taps, pos, pos_out):
    size = MIX_ROWS // 2

    def take(start, count):
        out, at = [], start
        while at < start + count:
            g = at // size
            n = min(start + count, (g + 1) * size) - at
            mine, got = ((a0, b0), (a1, b1))[g]
            out.append(rows_at(mine, got, place[g], at - g * size, n).astype(F32))
            at += n
        return out[0] if len(out) == 1 else jnp.concatenate(out, axis=0)

    wide = lambda start, rows, n: jnp.concatenate([take(start + c * rows, rows) for c in range(n)], axis=1)
    for base, one, two, e in ((0, mixout_one, mixout_two, INNER), (MIX_IN, mixin_one, mixin_two, 576)):
        ones = wide(base, INNER, 3)
        twos = wide(base + 3 * INNER, INNER, 2 * e // 128)
        for i in range(2):
            one[i] = ones[:, i * INNER : (i + 1) * INNER]
            two[i] = twos[:, i * e : (i + 1) * e].reshape(48, 4, e)
    small = take(MIX_SMALL, 48)
    for i in range(5):
        vecs[i : i + 1] = jnp.concatenate([small[3 * i + c : 3 * i + c + 1] for c in range(3)], axis=1)
    for i in range(3):
        taps[i : i + 1] = jnp.concatenate([small[15 + 9 * i + c : 16 + 9 * i + c] for c in range(9)], axis=1)
    pos[...] = take(MIX_POS, 16)[:8]
    pos_out[...] = wide(MIX_OUT, 128, 3)


def unpack_mixer(place, parts):
    outs = [
        ((2, INNER, INNER), F32), ((2, 48, 4, INNER), F32), ((2, INNER, INNER), F32), ((2, 48, 4, 576), F32), ((5, 384), F32),
        ((3, 1152), F32), ((8, 128), F32), ((128, 384), F32),
    ]
    return call(unpack_mixer_kernel, "unpack_mixer", outs, [], 24, 3, place, *parts)


def local(
    tokens, short_lengths, long_lengths, cotangent, norm1_gain, norm1_bias, mixin_one, mixin_two, conv_taps, skip_gain,
    pos_in, pos_bias, pos_out, mixout_one, mixout_two, norm2_gain, norm2_bias, gate_one, gate_two, up_one, up_two,
    down_one, down_two,
):
    mp_index = lax.axis_index("mp")
    dp_index = lax.axis_index("dp")
    total_bits = (lax.axis_size("dp") - 1).bit_length()
    mp = mp_index.astype(jnp.int32).reshape(1)
    place = ((dp_index >> jnp.arange(3)) & 1).astype(jnp.int32)
    const = tables()
    rows_first = lambda w: w.transpose(0, 2, 3, 1).reshape(w.shape[0], -1, w.shape[1])
    glu_own = (rows_first(gate_one), gate_two, rows_first(up_one), up_two, rows_first(down_one), down_two)
    glu_other = tuple(swap_pair(w) for w in glu_own)

    vecs, taps = small_params(norm1_gain, norm1_bias, norm2_gain, norm2_bias, skip_gain, conv_taps)
    mixed, sect_in = mixin_forward(
        short_lengths, long_lengths, tokens, vecs, rows_first(mixin_one), mixin_two, (mp, place)
    )
    sin_h, cos_h, kr, ks = make_filter(const, pos_in, pos_bias.reshape(1, -1), pos_out, (sect_in,))
    gated, spread, xr, xs, parts, mixed_saved = conv_forward(const, mixed, taps, vecs, kr, ks)
    middle, out, normed_two, sect_out, w1p_out, w2p_out = mixout_forward(
        tokens, gated, vecs, rows_first(mixout_one), mixout_two, glu_other
    )

    def block(h, weights, out, grad, after=()):
        return glu_block(h, normed_two, cotangent, out, grad, weights, after)

    out, grad, other = block(0, glu_other, out, None)
    out, grad, own = block(0, glu_own, out, grad)
    rest = tuple(range(2, total_bits))
    a = Steps(place, own, swap_pair(other), (0, 1), rest)
    token = a.step()
    out, grad, other = block(1, glu_other, out, grad, (token,))
    token = a.step((other,))
    out, grad, own = block(1, glu_own, out, grad, (token,))
    b = Steps(place, own, swap_pair(other), (1, 0), rest)
    both = lambda last: tuple(v.step(last) for v in (a, b) if not v.done)
    result, grad_middle, grad_gated, mixout_grads, norm2_small = middle_back(
        mp, middle, out, grad, cotangent, gated, sect_out, vecs, w1p_out, w2p_out, (a.step((own,)), b.step())
    )
    saved = (mixed_saved, parts, xr, xs, spread)
    last = (norm2_small,)
    grads, smalls, outs, hidden = [], [], [], []
    for c in range(D // CHUNK):
        g, small, pos_o, hid = conv_back(
            c, const, short_lengths, long_lengths, saved, taps, vecs, kr, ks, grad_gated, sin_h, cos_h, pos_out,
            hidden if c == D // CHUNK - 1 else [], both(last),
        )
        last = (small,)
        grads.append(g)
        smalls.append(small)
        outs.append(pos_o)
        hidden.append(hid)
    tokens_grad, norm1_small, normed, grad_sect = mixin_back(
        tokens, grads, grad_middle, vecs, rows_first(mixin_one), mixin_two, both(last)
    )
    own, other = mixin_grads(
        mp, grads, sect_in, normed, grad_sect, (mixout_grads, norm1_small, norm2_small, *smalls, *outs, hidden[-1]),
        both((norm1_small,)),
    )
    glu = []

    def between(level, token):
        if level >= 2 and not (a.done and b.done):
            return both((token,))
        if level == 6:
            glu.extend(unpack_glu(place, [*a.halves, *b.halves], (token,)))
        return ()

    parts = sum_mixer(place, own, swap_pair(other), tuple(range(3, total_bits)), between, ())
    mix = unpack_mixer(place, parts)

    natural = lambda v: v.transpose(0, 3, 1, 2)
    down_one_g, gate_two_g, up_two_g, gate_one_g, up_one_g, down_two_g = glu
    mixout_one_g, mixout_two_g, mixin_one_g, mixin_two_g, vecs_g, taps_g, pos_g, pos_out_g = mix
    pos_own = lax.dynamic_slice_in_dim(pos_g, mp_index * 64, 64, 1)
    one = lambda v: natural(v.reshape(2, 4, 48, INNER))
    return (
        result, tokens_grad, vecs_g[0], vecs_g[1], one(mixin_one_g), mixin_two_g, taps_g, vecs_g[4], pos_own[:5], pos_own[7],
        pos_out_g, one(mixout_one_g), mixout_two_g, vecs_g[2], vecs_g[3], natural(gate_one_g), gate_two_g, natural(up_one_g),
        up_two_g, natural(down_one_g.reshape(2, 4, 48, D)), down_two_g,
    )


def solution(mesh):
    return jax.shard_map(
        local,
        mesh=mesh,
        in_specs=(
            P(("dp", "mp"), None),
            P(("dp", "mp")),
            P(("dp", "mp")),
            P(("dp", "mp"), None),
            *[P()] * 13,
            P(None, None, "mp", None),
            P("mp", None, None, None),
            P(None, None, "mp", None),
            P("mp", None, None, None),
            P("mp", None, None, None),
            P(None, None, "mp", None),
        ),
        out_specs=(
            P(("dp", "mp"), None),
            P(("dp", "mp"), None),
            P("mp"),
            P("mp"),
            P("mp", None, None, None),
            P("mp", None, None, None),
            P(None, "mp"),
            P("mp"),
            P(None, "mp"),
            P("mp"),
            P(None, "mp"),
            P("mp", None, None, None),
            P("mp", None, None, None),
            P("mp"),
            P("mp"),
            P(None, None, "mp", None),
            P("mp", None, None, None),
            P(None, None, "mp", None),
            P("mp", None, None, None),
            P("mp", None, None, None),
            P(None, None, "mp", None),
        ),
        check_vma=False,
    )
```

```python
import functools
import math

import jax
import jax.numpy as jnp
import numpy as np
from jax import lax
from jax.experimental import pallas as pl
from jax.experimental.pallas import tpu as pltpu
from jax.sharding import PartitionSpec as P

BF, F32 = jnp.bfloat16, jnp.float32
SHORT, LONG = 128, 1024
ROWS = SHORT + LONG
D = 768
INNER = 192
EPS = 1e-05
SLOWEST = math.log(100.0) / 1.5
FASTEST = math.log(100.0) / 0.3
TILE = 384
CHUNK = 256
MIB = 1024 * 1024
GLU_ONE, GLU_TWO, GLU_ROWS = 18 * INNER, 21 * INNER, 4352
MIX_IN, MIX_SMALL, MIX_POS, MIX_OUT, MIX_ROWS = 6 * INNER, 18 * INNER, 18 * INNER + 48, 18 * INNER + 64, 4096


def nn(a, b):
    return jnp.dot(a, b, preferred_element_type=F32)


def tn(a, b):
    return lax.dot_general(a, b, (((0,), (0,)), ((), ())), preferred_element_type=F32)


def nt(a, b):
    return lax.dot_general(a, b, (((1,), (1,)), ((), ())), preferred_element_type=F32)


def iota(shape, dim):
    return lax.broadcasted_iota(jnp.int32, shape, dim)


def block_of(index, width, count):
    out = jnp.zeros_like(index)
    for i in range(1, count):
        out = out + (index >= width * i).astype(jnp.int32)
    return out


def ones_where(cond):
    return jnp.where(cond, 1.0, 0.0).astype(BF)


def window_starts(e):
    return [2 * e * (m // 2) + (e // 128 * 128) * (m % 2) for m in range(4)]


def select_rows():
    row, col = iota((256, INNER), 0), iota((256, INNER), 1)
    a, q = row >> 6, row & 63
    return ones_where((col == q * 4 + a) & (q < 48))


def pad_sections(pieces):
    zeros = jnp.zeros((16, pieces[0].shape[1]), pieces[0].dtype)
    return jnp.concatenate([v for p in pieces for v in (p, zeros)], axis=0)


def pad_window(v, k):
    zeros = jnp.zeros((v.shape[0], 64), v.dtype)
    return jnp.concatenate([zeros, v] if k % 2 else [v, zeros], axis=1)


def mixer_weights(w1, w2, w1p, w2p, e):
    for i in range(4):
        w1p[i] = pad_window(pad_sections([w1[i, 48 * m : 48 * m + 48] for m in range(4)]), i)
        w2p[i] = pad_window(nn(select_rows(), w2[i].reshape(INNER, e)).astype(BF), i)


def exchange(blocks):
    blocks = [b.astype(BF) for b in blocks]
    return [jnp.concatenate([b[:, 64 * m : 64 * m + 64] for b in blocks], axis=1) for m in range(4)]


def join(windows):
    out = []
    for a, b in (windows[:2], windows[2:]):
        n = a.shape[1] - 128
        out += [a[:, :n], a[:, n:] + b[:, :128], b[:, 128:]]
    return jnp.concatenate(out, axis=1)


def sections(x, w1p):
    return exchange([nt(x[:, s : s + 256], w1p[k]) for k, s in enumerate(window_starts(INNER))])


def pair_columns(a, b):
    n = a.shape[1] - 128
    lane = iota((a.shape[0], 128), 1)
    return jnp.concatenate([a[:, :n], jnp.where(lane < 64, a[:, n:], b[:, :128]), b[:, 128:]], axis=1)


def block_grads(width, left, right):
    full = tn(left, right)
    if width == 48:
        return jnp.concatenate([full[64 * m : 64 * m + 48] for m in range(4)], axis=0)
    return tn(select_rows(), full.astype(BF))


def norm_parts(x):
    centred = x - jnp.mean(x, axis=-1, keepdims=True)
    rstd = lax.rsqrt(jnp.mean(centred * centred, axis=-1, keepdims=True) + EPS)
    return centred * rstd, rstd


def norm_back(grad, xhat, rstd, gain):
    scaled = grad * gain
    first = jnp.mean(scaled, axis=-1, keepdims=True)
    second = jnp.mean(scaled * xhat, axis=-1, keepdims=True)
    return rstd * (scaled - first - xhat * second)


LIMITS = {"mixer_input": 20, "filters": 14, "conv_forward": 22, "mixer_output": 12, "feed_forward": 18, "feed_forward_sections": 12, "middle_back": 22, "conv_back": 21, "mixer_input_back": 18, "mixer_input_grads": 14, "result": 10, "tokens_grad": 10}
WHOLE, PINNED, FAR = "whole", "pinned", "far"


def by_rows(*shape):
    dim = len(shape) - 2
    block = shape[:dim] + (TILE,) + shape[dim + 1 :]
    return pl.BlockSpec(block, lambda i: (0,) * dim + (i, 0))


def by_columns(*shape):
    lead = len(shape) - 1
    return pl.BlockSpec(shape[:-1] + (CHUNK,), lambda i: (0,) * lead + (i,))


def call(kernel, name, outs, scratch, limit, us, *args, grid=None, aliases=None, after=()):
    inner = kernel
    count, skip = len(args), len(after)
    if skip:
        kernel = lambda *refs: inner(*refs[:count], *refs[count + skip :])
    in_specs, operands, out_specs, out_shape = [], [], [], []
    for arg in args:
        arg, mode = arg if isinstance(arg, tuple) else (arg, WHOLE)
        if arg.dtype == jnp.int32:
            in_specs.append(pl.BlockSpec(memory_space=pltpu.SMEM))
        elif mode == FAR:
            arg = pltpu.with_memory_space_constraint(arg, pltpu.HBM)
            in_specs.append(pl.BlockSpec(memory_space=pl.ANY))
        elif isinstance(mode, pl.BlockSpec):
            arg = pltpu.with_memory_space_constraint(arg, pltpu.HBM)
            in_specs.append(mode)
        else:
            if mode == PINNED:
                arg = pltpu.with_memory_space_constraint(arg, pltpu.VMEM)
            in_specs.append(pl.BlockSpec(memory_space=pltpu.VMEM))
        operands.append(arg)
    for arg in after:
        in_specs.append(pl.BlockSpec(memory_space=pl.ANY))
        operands.append(arg)
    for shape, dtype, *mode in outs:
        mode = mode[0] if mode else WHOLE
        if mode == FAR or isinstance(mode, pl.BlockSpec):
            out_specs.append(pl.BlockSpec(memory_space=pl.ANY) if mode == FAR else mode)
            out_shape.append(pltpu.HBM(shape, dtype))
        else:
            out_specs.append(pl.BlockSpec(memory_space=pltpu.VMEM))
            out_shape.append(pltpu.VMEM(shape, dtype) if mode == PINNED else jax.ShapeDtypeStruct(shape, dtype))
    return pl.pallas_call(
        kernel,
        out_shape=out_shape,
        in_specs=in_specs,
        out_specs=out_specs,
        grid=(grid,) if grid else (),
        scratch_shapes=[pltpu.VMEM(*v) if isinstance(v, tuple) else v for v in scratch],
        input_output_aliases=aliases or {},
        cost_estimate=pl.CostEstimate(flops=int(us * 1.0e9), bytes_accessed=0, transcendentals=0),
        compiler_params=pltpu.CompilerParams(vmem_limit_bytes=LIMITS.get(name, 6) * MIB),
        name=name,
    )(*operands)


TILES = [slice(start, start + TILE) for start in range(0, ROWS, TILE)]
CHUNKS = [slice(start, start + CHUNK) for start in range(0, D, CHUNK)]
ROW_CUTS = [(rows,) for rows in TILES]
COLUMN_CUTS = [(Ellipsis, cols) for cols in CHUNKS]
SEMS = pltpu.SemaphoreType.DMA((3,))


def copies(source, target, sems, cuts):
    return [pltpu.make_async_copy(source.at[cut], target.at[cut], sems.at[i]) for i, cut in enumerate(cuts)]


def start_all(moves):
    for move in moves:
        move.start()
    return moves


def wait_all(*groups):
    for moves in groups:
        for move in moves:
            move.wait()


def first_step(body):
    pl.when(pl.program_id(0) == 0)(body)


def last_step(body):
    pl.when(pl.program_id(0) == pl.num_programs(0) - 1)(body)


def grid_part(size):
    start = pl.multiple_of(pl.program_id(0) * size, size)
    return pl.ds(start, size), start


def tables():
    def phases(n, f, t):
        whole = ((2 * f[:, None] + 1) * (2 * t[None, :] + 1)) % (8 * n)
        angle = whole.astype(np.float64) * (math.pi / (4 * n))
        return np.cos(angle), np.sin(angle)

    half = LONG // 2
    low = np.arange(half, dtype=np.int64)
    short = np.concatenate(phases(SHORT, np.arange(SHORT), np.arange(SHORT)), axis=1)
    parts = [np.concatenate(phases(LONG, low, 2 * low + odd), axis=0) for odd in (0, 1)]
    fraction = np.concatenate([np.arange(SHORT) / SHORT, np.arange(LONG) / LONG])
    order = np.concatenate([low, LONG - 1 - low])
    shift = np.concatenate(
        [(2 * f + 1) * (math.pi / (4 * n)) for f, n in ((np.arange(SHORT), SHORT), (order, LONG))]
    )
    aux = np.zeros((ROWS, 8), np.float32)
    aux[:, 0] = fraction
    for i, band in enumerate((1, 2)):
        aux[:, 1 + i] = np.cos(2.0 * math.pi * band * fraction)
        aux[:, 3 + i] = np.sin(2.0 * math.pi * band * fraction)
    aux[:, 5] = np.cos(shift)
    aux[:, 6] = np.sin(shift)
    aux[:, 7] = 1.0
    rates = SLOWEST + (FASTEST - SLOWEST) * np.arange(D) / (D - 1)
    low_type = lambda t: jnp.asarray(t.astype(np.float32), BF)
    return (
        (low_type(short), *[low_type(p) for p in parts], *[low_type(np.ascontiguousarray(p.T)) for p in parts]),
        jnp.asarray(aux),
        low_type(np.ascontiguousarray(aux.T)),
        jnp.asarray(rates[None].astype(np.float32)),
    )


def scale_rows(shape):
    return jnp.where(iota(shape, 0) < SHORT, 1.0 / SHORT, 1.0 / LONG)


def parity(odd):
    return pl.ds(odd, LONG // 2, stride=2)


LANES = [slice(i, i + 128) for i in range(0, CHUNK, 128)]


def transform(v, tabs, room):
    ts, fe, fo, _, _ = tabs
    head = v[:SHORT].astype(BF)
    for i, lanes in enumerate(LANES):
        room[i] = v[SHORT:, lanes]
    even, odd = [jnp.concatenate([room[i, parity(p)] for i in range(2)], axis=1).astype(BF) for p in (0, 1)]
    e, o = nn(fe[...], even), nn(fo[...], odd)
    h = LONG // 2
    real = jnp.concatenate([nn(ts[:, :SHORT], head), e[:h] + o[:h], e[h:] - o[h:]], axis=0)
    imag = jnp.concatenate([nn(ts[:, SHORT:], head), e[h:] + o[h:], e[:h] - o[:h]], axis=0)
    return real, imag


def restore(real, imag, tabs, room):
    ts, _, _, ie, io = tabs
    h = SHORT + LONG // 2
    head = nn(ts[...], jnp.concatenate([real[:SHORT], imag[:SHORT]], axis=0).astype(BF))
    r0, r1, i0, i1 = real[SHORT:h], real[h:], imag[SHORT:h], imag[h:]
    even = nn(ie[...], jnp.concatenate([r0 + i1, i0 + r1], axis=0).astype(BF))
    odd = nn(io[...], jnp.concatenate([r0 - i1, i0 - r1], axis=0).astype(BF))
    for i, lanes in enumerate(LANES):
        room[i, parity(0)] = even[:, lanes]
        room[i, parity(1)] = odd[:, lanes]
    return jnp.concatenate([head, jnp.concatenate([room[0], room[1]], axis=1)], axis=0)


ROOM = ((2, LONG, 128), F32)


def chunks(body):
    for c in range(D // CHUNK):
        body(slice(c * CHUNK, (c + 1) * CHUNK))


def tiles(body):
    for start in range(0, ROWS, TILE):
        body(slice(start, start + TILE), start)


def small_kernel(*refs):
    far, (vecs_o, taps_o), near, sems = refs[:6], refs[6:8], refs[8:14], refs[14]
    copies = [pltpu.make_async_copy(f, n, sems.at[i]) for i, (f, n) in enumerate(zip(far, near))]
    for copy in copies:
        copy.start()
    for copy in copies:
        copy.wait()
    vecs_o[...] = jnp.concatenate([v[...].reshape(1, D) for v in near[:5]] + [jnp.zeros((3, D), F32)], axis=0)
    taps = [near[5][i : i + 1, j * D : (j + 1) * D] for j in range(3) for i in range(3)]
    taps_o[...] = jnp.concatenate(taps + [jnp.zeros((7, D), F32)], axis=0)


def small_params(*args):
    return call(
        small_kernel, "small_parameters", [((8, D), F32), ((16, D), F32)],
        [((D,), F32)] * 5 + [((3, 3 * D), F32), pltpu.SemaphoreType.DMA((6,))], 8, 1, *[(v, FAR) for v in args],
    )


def sin_cos(x):
    turns = jnp.floor(x * (2.0 / math.pi) + 0.5)
    r = ((x - turns * 1.5703125) - turns * 4.837512969970703125e-4) - turns * 7.54978995489188216e-8
    z = r * r
    s = r + r * z * (-1.6666654611e-1 + z * (8.3321608736e-3 - 1.9515295891e-4 * z))
    c = 1.0 - 0.5 * z + z * z * (4.166664568298827e-2 + z * (-1.388731625493765e-3 + 2.443315711809948e-5 * z))
    quarter = turns.astype(jnp.int32) & 3
    odd = (quarter & 1) == 1
    sine = jnp.where(odd, c, s)
    cosine = jnp.where(odd, s, c)
    return jnp.where(quarter >= 2, -sine, sine), jnp.where((quarter == 1) | (quarter == 2), -cosine, cosine)


def filter_kernel(aux, pos_in, pos_bias, pos_out, rates, *refs):
    *tabs, sin_o, cos_o, kr_o, ks_o, room = refs
    pre = jnp.broadcast_to(pos_bias[...], (ROWS, 128))
    for i in range(5):
        pre = pre + aux[:, i : i + 1] * pos_in[i : i + 1, :]
    sin_o[...], cos_o[...] = sin_cos(pre)

    for c, cols in enumerate(CHUNKS):
        hidden = sin_o[...]
        high = hidden.astype(BF)
        low = (hidden - high.astype(F32)).astype(BF)
        w = pos_out[:, cols]
        w_high = w.astype(BF)
        w_low = (w - w_high.astype(F32)).astype(BF)
        shaped = nn(high, w_high) + nn(high, w_low) + nn(low, w_high)
        kern = shaped * jnp.exp(-aux[:, 0:1] * rates[:, cols])
        a, b = transform(kern, tabs, room.at[c])
        cos_h, sin_h = aux[:, 5:6], aux[:, 6:7]
        scale = scale_rows((ROWS, 1))
        kr_o[:, cols] = ((cos_h * a + sin_h * b) * scale).astype(BF)
        ks_o[:, cols] = ((cos_h * b - sin_h * a) * scale).astype(BF)


def make_filter(const, pos_in, pos_bias, pos_out, after):
    tabs, aux, _, rates = const
    return call(
        filter_kernel, "filters", [((ROWS, 128), F32, PINNED)] * 2 + [((ROWS, D), BF, PINNED)] * 2, [((3, *ROOM[0]), F32)], 10, 6,
        aux, pos_in, pos_bias, pos_out, rates, *tabs, after=after,
    )


def row_valid(short_len, long_len, start, rows):
    row = iota((rows, 1), 0) + start
    limit = jnp.where(row < SHORT, short_len[0], long_len[0] + SHORT)
    return row < limit


def mixin_kernel(
    short_len, long_len, tokens_h, vecs, w1, w2, mixed_o, sect_h, w1p, w2p, tokens, sect_s, in_sems, out_sems
):
    loads = start_all(copies(tokens_h, tokens, in_sems, ROW_CUTS))
    stores = copies(sect_s, sect_h, out_sems, ROW_CUTS)
    mixer_weights(w1, w2, w1p, w2p, 576)
    for i, rows in enumerate(TILES):
        loads[i].wait()
        xhat, _ = norm_parts(tokens[rows].astype(F32))
        normed = (xhat * vecs[0:1] + vecs[1:2]).astype(BF)
        sect = sections(normed, w1p)
        for m in range(4):
            sect_s[rows, m * 256 : (m + 1) * 256] = sect[m]
        stores[i].start()
        valid = row_valid(short_len, long_len, rows.start, TILE)
        full = jnp.where(valid, join([nn(sect[m], w2p[m]) for m in range(4)]), 0.0).astype(BF)
        for j in range(3):
            mixed_o[j, rows] = full[:, j * D : (j + 1) * D]
    wait_all(stores)


def mixin_forward(short_len, long_len, tokens, vecs, w1, w2, after):
    return call(
        mixin_kernel, "mixer_input", [((3, ROWS, D), BF, PINNED), ((ROWS, 1024), BF, FAR)],
        [((4, 256, 256), BF), ((4, 256, 640), BF), ((ROWS, D), BF), ((ROWS, 1024), BF), SEMS, SEMS], 22, 6,
        short_len, long_len, (tokens, FAR), vecs, w1, w2, after=after,
    )


def edges(shape):
    row = iota(shape, 0)
    first = (row == 0) | (row == SHORT)
    last = (row == SHORT - 1) | (row == ROWS - 1)
    return first, last


def before(v, first):
    return jnp.where(first, 0.0, pltpu.roll(v, 1, 0))


def after(v, last):
    return jnp.where(last, 0.0, pltpu.roll(v, ROWS - 1, 0))


def tap_rows(taps, cols, j):
    return [taps[3 * j + i : 3 * j + i + 1, cols] for i in range(3)]


def conv_forward_kernel(mixed, taps, vecs, kr, ks, *refs):
    tabs, gated_o, far, near, (mixed_h, room), sems = refs[:5], refs[5], refs[6:10], refs[11:15], (refs[10], refs[15]), refs[16]
    save = pltpu.make_async_copy(mixed, mixed_h, sems.at[4, 0])
    save.start()
    stores = [copies(v, f, sems.at[i], COLUMN_CUTS) for i, (v, f) in enumerate(zip(near, far))]
    spread_s, xr_s, xs_s, parts_s = near
    first, last = edges((ROWS, CHUNK))
    for c, cols in enumerate(CHUNKS):
        parts = []
        for j in range(3):
            m = mixed[j, :, cols].astype(F32)
            t0, t1, t2 = tap_rows(taps, cols, j)
            parts.append(t0 * before(m, first) + t1 * m + t2 * after(m, last))
            parts_s[j, :, cols] = parts[j].astype(BF)
        stores[3][c].start()
        product = parts[0] * parts[2]
        real, imag = transform(product, tabs, room.at[c])
        xr_s[:, cols] = real.astype(BF)
        xs_s[:, cols] = imag.astype(BF)
        stores[1][c].start()
        stores[2][c].start()
        a, b = kr[:, cols].astype(F32), ks[:, cols].astype(F32)
        spread = restore(real * a - imag * b, real * b + imag * a, tabs, room.at[c])
        spread = spread + vecs[4:5, cols] * product
        spread_s[:, cols] = spread.astype(BF)
        gated_o[:, cols] = (spread * parts[1]).astype(BF)
        stores[0][c].start()
    wait_all([save], *stores)


def conv_forward(const, mixed, taps, vecs, kr, ks):
    one, three = ((ROWS, D), BF), ((3, ROWS, D), BF)
    return call(
        conv_forward_kernel, "conv_forward",
        [(*one, PINNED), (*one, FAR), (*one, FAR), (*one, FAR), (*three, FAR), (*three, FAR)],
        [one, one, one, three, ((3, *ROOM[0]), F32), pltpu.SemaphoreType.DMA((5, 3))], 22, 9,
        (mixed, PINNED), taps, vecs, (kr, PINNED), (ks, PINNED), *const[0],
    )


def conv_back_kernel(
    c, short_len, long_len, mixed_h, parts_h, taps, vecs, kr, ks, xr_h, xs_h, spread_h, grad_gated, sin_h, cos_h, aux, features, pos_out,
    rates, *rest
):
    tabs = rest[:5]
    *earlier, grad_o, small_o, pos_out_o, hidden_o, mixed, parts, xr, xs, spread, sems, room = rest[5:]
    cols = slice(c * CHUNK, (c + 1) * CHUNK)
    copies = [
        pltpu.make_async_copy(far.at[..., cols], near, sems.at[i])
        for i, (far, near) in enumerate(((parts_h, parts), (xr_h, xr), (xs_h, xs), (spread_h, spread), (mixed_h, mixed)))
    ]
    for copy in copies:
        copy.start()
    first, last = edges((ROWS, CHUNK))
    gg = grad_gated[:, cols].astype(F32)
    copies[0].wait()
    grad_spread = gg * parts[1].astype(F32)
    real, imag = transform(grad_spread, tabs, room)
    a, b = kr[:, cols].astype(F32), ks[:, cols].astype(F32)
    grad_product = restore(a * real + b * imag, a * imag - b * real, tabs, room)
    grad_product = grad_product + vecs[4:5, cols] * grad_spread
    copies[1].wait()
    copies[2].wait()
    x_real, x_imag = xr[...].astype(F32), xs[...].astype(F32)
    z_real = x_real * real + x_imag * imag
    z_imag = x_real * imag - x_imag * real
    cos_p, sin_p = aux[:, 5:6], aux[:, 6:7]
    grad_kernel = restore(cos_p * z_real - sin_p * z_imag, cos_p * z_imag + sin_p * z_real, tabs, room)
    shaped_grad = (grad_kernel * (scale_rows((ROWS, 1)) * jnp.exp(-aux[:, 0:1] * rates[:, cols]))).astype(BF)
    pos_out_o[...] = tn(sin_h[...].astype(BF), shaped_grad)
    hidden = nt(shaped_grad, pos_out[:, cols].astype(BF))
    copies[3].wait()
    copies[4].wait()
    front = parts[0].astype(F32)
    value = parts[2].astype(F32)
    grads = (grad_product * value, gg * spread[...].astype(F32), grad_product * front)
    valid = row_valid(short_len, long_len, 0, ROWS)
    small = []
    for j in range(3):
        m = mixed[j].astype(F32)
        g = grads[j]
        up, down = after(g, last), before(g, first)
        t0, t1, t2 = tap_rows(taps, cols, j)
        small += [jnp.sum(v * m, axis=0, keepdims=True) for v in (up, g, down)]
        grad_o[j] = jnp.where(valid, t0 * up + t1 * g + t2 * down, 0.0).astype(BF)
    small.append(jnp.sum(grad_spread * front * value, axis=0, keepdims=True))
    small.append(jnp.zeros((6, CHUNK), F32))
    small_o[...] = jnp.concatenate(small, axis=0)
    if not earlier:
        hidden_o[...] = hidden
    else:
        pre = (hidden + earlier[0][...] + earlier[1][...]) * cos_h[...]
        hidden_o[...] = nn(features[...], pre.astype(BF))


def conv_back(c, const, short_len, long_len, saved, taps, vecs, kr, ks, grad_gated, sin_h, cos_h, pos_out, earlier, after):
    tabs, aux, features, rates = const
    mixed, parts, xr, xs, spread = saved
    final = len(earlier) > 0
    one = ((ROWS, CHUNK), BF)
    three = ((3, ROWS, CHUNK), BF)
    return call(
        functools.partial(conv_back_kernel, c), "conv_back",
        [(*three, PINNED), ((16, CHUNK), F32), ((128, CHUNK), F32)] + ([((8, 128), F32)] if final else [((ROWS, 128), F32, PINNED)]),
        [three, three, one, one, one, pltpu.SemaphoreType.DMA((5,)), ROOM], 30, 8,
        short_len, long_len, (mixed, FAR), (parts, FAR), taps, vecs, (kr, PINNED), (ks, PINNED), (xr, FAR), (xs, FAR),
        (spread, FAR), (grad_gated, PINNED), (sin_h, PINNED), (cos_h, PINNED), aux, features, pos_out, rates, *tabs,
        *[(v, PINNED) for v in earlier], after=after,
    )


def mixout_kernel(
    tokens_h, gated, vecs, w1, w2, middle_h, normed_o, sect_o, w1p, w2p, tokens, middle_s, in_sems, out_sems
):
    loads = start_all(copies(tokens_h, tokens, in_sems, ROW_CUTS))
    stores = copies(middle_s, middle_h, out_sems, ROW_CUTS)
    mixer_weights(w1, w2, w1p, w2p, INNER)
    for i, rows in enumerate(TILES):
        sect = sections(gated[rows], w1p)
        for m in range(4):
            sect_o[rows, m * 256 : (m + 1) * 256] = sect[m]
        loads[i].wait()
        middle = tokens[rows].astype(F32) + join([nn(sect[m], w2p[m]) for m in range(4)])
        middle_s[rows] = middle
        stores[i].start()
        xhat, _ = norm_parts(middle)
        normed_o[rows] = (xhat * vecs[2:3] + vecs[3:4]).astype(BF)
    wait_all(stores)


def mixout_forward(tokens, gated, vecs, w1, w2, after):
    return call(
        mixout_kernel, "mixer_output",
        [
            ((ROWS, D), F32, FAR), ((ROWS, D), BF, PINNED), ((ROWS, 1024), BF, PINNED), ((4, 256, 256), BF, PINNED),
            ((4, 256, 256), BF, PINNED),
        ],
        [((ROWS, D), BF), ((ROWS, D), F32), SEMS, SEMS], 18, 5, (tokens, FAR), (gated, PINNED), vecs, w1, w2, after=after,
    )


def select_pair():
    row, col = iota((256, INNER), 0), iota((256, INNER), 1)
    block, q = row >> 6, row & 63
    return ones_where((col == (block & 1) * 96 + q * 2 + (block >> 1)) & (q < 48))


def sections_kernel(normed, cot, g1, u1, d2, own_g1, own_u1, own_d2, *refs):
    gate_o, up_o, grad_o, (g1p, u1p, d2p) = refs[:4], refs[4:8], refs[8:12], refs[12:]

    for i in range(4):
        for out, pair in ((g1p, (g1, own_g1)), (u1p, (u1, own_u1))):
            out[i] = pad_window(pad_sections([w[i, 48 * h : 48 * h + 48] for h in range(2) for w in pair]), i)
        both = jnp.concatenate([w[i].reshape(96, INNER) for w in (d2, own_d2)], axis=0)
        d2p[i] = pad_window(nn(select_pair(), both).astype(BF), i)
    for rows in TILES:
        for x, weights, outs in ((normed, g1p, gate_o), (normed, u1p, up_o), (cot, d2p, grad_o)):
            for out, v in zip(outs, sections(x[rows], weights)):
                out[rows] = v


def glu_sections(normed, cot, own, other):
    return call(
        sections_kernel, "feed_forward_sections", [((ROWS, 256), BF, PINNED)] * 12 + [((4, 256, 256), BF, PINNED)] * 3, [], 8, 4,
        (normed, PINNED), cot, other[0], other[2], other[5], own[0], own[2], own[5],
    )


def glu_kernel(
    h, normed, cot, gate_sect, up_sect, grad_sect, g2, u2, d1, sect_o, gate_grad_o, up_grad_o, grads_o,
    g2p, u2p, d1p, hidden_s, gate_s, up_s
):
    g2p[...] = nn(select_rows(), g2[h].reshape(INNER, D)).astype(BF)
    u2p[...] = nn(select_rows(), u2[h].reshape(INNER, D)).astype(BF)
    d1p[...] = pad_sections([d1[h, 48 * m : 48 * m + 48] for m in range(4)])

    def body(rows, start):
        gate = nn(gate_sect[rows], g2p[...])
        up = nn(up_sect[rows], u2p[...])
        sig = jax.nn.sigmoid(gate)
        act = gate * sig
        hidden = (act * up).astype(BF)
        sect_o[rows] = nt(hidden, d1p[...]).astype(BF)
        grad_hidden = nn(grad_sect[rows], d1p[...])
        grad_gate = (grad_hidden * up * (sig * (1.0 + gate * (1.0 - sig)))).astype(BF)
        grad_up = (grad_hidden * act).astype(BF)
        gate_grad_o[rows] = nt(grad_gate, g2p[...]).astype(BF)
        up_grad_o[rows] = nt(grad_up, u2p[...]).astype(BF)
        hidden_s[rows] = hidden
        gate_s[rows] = grad_gate
        up_s[rows] = grad_up

    tiles(body)
    for i, (a, b, width) in enumerate(((grad_sect, hidden_s, 48), (gate_sect, gate_s, 4), (up_sect, up_s, 4))):
        term = block_grads(width, a[...], b[...])
        for c in range(6):
            start = (i * 6 + c) * INNER
            grads_o[start : start + INNER] = term[:, c * 128 : (c + 1) * 128].astype(BF)

    def diagonal(left, right):
        full = tn(left[...], right[...])
        pieces = [full[64 * k : 64 * k + 48, s : s + 256] for k, s in enumerate(window_starts(INNER))]
        return [pair_columns(*pieces[:2]), pair_columns(*pieces[2:])]

    for i, a in enumerate((gate_grad_o, up_grad_o)):
        one = jnp.concatenate(diagonal(a, normed), axis=1).astype(BF)
        for c in range(6):
            start = GLU_ONE + 96 * c + 48 * i
            grads_o[start : start + 48] = one[:, c * 128 : (c + 1) * 128]
    for i, two in enumerate(diagonal(sect_o, cot)):
        for c in range(3):
            start = GLU_TWO + 48 * (3 * i + c)
            grads_o[start : start + 48] = two[:, c * 128 : (c + 1) * 128].astype(BF)
    grads_o[GLU_TWO + 288 :] = jnp.zeros((32, 128), BF)


def glu_block(h, normed, cot, sects, weights, after=()):
    return call(
        functools.partial(glu_kernel, h), "feed_forward", [((ROWS, 256), BF, PINNED)] * 3 + [((GLU_ROWS, 128), BF)],
        [((256, D), BF)] * 3 + [((ROWS, D), BF)] * 3, 26, 9, (normed, PINNED), cot, *[(v, PINNED) for v in sects],
        weights[1], weights[3], weights[4], after=after,
    )


def column_sums(pair):
    rows = [jnp.sum(v, axis=0, keepdims=True) for v in pair]
    return jnp.concatenate(rows + [jnp.zeros((6, D), F32)], axis=0)


def slot_of(mp, half):
    return jnp.where(mp[0] == half, 0, 1)


def middle_back_kernel(mp, middle_h, cot, gated, sect, vecs, w1p, w2p, *refs):
    glu, (g1p, u1p), outs = [refs[i : i + 4] for i in (0, 4)], refs[8:10], refs[10:]
    (grad_middle_o, grad_gated_o, grads_o, small_o, branch_s, grad_sect_s, middle, in_sems) = outs
    loads = start_all(copies(middle_h, middle, in_sems, ROW_CUTS))
    starts = window_starts(INNER)
    small = jnp.zeros((8, D), F32)
    for i, rows in enumerate(TILES):
        gates, ups = [exchange([v[rows] for v in group]) for group in glu]
        grad = join([nn(gates[k], g1p[k]) + nn(ups[k], u1p[k]) for k in range(4)])
        loads[i].wait()
        mid = middle[rows]
        xhat, rstd = norm_parts(mid)
        small = small + column_sums((grad * xhat, grad))
        grad_middle = cot[rows].astype(F32) + norm_back(grad, xhat, rstd, vecs[2:3])
        grad_middle_o[rows] = grad_middle
        branch = grad_middle.astype(BF)
        branch_s[rows] = branch
        grad_sect = exchange([nt(branch[:, s : s + 256], w2p[m]) for m, s in enumerate(starts)])
        for k in range(4):
            grad_sect_s[rows, k * 256 : (k + 1) * 256] = grad_sect[k]
        grad_gated_o[rows] = join([nn(grad_sect[k], w1p[k]) for k in range(4)]).astype(BF)
    small_o[...] = small
    part = lambda i: slice(i * 256, (i + 1) * 256)
    for half in range(2):
        slot = slot_of(mp, half)
        pair = (2 * half, 2 * half + 1)
        one = pair_columns(*[block_grads(48, grad_sect_s[:, part(k)], gated[:, starts[k] : starts[k] + 256]) for k in pair])
        two = pair_columns(*[block_grads(4, sect[:, part(m)], branch_s[:, starts[m] : starts[m] + 256]) for m in pair])
        for i, v in enumerate((one, two)):
            for c in range(3):
                at = (3 * i + c) * INNER
                grads_o[slot, at : at + INNER] = v[:, c * 128 : (c + 1) * 128].astype(BF)


def result_kernel(middle_h, *refs):
    sects, (d2p, result_h, mark, middle, result_s, in_sems, out_sems) = refs[:4], refs[4:]
    mark[...] = jnp.zeros((8, 128), F32)
    loads = start_all(copies(middle_h, middle, in_sems, ROW_CUTS))
    stores = copies(result_s, result_h, out_sems, ROW_CUTS)
    for i, rows in enumerate(TILES):
        out = join([nn(v, d2p[m]) for m, v in enumerate(exchange([v[rows] for v in sects]))])
        loads[i].wait()
        result_s[rows] = (middle[rows] + out).astype(BF)
        stores[i].start()
    wait_all(stores)


def make_result(middle, sects, d2p, after):
    return call(
        result_kernel, "result", [((ROWS, D), BF, FAR), ((8, 128), F32)],
        [((ROWS, D), F32), ((ROWS, D), BF), SEMS, SEMS], 18, 1, (middle, FAR), *sects, d2p, after=after,
    )


def middle_back(mp, middle, cot, gated, sect, vecs, w1p, w2p, glu, after):
    return call(
        middle_back_kernel, "middle_back",
        [((ROWS, D), F32, PINNED), ((ROWS, D), BF, PINNED), ((2, 6 * INNER, 128), BF), ((8, D), F32)],
        [((ROWS, D), BF), ((ROWS, 1024), BF), ((ROWS, D), F32), SEMS], 26, 9,
        mp, (middle, FAR), cot, (gated, PINNED), (sect, PINNED), vecs, (w1p, PINNED), (w2p, PINNED),
        *[(v, PINNED) for v in glu], after=after,
    )


def mixed_window(grads, start, rows):
    out, width = [], 640
    while width:
        j, at = start // D, start % D
        c, at = at // CHUNK, at % CHUNK
        n = min(width, CHUNK - at)
        out.append(grads[c][j, rows, at : at + n])
        start, width = start + n, width - n
    return jnp.concatenate(out, axis=1)


def mixin_back_kernel(
    tokens_h, m0, m1, m2, vecs, w1, w2, grad_o, norm1, normed_o, grad_sect_o, w1p, w2p, tokens, in_sems
):
    loads = start_all(copies(tokens_h, tokens, in_sems, ROW_CUTS))
    mixer_weights(w1, w2, w1p, w2p, 576)
    small = jnp.zeros((8, D), F32)
    for i, rows in enumerate(TILES):
        windows = [mixed_window((m0, m1, m2), s, rows) for s in window_starts(576)]
        grad_sect = exchange([nt(v, w2p[m]) for m, v in enumerate(windows)])
        for k in range(4):
            grad_sect_o[rows, k * 256 : (k + 1) * 256] = grad_sect[k]
        grad = join([nn(grad_sect[k], w1p[k]) for k in range(4)])
        loads[i].wait()
        xhat, _ = norm_parts(tokens[rows].astype(F32))
        normed_o[rows] = (xhat * vecs[0:1] + vecs[1:2]).astype(BF)
        small = small + column_sums((grad * xhat, grad))
        grad_o[rows] = grad
    norm1[...] = small


def mixin_back(tokens, grads, vecs, w1, w2, after):
    return call(
        mixin_back_kernel, "mixer_input_back",
        [((ROWS, D), F32, PINNED), ((8, D), F32), ((ROWS, D), BF, PINNED), ((ROWS, 1024), BF, PINNED)],
        [((4, 256, 256), BF), ((4, 256, 640), BF), ((ROWS, D), BF), SEMS], 26, 7,
        (tokens, FAR), *[(g, PINNED) for g in grads], vecs, w1, w2, after=after,
    )


def tokens_kernel(tokens_h, grad, grad_middle, vecs, out_h, mark, tokens, out_s, in_sems, out_sems):
    mark[...] = jnp.zeros((8, 128), F32)
    loads = start_all(copies(tokens_h, tokens, in_sems, ROW_CUTS))
    stores = copies(out_s, out_h, out_sems, ROW_CUTS)
    for i, rows in enumerate(TILES):
        loads[i].wait()
        xhat, rstd = norm_parts(tokens[rows].astype(F32))
        out_s[rows] = (grad_middle[rows] + norm_back(grad[rows], xhat, rstd, vecs[0:1])).astype(BF)
        stores[i].start()
    wait_all(stores)


def make_tokens_grad(tokens, grad, grad_middle, vecs, after):
    return call(
        tokens_kernel, "tokens_grad", [((ROWS, D), BF, FAR), ((8, 128), F32)],
        [((ROWS, D), BF), ((ROWS, D), BF), SEMS, SEMS], 18, 1,
        (tokens, FAR), (grad, PINNED), (grad_middle, PINNED), vecs, after=after,
    )


def mixin_grads_kernel(
    own, mp, m0, m1, m2, sect_h, normed, grad_sect, mixout_grads, norm1, norm2, c0, c1, c2, p0, p1, p2, pos, out, sect, sem
):
    part = lambda i: slice(i * 256, (i + 1) * 256)

    def work(half):
        load = pltpu.make_async_copy(sect_h.at[:, half * 512 : half * 512 + 512], sect, sem.at[0])
        load.start()
        pair = (2 * half, 2 * half + 1)
        starts = window_starts(INNER)
        one = pair_columns(*[block_grads(48, grad_sect[:, part(k)], normed[:, starts[k] : starts[k] + 256]) for k in pair])
        load.wait()
        starts = window_starts(576)
        two = pair_columns(
            *[block_grads(4, sect[:, part(m % 2)], mixed_window((m0, m1, m2), starts[m], slice(None))) for m in pair]
        )
        for at, v in ((MIX_IN, one), (MIX_IN + 3 * INNER, two)):
            for c in range(v.shape[1] // 128):
                out[at + c * INNER : at + (c + 1) * INNER] = v[:, c * 128 : (c + 1) * 128].astype(BF)
        cut = lambda v, r, col: v[r : r + 1, col : col + 128]
        conv = lambda r, col: (c0, c1, c2)[col // CHUNK][r : r + 1, col % CHUNK : col % CHUNK + 128]
        small = []
        for v, r in ((norm1, 0), (norm1, 1), (norm2, 0), (norm2, 1)):
            small += [cut(v, r, half * 384 + 128 * i) for i in range(3)]
        small += [conv(9, half * 384 + 128 * i) for i in range(3)]
        for tap in range(3):
            for i in range(9):
                col = half * 1152 + 128 * i
                small.append(conv(3 * (col // D) + tap, col % D))
        small.append(jnp.zeros((6, 128), F32))
        out[MIX_SMALL : MIX_SMALL + 48] = jnp.concatenate(small, axis=0).astype(BF)
        for i in range(3):
            col = half * 384 + 128 * i
            at = MIX_OUT + 128 * i
            out[at : at + 128] = (p0, p1, p2)[col // CHUNK][:, col % CHUNK : col % CHUNK + 128].astype(BF)

    for half in range(2):
        pl.when(mp[0] == (half if own else 1 - half))(functools.partial(work, half))
    out[:MIX_IN] = mixout_grads[0 if own else 1]
    out[MIX_POS : MIX_POS + 16] = jnp.concatenate([pos[...], jnp.zeros((8, 128), F32)], axis=0).astype(BF)
    out[MIX_OUT + 384 :] = jnp.zeros((MIX_ROWS - MIX_OUT - 384, 128), BF)


def mixin_grads(own, mp, grads, sect, normed, grad_sect, extra, after):
    return call(
        functools.partial(mixin_grads_kernel, own), "mixer_input_grads", [((MIX_ROWS, 128), BF)],
        [((ROWS, 512), BF), pltpu.SemaphoreType.DMA((1,))], 20, 0.5, mp, *[(g, PINNED) for g in grads],
        (sect, FAR), (normed, PINNED), (grad_sect, PINNED), *extra, after=after,
    )[0]


def swap_pair(v):
    n = lax.axis_size("mp")
    return lax.ppermute(v, "mp", [(i, (i + 1) % n) for i in range(n)])


def swap_bit(v, bit):
    n = lax.axis_size("dp")
    return lax.ppermute(v, "dp", [(i, i ^ (1 << bit)) for i in range(n)])


def sum_of(a, b):
    return (a.astype(F32) + b.astype(F32)).astype(BF)


def part_of(ref, bit, half):
    return ref[pl.ds(pl.multiple_of(bit * half, 16), half)]


def split_kernel(bits, place, *refs):
    n = len(bits)
    for i in range(n):
        keep, got = refs[2 * i], refs[2 * i + 1]
        send_o, keep_o = refs[2 * n + 2 * i], refs[2 * n + 2 * i + 1]
        half, bit = send_o.shape[0], place[bits[i]]
        send_o[...] = sum_of(part_of(keep, 1 - bit, half), part_of(got, 1 - bit, half))
        keep_o[...] = sum_of(part_of(keep, bit, half), part_of(got, bit, half))


def split(place, bits, pairs, after=()):
    outs = [((p[0].shape[0] // 2, 128), BF) for p in pairs for _ in range(2)]
    flat = [v for p in pairs for v in p]
    got = call(functools.partial(split_kernel, bits), "split", outs, [], 8, 0.1, place, *flat, after=after)
    return [(got[2 * i], got[2 * i + 1]) for i in range(len(pairs))]


def sum_kernel(mine, got, out):
    out[...] = sum_of(mine[...], got[...])


def total(mine, got, after=()):
    return call(sum_kernel, "sum", [(mine.shape, BF)], [], 8, 0.1, mine, got, after=after)[0]


def merge_kernel(bits, place, *refs):
    n = len(bits)
    for i in range(n):
        mine, got, out = refs[2 * i], refs[2 * i + 1], refs[2 * n + i]
        half, bit = mine.shape[0], place[bits[i]]
        out[pl.ds(pl.multiple_of(bit * half, 16), half)] = mine[...]
        out[pl.ds(pl.multiple_of((1 - bit) * half, 16), half)] = got[...]


def merge(place, bits, pairs, after=()):
    outs = [((2 * p[0].shape[0], 128), BF) for p in pairs]
    flat = [v for p in pairs for v in p]
    return call(functools.partial(merge_kernel, bits), "merge", outs, [], 8, 0.1, place, *flat, after=after)


def second_kernel(place, ka, ra, kb, rb, send_a, send_b, keep):
    for i, (mine, got, send, bit) in enumerate(((ka, ra, send_a, place[1]), (kb, rb, send_b, place[0]))):
        half = send.shape[0]
        send[...] = sum_of(part_of(mine, 1 - bit, half), part_of(got, 1 - bit, half))
        keep[i * half : (i + 1) * half] = sum_of(part_of(mine, bit, half), part_of(got, bit, half))


def third_kernel(place, keep, ra, rb, send_o, keep_o):
    size = ra.shape[0]
    half, bit = size // 2, place[2]
    for i, got in enumerate((ra, rb)):
        base = i * size
        for out, b in ((send_o, 1 - bit), (keep_o, bit)):
            rows = pl.ds(pl.multiple_of(base + b * half, 16), half)
            out[i * half : (i + 1) * half] = sum_of(keep[rows], part_of(got, b, half))


def fifth_kernel(place, mine, got, a, b):
    half, bit = mine.shape[0] // 2, place[2]
    for i, out in enumerate((a, b)):
        rows = slice(i * half, (i + 1) * half)
        out[pl.ds(pl.multiple_of(bit * half, 16), half)] = mine[rows]
        out[pl.ds(pl.multiple_of((1 - bit) * half, 16), half)] = got[rows]


def joint_steps(place, ka, ra, kb, rb, rest):
    rows = lambda n: ((n, 128), BF)
    size = ka.shape[0]
    after = yield None
    sa, sb, keep = call(
        second_kernel, "second_split", [rows(size // 2)] * 2 + [rows(size)], [], 8, 0.1, place, ka, ra, kb, rb, after=after
    )
    ra, rb = swap_bit(sa, 1), swap_bit(sb, 0)
    after = yield keep, (ra, rb), None
    send, keep = call(third_kernel, "third_split", [rows(size // 2)] * 2, [], 8, 0.1, place, keep, ra, rb, after=after)
    got = swap_bit(send, 2)
    after = yield keep, (got,), None
    out = total(keep, got, after)
    for bit in rest:
        got = swap_bit(out, bit)
        after = yield out, (got,), None
        out = total(out, got, after)
    got = swap_bit(out, 2)
    after = yield out, (got,), None
    a, b = call(fifth_kernel, "first_merge", [rows(size // 2)] * 2, [], 8, 0.1, place, out, got, after=after)
    ra, rb = swap_bit(a, 1), swap_bit(b, 0)
    after = yield a, (ra, rb), None
    a, b = merge(place, (1, 0), [(a, ra), (b, rb)], after)
    ra, rb = swap_bit(a, 0), swap_bit(b, 1)
    yield a, (ra, rb), (a, ra, b, rb)


class Joint:
    def __init__(self, *args):
        self.run = joint_steps(*args)
        next(self.run)
        self.halves = None

    def step(self, *after):
        token, self.coming, self.halves = self.run.send(after)
        return token


def rows_at(mine, got, bit, start, count):
    half = mine.shape[0]
    out, at = [], start
    while at < start + count:
        n = min(count - (at - start), half - at % half)
        local, lower = at % half, at < half
        a, b = mine[local : local + n], got[local : local + n]
        first = bit == 0 if lower else bit == 1
        out.append(jnp.where(first, a, b))
        at += n
    return out[0] if len(out) == 1 else jnp.concatenate(out, axis=0)


def unpack_glu_kernel(place, a0, b0, a1, b1, down_one, gate_two, up_two, gate_one, up_one, down_two, mark):
    mark[...] = jnp.zeros((8, 128), F32)
    for h, (mine, got) in enumerate(((a0, b0), (a1, b1))):
        take = lambda start, count: rows_at(mine, got, place[h], start, count).astype(F32)
        wide = lambda start, rows: jnp.concatenate([take(start + c * rows, rows) for c in range(6)], axis=1)
        down_one[h] = wide(0, INNER)
        gate_two[h] = wide(6 * INNER, INNER).reshape(48, 4, D)
        up_two[h] = wide(12 * INNER, INNER).reshape(48, 4, D)
        ones = wide(GLU_ONE, 96)
        for k in range(4):
            gate_one[k, h] = ones[:48, k * INNER : (k + 1) * INNER]
            up_one[k, h] = ones[48:, k * INNER : (k + 1) * INNER]
        for i in range(2):
            two = jnp.concatenate([take(GLU_TWO + 48 * (3 * i + c), 48) for c in range(3)], axis=1)
            for m in range(2):
                down_two[2 * i + m, :, h, :] = two[:, m * INNER : (m + 1) * INNER]


def unpack_glu(place, parts, after=()):
    outs = [
        ((2, INNER, D), F32), ((2, 48, 4, D), F32), ((2, 48, 4, D), F32), ((4, 2, 48, INNER), F32), ((4, 2, 48, INNER), F32),
        ((4, 48, 2, INNER), F32), ((8, 128), F32),
    ]
    return call(unpack_glu_kernel, "unpack_feed_forward", outs, [], 24, 0.1, place, *parts, after=after)


def unpack_mixer_kernel(place, mp, a0, b0, a1, b1, mixout_one, mixout_two, mixin_one, mixin_two, *refs):
    vecs, (taps, pos_in, pos_bias, pos_out) = refs[:5], refs[5:]
    size = MIX_ROWS // 2

    def take(start, count):
        out, at = [], start
        while at < start + count:
            g = at // size
            n = min(start + count, (g + 1) * size) - at
            mine, got = ((a0, b0), (a1, b1))[g]
            out.append(rows_at(mine, got, place[g], at - g * size, n).astype(F32))
            at += n
        return out[0] if len(out) == 1 else jnp.concatenate(out, axis=0)

    wide = lambda start, rows, n: jnp.concatenate([take(start + c * rows, rows) for c in range(n)], axis=1)
    for base, one, two, e in ((0, mixout_one, mixout_two, INNER), (MIX_IN, mixin_one, mixin_two, 576)):
        ones = wide(base, INNER, 3)
        twos = wide(base + 3 * INNER, INNER, 2 * e // 128)
        for i in range(2):
            one[i] = ones[:, i * INNER : (i + 1) * INNER]
            two[i] = twos[:, i * e : (i + 1) * e].reshape(48, 4, e)
    small = take(MIX_SMALL, 48)
    for i in range(5):
        vecs[i][...] = jnp.concatenate([small[3 * i + c : 3 * i + c + 1] for c in range(3)], axis=1).reshape(384)
    for i in range(3):
        taps[i : i + 1] = jnp.concatenate([small[15 + 9 * i + c : 16 + 9 * i + c] for c in range(9)], axis=1)
    pos = take(MIX_POS, 16)
    pos = jnp.where(mp[0] == 0, pos[:8], pltpu.roll(pos[:8], 64, 1))[:, :64]
    pos_in[...] = pos[:5]
    pos_bias[...] = pos[7:8].reshape(64)
    pos_out[...] = wide(MIX_OUT, 128, 3)


def unpack_mixer(place, mp, parts, after):
    outs = [
        ((2, INNER, INNER), F32), ((2, 48, 4, INNER), F32), ((2, INNER, INNER), F32), ((2, 48, 4, 576), F32),
        *[((384,), F32)] * 5, ((3, 1152), F32), ((5, 64), F32), ((64,), F32), ((128, 384), F32),
    ]
    return call(unpack_mixer_kernel, "unpack_mixer", outs, [], 24, 3, place, mp, *parts, after=after)


def local(
    tokens, short_lengths, long_lengths, cotangent, norm1_gain, norm1_bias, mixin_one, mixin_two, conv_taps, skip_gain,
    pos_in, pos_bias, pos_out, mixout_one, mixout_two, norm2_gain, norm2_bias, gate_one, gate_two, up_one, up_two,
    down_one, down_two,
):
    mp_index = lax.axis_index("mp")
    dp_index = lax.axis_index("dp")
    total_bits = (lax.axis_size("dp") - 1).bit_length()
    mp = mp_index.astype(jnp.int32).reshape(1)
    place = ((dp_index >> jnp.arange(3)) & 1).astype(jnp.int32)
    const = tables()
    rows_first = lambda w: w.transpose(0, 2, 3, 1).reshape(w.shape[0], -1, w.shape[1])
    glu_own = (rows_first(gate_one), gate_two, rows_first(up_one), up_two, rows_first(down_one), down_two)
    glu_other = tuple(swap_pair(w) for w in glu_own)

    vecs, taps = small_params(norm1_gain, norm1_bias, norm2_gain, norm2_bias, skip_gain, conv_taps)
    mixed, sect_in = mixin_forward(
        short_lengths, long_lengths, tokens, vecs, rows_first(mixin_one), mixin_two, (mp, place)
    )
    sin_h, cos_h, kr, ks = make_filter(const, pos_in, pos_bias.reshape(1, -1), pos_out, (sect_in,))
    gated, spread, xr, xs, parts, mixed_saved = conv_forward(const, mixed, taps, vecs, kr, ks)
    middle, normed_two, sect_out, w1p_out, w2p_out = mixout_forward(
        tokens, gated, vecs, rows_first(mixout_one), mixout_two, glu_other
    )

    *sects, g1p, u1p, d2p = glu_sections(normed_two, cotangent, glu_own, glu_other)
    glu_parts = []

    def block(i, after=()):
        weights = glu_own if i % 2 else glu_other
        *parts, grads = glu_block(i // 2, normed_two, cotangent, sects[i::4], weights, after)
        glu_parts.append(parts)
        return grads

    other = block(0)
    own = block(1)
    ((send, keep_a),) = split(place, (0,), [(own, swap_pair(other))])
    got_a = swap_bit(send, 0)
    other = block(2, (keep_a,))
    own = block(3)
    ((send, keep_b),) = split(place, (1,), [(own, swap_pair(other))])
    rest = tuple(range(3, total_bits))
    glu_sum = Joint(place, keep_a, got_a, keep_b, swap_bit(send, 1), rest)
    grad_middle, grad_gated, mixout_grads, norm2_small = middle_back(
        mp, middle, cotangent, gated, sect_out, vecs, w1p_out, w2p_out,
        [parts[i] for i in (1, 2) for parts in glu_parts] + [g1p, u1p], (keep_b,),
    )
    saved = (mixed_saved, parts, xr, xs, spread)
    result, last = make_result(middle, [v[0] for v in glu_parts], d2p, (norm2_small,))
    grads, smalls, outs, hidden = [], [], [], []
    for c in range(D // CHUNK):
        g, small, pos_o, hid = conv_back(
            c, const, short_lengths, long_lengths, saved, taps, vecs, kr, ks, grad_gated, sin_h, cos_h, pos_out,
            hidden if c == D // CHUNK - 1 else [], (glu_sum.step(last),),
        )
        last = small
        grads.append(g)
        smalls.append(small)
        outs.append(pos_o)
        hidden.append(hid)
    grad_normed, norm1_small, normed, grad_sect = mixin_back(
        tokens, grads, vecs, rows_first(mixin_one), mixin_two, (glu_sum.step(last),)
    )
    extra = (mixout_grads, norm1_small, norm2_small, *smalls, *outs, hidden[-1])
    other = mixin_grads(False, mp, grads, sect_in, normed, grad_sect, extra, ())
    own = mixin_grads(True, mp, grads, sect_in, normed, grad_sect, extra, (other,))
    got = swap_pair(other)
    size = MIX_ROWS // 2
    (send_a, keep_a), (send_b, keep_b) = split(place, (0, 1), [(own[:size], got[:size]), (own[size:], got[size:])])
    mix_sum = Joint(place, keep_a, swap_bit(send_a, 0), keep_b, swap_bit(send_b, 1), rest)
    tokens_grad, token = make_tokens_grad(tokens, grad_normed, grad_middle, vecs, (keep_b,))
    for which in (mix_sum, mix_sum, glu_sum, mix_sum, mix_sum, glu_sum):
        token = which.step(token)
    for which in (glu_sum, mix_sum):
        while which.halves is None:
            token = which.step(token)
    down_one_g, gate_two_g, up_two_g, gate_one_g, up_one_g, down_two_g, mark = unpack_glu(place, glu_sum.halves, (token,))
    mixout_one_g, mixout_two_g, mixin_one_g, mixin_two_g, *vecs_g, taps_g, pos_in_g, pos_bias_g, pos_out_g = unpack_mixer(
        place, mp, mix_sum.halves, (mark,)
    )

    natural = lambda v: v.transpose(0, 3, 1, 2)
    one = lambda v: natural(v.reshape(2, 4, 48, INNER))
    return (
        result, tokens_grad, vecs_g[0], vecs_g[1], one(mixin_one_g), mixin_two_g, taps_g, vecs_g[4], pos_in_g, pos_bias_g,
        pos_out_g, one(mixout_one_g), mixout_two_g, vecs_g[2], vecs_g[3], natural(gate_one_g), gate_two_g, natural(up_one_g),
        up_two_g, natural(down_one_g.reshape(2, 4, 48, D)), down_two_g,
    )


def solution(mesh):
    return jax.shard_map(
        local,
        mesh=mesh,
        in_specs=(
            P(("dp", "mp"), None),
            P(("dp", "mp")),
            P(("dp", "mp")),
            P(("dp", "mp"), None),
            *[P()] * 13,
            P(None, None, "mp", None),
            P("mp", None, None, None),
            P(None, None, "mp", None),
            P("mp", None, None, None),
            P("mp", None, None, None),
            P(None, None, "mp", None),
        ),
        out_specs=(
            P(("dp", "mp"), None),
            P(("dp", "mp"), None),
            P("mp"),
            P("mp"),
            P("mp", None, None, None),
            P("mp", None, None, None),
            P(None, "mp"),
            P("mp"),
            P(None, "mp"),
            P("mp"),
            P(None, "mp"),
            P("mp", None, None, None),
            P("mp", None, None, None),
            P("mp"),
            P("mp"),
            P(None, None, "mp", None),
            P("mp", None, None, None),
            P(None, None, "mp", None),
            P("mp", None, None, None),
            P("mp", None, None, None),
            P(None, None, "mp", None),
        ),
        check_vma=False,
    )
```

```python
import functools
import math

import jax
import jax.numpy as jnp
import numpy as np
from jax import lax
from jax.experimental import pallas as pl
from jax.experimental.pallas import tpu as pltpu
from jax.sharding import PartitionSpec as P

BF, F32 = jnp.bfloat16, jnp.float32
SHORT, LONG = 128, 1024
ROWS = SHORT + LONG
D = 768
INNER = 192
EPS = 1e-05
SLOWEST = math.log(100.0) / 1.5
FASTEST = math.log(100.0) / 0.3
TILE = 384
CHUNK = 256
MIB = 1024 * 1024
GLU_ONE, GLU_TWO, GLU_ROWS = 18 * INNER, 21 * INNER, 4352
MIX_IN, MIX_SMALL, MIX_POS, MIX_OUT, MIX_ROWS = 6 * INNER, 18 * INNER, 18 * INNER + 48, 18 * INNER + 64, 4096


def nn(a, b):
    return jnp.dot(a, b, preferred_element_type=F32)


def tn(a, b):
    return lax.dot_general(a, b, (((0,), (0,)), ((), ())), preferred_element_type=F32)


def nt(a, b):
    return lax.dot_general(a, b, (((1,), (1,)), ((), ())), preferred_element_type=F32)


def iota(shape, dim):
    return lax.broadcasted_iota(jnp.int32, shape, dim)


def block_of(index, width, count):
    out = jnp.zeros_like(index)
    for i in range(1, count):
        out = out + (index >= width * i).astype(jnp.int32)
    return out


def ones_where(cond):
    return jnp.where(cond, 1.0, 0.0).astype(BF)


def window_starts(e):
    return [2 * e * (m // 2) + (e // 128 * 128) * (m % 2) for m in range(4)]


def select_rows():
    row, col = iota((256, INNER), 0), iota((256, INNER), 1)
    a, q = row >> 6, row & 63
    return ones_where((col == q * 4 + a) & (q < 48))


def pad_sections(pieces):
    zeros = jnp.zeros((16, pieces[0].shape[1]), pieces[0].dtype)
    return jnp.concatenate([v for p in pieces for v in (p, zeros)], axis=0)


def pad_window(v, k):
    zeros = jnp.zeros((v.shape[0], 64), v.dtype)
    return jnp.concatenate([zeros, v] if k % 2 else [v, zeros], axis=1)


def mixer_weights(w1, w2, w1p, w2p, e):
    for i in range(4):
        w1p[i] = pad_window(pad_sections([w1[i, 48 * m : 48 * m + 48] for m in range(4)]), i)
        w2p[i] = pad_window(nn(select_rows(), w2[i].reshape(INNER, e)).astype(BF), i)


def exchange(blocks):
    blocks = [b.astype(BF) for b in blocks]
    return [jnp.concatenate([b[:, 64 * m : 64 * m + 64] for b in blocks], axis=1) for m in range(4)]


def join(windows):
    out = []
    for a, b in (windows[:2], windows[2:]):
        n = a.shape[1] - 128
        out += [a[:, :n], a[:, n:] + b[:, :128], b[:, 128:]]
    return jnp.concatenate(out, axis=1)


def sections(x, w1p):
    return exchange([nt(x[:, s : s + 256], w1p[k]) for k, s in enumerate(window_starts(INNER))])


def pair_columns(a, b):
    n = a.shape[1] - 128
    lane = iota((a.shape[0], 128), 1)
    return jnp.concatenate([a[:, :n], jnp.where(lane < 64, a[:, n:], b[:, :128]), b[:, 128:]], axis=1)


def block_grads(width, left, right):
    full = tn(left, right)
    if width == 48:
        return jnp.concatenate([full[64 * m : 64 * m + 48] for m in range(4)], axis=0)
    return tn(select_rows(), full.astype(BF))


def norm_parts(x):
    centred = x - jnp.mean(x, axis=-1, keepdims=True)
    rstd = lax.rsqrt(jnp.mean(centred * centred, axis=-1, keepdims=True) + EPS)
    return centred * rstd, rstd


def norm_back(grad, xhat, rstd, gain):
    scaled = grad * gain
    first = jnp.mean(scaled, axis=-1, keepdims=True)
    second = jnp.mean(scaled * xhat, axis=-1, keepdims=True)
    return rstd * (scaled - first - xhat * second)


LIMITS = {"mixer_input": 20, "filters": 14, "conv_forward": 22, "mixer_output": 12, "feed_forward": 18, "feed_forward_sections": 12, "middle_back": 22, "conv_back": 21, "mixer_input_back": 18, "mixer_input_grads": 14, "result": 10, "tokens_grad": 10}
WHOLE, PINNED, FAR = "whole", "pinned", "far"


def by_rows(*shape):
    dim = len(shape) - 2
    block = shape[:dim] + (TILE,) + shape[dim + 1 :]
    return pl.BlockSpec(block, lambda i: (0,) * dim + (i, 0))


def by_columns(*shape):
    lead = len(shape) - 1
    return pl.BlockSpec(shape[:-1] + (CHUNK,), lambda i: (0,) * lead + (i,))


def call(kernel, name, outs, scratch, limit, us, *args, grid=None, aliases=None, after=()):
    inner = kernel
    count, skip = len(args), len(after)
    if skip:
        kernel = lambda *refs: inner(*refs[:count], *refs[count + skip :])
    in_specs, operands, out_specs, out_shape = [], [], [], []
    for arg in args:
        arg, mode = arg if isinstance(arg, tuple) else (arg, WHOLE)
        if arg.dtype == jnp.int32:
            in_specs.append(pl.BlockSpec(memory_space=pltpu.SMEM))
        elif mode == FAR:
            arg = pltpu.with_memory_space_constraint(arg, pltpu.HBM)
            in_specs.append(pl.BlockSpec(memory_space=pl.ANY))
        elif isinstance(mode, pl.BlockSpec):
            arg = pltpu.with_memory_space_constraint(arg, pltpu.HBM)
            in_specs.append(mode)
        else:
            if mode == PINNED:
                arg = pltpu.with_memory_space_constraint(arg, pltpu.VMEM)
            in_specs.append(pl.BlockSpec(memory_space=pltpu.VMEM))
        operands.append(arg)
    for arg in after:
        in_specs.append(pl.BlockSpec(memory_space=pl.ANY))
        operands.append(arg)
    for shape, dtype, *mode in outs:
        mode = mode[0] if mode else WHOLE
        if mode == FAR or isinstance(mode, pl.BlockSpec):
            out_specs.append(pl.BlockSpec(memory_space=pl.ANY) if mode == FAR else mode)
            out_shape.append(pltpu.HBM(shape, dtype))
        else:
            out_specs.append(pl.BlockSpec(memory_space=pltpu.VMEM))
            out_shape.append(pltpu.VMEM(shape, dtype) if mode == PINNED else jax.ShapeDtypeStruct(shape, dtype))
    return pl.pallas_call(
        kernel,
        out_shape=out_shape,
        in_specs=in_specs,
        out_specs=out_specs,
        grid=(grid,) if grid else (),
        scratch_shapes=[pltpu.VMEM(*v) if isinstance(v, tuple) else v for v in scratch],
        input_output_aliases=aliases or {},
        cost_estimate=pl.CostEstimate(flops=int(us * 1.0e9), bytes_accessed=0, transcendentals=0),
        compiler_params=pltpu.CompilerParams(vmem_limit_bytes=LIMITS.get(name, 6) * MIB),
        name=name,
    )(*operands)


TILES = [slice(start, start + TILE) for start in range(0, ROWS, TILE)]
CHUNKS = [slice(start, start + CHUNK) for start in range(0, D, CHUNK)]
ROW_CUTS = [(rows,) for rows in TILES]
COLUMN_CUTS = [(Ellipsis, cols) for cols in CHUNKS]
SEMS = pltpu.SemaphoreType.DMA((3,))


def copies(source, target, sems, cuts):
    return [pltpu.make_async_copy(source.at[cut], target.at[cut], sems.at[i]) for i, cut in enumerate(cuts)]


def start_all(moves):
    for move in moves:
        move.start()
    return moves


def wait_all(*groups):
    for moves in groups:
        for move in moves:
            move.wait()


def first_step(body):
    pl.when(pl.program_id(0) == 0)(body)


def last_step(body):
    pl.when(pl.program_id(0) == pl.num_programs(0) - 1)(body)


def grid_part(size):
    start = pl.multiple_of(pl.program_id(0) * size, size)
    return pl.ds(start, size), start


def tables():
    def phases(n, f, t):
        whole = ((2 * f[:, None] + 1) * (2 * t[None, :] + 1)) % (8 * n)
        angle = whole.astype(np.float64) * (math.pi / (4 * n))
        return np.cos(angle), np.sin(angle)

    half = LONG // 2
    low = np.arange(half, dtype=np.int64)
    short = np.concatenate(phases(SHORT, np.arange(SHORT), np.arange(SHORT)), axis=1)
    parts = [np.concatenate(phases(LONG, low, 2 * low + odd), axis=0) for odd in (0, 1)]
    fraction = np.concatenate([np.arange(SHORT) / SHORT, np.arange(LONG) / LONG])
    order = np.concatenate([low, LONG - 1 - low])
    shift = np.concatenate(
        [(2 * f + 1) * (math.pi / (4 * n)) for f, n in ((np.arange(SHORT), SHORT), (order, LONG))]
    )
    aux = np.zeros((ROWS, 8), np.float32)
    aux[:, 0] = fraction
    for i, band in enumerate((1, 2)):
        aux[:, 1 + i] = np.cos(2.0 * math.pi * band * fraction)
        aux[:, 3 + i] = np.sin(2.0 * math.pi * band * fraction)
    aux[:, 5] = np.cos(shift)
    aux[:, 6] = np.sin(shift)
    aux[:, 7] = 1.0
    rates = SLOWEST + (FASTEST - SLOWEST) * np.arange(D) / (D - 1)
    low_type = lambda t: jnp.asarray(t.astype(np.float32), BF)
    return (
        (low_type(short), *[low_type(p) for p in parts], *[low_type(np.ascontiguousarray(p.T)) for p in parts]),
        jnp.asarray(aux),
        low_type(np.ascontiguousarray(aux.T)),
        jnp.asarray(rates[None].astype(np.float32)),
    )


def scale_rows(shape):
    return jnp.where(iota(shape, 0) < SHORT, 1.0 / SHORT, 1.0 / LONG)


def parity(odd):
    return pl.ds(odd, LONG // 2, stride=2)


LANES = [slice(i, i + 128) for i in range(0, CHUNK, 128)]


def transform(v, tabs, room):
    ts, fe, fo, _, _ = tabs
    head = v[:SHORT].astype(BF)
    for i, lanes in enumerate(LANES):
        room[i] = v[SHORT:, lanes]
    even, odd = [jnp.concatenate([room[i, parity(p)] for i in range(2)], axis=1).astype(BF) for p in (0, 1)]
    e, o = nn(fe[...], even), nn(fo[...], odd)
    h = LONG // 2
    real = jnp.concatenate([nn(ts[:, :SHORT], head), e[:h] + o[:h], e[h:] - o[h:]], axis=0)
    imag = jnp.concatenate([nn(ts[:, SHORT:], head), e[h:] + o[h:], e[:h] - o[:h]], axis=0)
    return real, imag


def restore(real, imag, tabs, room):
    ts, _, _, ie, io = tabs
    h = SHORT + LONG // 2
    head = nn(ts[...], jnp.concatenate([real[:SHORT], imag[:SHORT]], axis=0).astype(BF))
    r0, r1, i0, i1 = real[SHORT:h], real[h:], imag[SHORT:h], imag[h:]
    even = nn(ie[...], jnp.concatenate([r0 + i1, i0 + r1], axis=0).astype(BF))
    odd = nn(io[...], jnp.concatenate([r0 - i1, i0 - r1], axis=0).astype(BF))
    for i, lanes in enumerate(LANES):
        room[i, parity(0)] = even[:, lanes]
        room[i, parity(1)] = odd[:, lanes]
    return jnp.concatenate([head, jnp.concatenate([room[0], room[1]], axis=1)], axis=0)


ROOM = ((2, LONG, 128), F32)


def chunks(body):
    for c in range(D // CHUNK):
        body(slice(c * CHUNK, (c + 1) * CHUNK))


def tiles(body):
    for start in range(0, ROWS, TILE):
        body(slice(start, start + TILE), start)


def small_kernel(*refs):
    far, (vecs_o, taps_o), near, sems = refs[:6], refs[6:8], refs[8:14], refs[14]
    copies = [pltpu.make_async_copy(f, n, sems.at[i]) for i, (f, n) in enumerate(zip(far, near))]
    for copy in copies:
        copy.start()
    for copy in copies:
        copy.wait()
    vecs_o[...] = jnp.concatenate([v[...].reshape(1, D) for v in near[:5]] + [jnp.zeros((3, D), F32)], axis=0)
    taps = [near[5][i : i + 1, j * D : (j + 1) * D] for j in range(3) for i in range(3)]
    taps_o[...] = jnp.concatenate(taps + [jnp.zeros((7, D), F32)], axis=0)


def small_params(*args):
    return call(
        small_kernel, "small_parameters", [((8, D), F32), ((16, D), F32)],
        [((D,), F32)] * 5 + [((3, 3 * D), F32), pltpu.SemaphoreType.DMA((6,))], 8, 1, *[(v, FAR) for v in args],
    )


def sin_cos(x):
    turns = jnp.floor(x * (2.0 / math.pi) + 0.5)
    r = ((x - turns * 1.5703125) - turns * 4.837512969970703125e-4) - turns * 7.54978995489188216e-8
    z = r * r
    s = r + r * z * (-1.6666654611e-1 + z * (8.3321608736e-3 - 1.9515295891e-4 * z))
    c = 1.0 - 0.5 * z + z * z * (4.166664568298827e-2 + z * (-1.388731625493765e-3 + 2.443315711809948e-5 * z))
    quarter = turns.astype(jnp.int32) & 3
    odd = (quarter & 1) == 1
    sine = jnp.where(odd, c, s)
    cosine = jnp.where(odd, s, c)
    return jnp.where(quarter >= 2, -sine, sine), jnp.where((quarter == 1) | (quarter == 2), -cosine, cosine)


def filter_kernel(aux, pos_in, pos_bias, pos_out, rates, *refs):
    *tabs, sin_o, cos_o, kr_o, ks_o, room = refs
    pre = jnp.broadcast_to(pos_bias[...], (ROWS, 128))
    for i in range(5):
        pre = pre + aux[:, i : i + 1] * pos_in[i : i + 1, :]
    sin_o[...], cos_o[...] = sin_cos(pre)

    for c, cols in enumerate(CHUNKS):
        hidden = sin_o[...]
        high = hidden.astype(BF)
        low = (hidden - high.astype(F32)).astype(BF)
        w = pos_out[:, cols]
        w_high = w.astype(BF)
        w_low = (w - w_high.astype(F32)).astype(BF)
        shaped = nn(high, w_high) + nn(high, w_low) + nn(low, w_high)
        kern = shaped * jnp.exp(-aux[:, 0:1] * rates[:, cols])
        a, b = transform(kern, tabs, room.at[c])
        cos_h, sin_h = aux[:, 5:6], aux[:, 6:7]
        scale = scale_rows((ROWS, 1))
        kr_o[:, cols] = ((cos_h * a + sin_h * b) * scale).astype(BF)
        ks_o[:, cols] = ((cos_h * b - sin_h * a) * scale).astype(BF)


def make_filter(const, pos_in, pos_bias, pos_out, after):
    tabs, aux, _, rates = const
    return call(
        filter_kernel, "filters", [((ROWS, 128), F32, PINNED)] * 2 + [((ROWS, D), BF, PINNED)] * 2, [((3, *ROOM[0]), F32)], 10, 6,
        aux, pos_in, pos_bias, pos_out, rates, *tabs, after=after,
    )


def row_valid(short_len, long_len, start, rows):
    row = iota((rows, 1), 0) + start
    limit = jnp.where(row < SHORT, short_len[0], long_len[0] + SHORT)
    return row < limit


def mixin_kernel(
    short_len, long_len, tokens_h, vecs, w1, w2, mixed_o, sect_h, w1p, w2p, tokens, sect_s, in_sems, out_sems
):
    loads = start_all(copies(tokens_h, tokens, in_sems, ROW_CUTS))
    stores = copies(sect_s, sect_h, out_sems, ROW_CUTS)
    mixer_weights(w1, w2, w1p, w2p, 576)
    for i, rows in enumerate(TILES):
        loads[i].wait()
        xhat, _ = norm_parts(tokens[rows].astype(F32))
        normed = (xhat * vecs[0:1] + vecs[1:2]).astype(BF)
        sect = sections(normed, w1p)
        for m in range(4):
            sect_s[rows, m * 256 : (m + 1) * 256] = sect[m]
        stores[i].start()
        valid = row_valid(short_len, long_len, rows.start, TILE)
        full = jnp.where(valid, join([nn(sect[m], w2p[m]) for m in range(4)]), 0.0).astype(BF)
        for j in range(3):
            mixed_o[j, rows] = full[:, j * D : (j + 1) * D]
    wait_all(stores)


def mixin_forward(short_len, long_len, tokens, vecs, w1, w2, after):
    return call(
        mixin_kernel, "mixer_input", [((3, ROWS, D), BF, PINNED), ((ROWS, 1024), BF, FAR)],
        [((4, 256, 256), BF), ((4, 256, 640), BF), ((ROWS, D), BF), ((ROWS, 1024), BF), SEMS, SEMS], 22, 6,
        short_len, long_len, (tokens, FAR), vecs, w1, w2, after=after,
    )


def edges(shape):
    row = iota(shape, 0)
    first = (row == 0) | (row == SHORT)
    last = (row == SHORT - 1) | (row == ROWS - 1)
    return first, last


def before(v, first):
    return jnp.where(first, 0.0, pltpu.roll(v, 1, 0))


def after(v, last):
    return jnp.where(last, 0.0, pltpu.roll(v, ROWS - 1, 0))


def tap_rows(taps, cols, j):
    return [taps[3 * j + i : 3 * j + i + 1, cols] for i in range(3)]


def conv_forward_kernel(mixed, taps, vecs, kr, ks, *refs):
    tabs, gated_o, far, near, (mixed_h, room), sems = refs[:5], refs[5], refs[6:10], refs[11:15], (refs[10], refs[15]), refs[16]
    save = pltpu.make_async_copy(mixed, mixed_h, sems.at[4, 0])
    save.start()
    stores = [copies(v, f, sems.at[i], COLUMN_CUTS) for i, (v, f) in enumerate(zip(near, far))]
    spread_s, xr_s, xs_s, parts_s = near
    first, last = edges((ROWS, CHUNK))
    for c, cols in enumerate(CHUNKS):
        parts = []
        for j in range(3):
            m = mixed[j, :, cols].astype(F32)
            t0, t1, t2 = tap_rows(taps, cols, j)
            parts.append(t0 * before(m, first) + t1 * m + t2 * after(m, last))
            parts_s[j, :, cols] = parts[j].astype(BF)
        stores[3][c].start()
        product = parts[0] * parts[2]
        real, imag = transform(product, tabs, room.at[c])
        xr_s[:, cols] = real.astype(BF)
        xs_s[:, cols] = imag.astype(BF)
        stores[1][c].start()
        stores[2][c].start()
        a, b = kr[:, cols].astype(F32), ks[:, cols].astype(F32)
        spread = restore(real * a - imag * b, real * b + imag * a, tabs, room.at[c])
        spread = spread + vecs[4:5, cols] * product
        spread_s[:, cols] = spread.astype(BF)
        gated_o[:, cols] = (spread * parts[1]).astype(BF)
        stores[0][c].start()
    wait_all([save], *stores)


def conv_forward(const, mixed, taps, vecs, kr, ks):
    one, three = ((ROWS, D), BF), ((3, ROWS, D), BF)
    return call(
        conv_forward_kernel, "conv_forward",
        [(*one, PINNED), (*one, FAR), (*one, FAR), (*one, FAR), (*three, FAR), (*three, FAR)],
        [one, one, one, three, ((3, *ROOM[0]), F32), pltpu.SemaphoreType.DMA((5, 3))], 22, 9,
        (mixed, PINNED), taps, vecs, (kr, PINNED), (ks, PINNED), *const[0],
    )


def conv_back_kernel(
    c, short_len, long_len, mixed_h, parts_h, taps, vecs, kr, ks, xr_h, xs_h, spread_h, grad_gated, sin_h, cos_h, aux, features, pos_out,
    rates, *rest
):
    tabs = rest[:5]
    *earlier, grad_o, small_o, pos_out_o, hidden_o, mixed, parts, xr, xs, spread, sems, room = rest[5:]
    cols = slice(c * CHUNK, (c + 1) * CHUNK)
    copies = [
        pltpu.make_async_copy(far.at[..., cols], near, sems.at[i])
        for i, (far, near) in enumerate(((parts_h, parts), (xr_h, xr), (xs_h, xs), (spread_h, spread), (mixed_h, mixed)))
    ]
    for copy in copies:
        copy.start()
    first, last = edges((ROWS, CHUNK))
    gg = grad_gated[:, cols].astype(F32)
    copies[0].wait()
    grad_spread = gg * parts[1].astype(F32)
    real, imag = transform(grad_spread, tabs, room)
    a, b = kr[:, cols].astype(F32), ks[:, cols].astype(F32)
    grad_product = restore(a * real + b * imag, a * imag - b * real, tabs, room)
    grad_product = grad_product + vecs[4:5, cols] * grad_spread
    copies[1].wait()
    copies[2].wait()
    x_real, x_imag = xr[...].astype(F32), xs[...].astype(F32)
    z_real = x_real * real + x_imag * imag
    z_imag = x_real * imag - x_imag * real
    cos_p, sin_p = aux[:, 5:6], aux[:, 6:7]
    grad_kernel = restore(cos_p * z_real - sin_p * z_imag, cos_p * z_imag + sin_p * z_real, tabs, room)
    shaped_grad = (grad_kernel * (scale_rows((ROWS, 1)) * jnp.exp(-aux[:, 0:1] * rates[:, cols]))).astype(BF)
    pos_out_o[...] = tn(sin_h[...].astype(BF), shaped_grad)
    hidden = nt(shaped_grad, pos_out[:, cols].astype(BF))
    copies[3].wait()
    copies[4].wait()
    front = parts[0].astype(F32)
    value = parts[2].astype(F32)
    grads = (grad_product * value, gg * spread[...].astype(F32), grad_product * front)
    valid = row_valid(short_len, long_len, 0, ROWS)
    small = []
    for j in range(3):
        m = mixed[j].astype(F32)
        g = grads[j]
        up, down = after(g, last), before(g, first)
        t0, t1, t2 = tap_rows(taps, cols, j)
        small += [jnp.sum(v * m, axis=0, keepdims=True) for v in (up, g, down)]
        grad_o[j] = jnp.where(valid, t0 * up + t1 * g + t2 * down, 0.0).astype(BF)
    small.append(jnp.sum(grad_spread * front * value, axis=0, keepdims=True))
    small.append(jnp.zeros((6, CHUNK), F32))
    small_o[...] = jnp.concatenate(small, axis=0)
    if not earlier:
        hidden_o[...] = hidden
    else:
        pre = (hidden + earlier[0][...] + earlier[1][...]) * cos_h[...]
        hidden_o[...] = nn(features[...], pre.astype(BF))


def conv_back(c, const, short_len, long_len, saved, taps, vecs, kr, ks, grad_gated, sin_h, cos_h, pos_out, earlier, after):
    tabs, aux, features, rates = const
    mixed, parts, xr, xs, spread = saved
    final = len(earlier) > 0
    one = ((ROWS, CHUNK), BF)
    three = ((3, ROWS, CHUNK), BF)
    return call(
        functools.partial(conv_back_kernel, c), "conv_back",
        [(*three, PINNED), ((16, CHUNK), F32), ((128, CHUNK), F32)] + ([((8, 128), F32)] if final else [((ROWS, 128), F32, PINNED)]),
        [three, three, one, one, one, pltpu.SemaphoreType.DMA((5,)), ROOM], 30, 8,
        short_len, long_len, (mixed, FAR), (parts, FAR), taps, vecs, (kr, PINNED), (ks, PINNED), (xr, FAR), (xs, FAR),
        (spread, FAR), (grad_gated, PINNED), (sin_h, PINNED), (cos_h, PINNED), aux, features, pos_out, rates, *tabs,
        *[(v, PINNED) for v in earlier], after=after,
    )


def mixout_kernel(
    tokens_h, gated, vecs, w1, w2, middle_h, normed_o, sect_o, w1p, w2p, tokens, middle_s, in_sems, out_sems
):
    loads = start_all(copies(tokens_h, tokens, in_sems, ROW_CUTS))
    stores = copies(middle_s, middle_h, out_sems, ROW_CUTS)
    mixer_weights(w1, w2, w1p, w2p, INNER)
    for i, rows in enumerate(TILES):
        sect = sections(gated[rows], w1p)
        for m in range(4):
            sect_o[rows, m * 256 : (m + 1) * 256] = sect[m]
        loads[i].wait()
        middle = tokens[rows].astype(F32) + join([nn(sect[m], w2p[m]) for m in range(4)])
        middle_s[rows] = middle
        stores[i].start()
        xhat, _ = norm_parts(middle)
        normed_o[rows] = (xhat * vecs[2:3] + vecs[3:4]).astype(BF)
    wait_all(stores)


def mixout_forward(tokens, gated, vecs, w1, w2, after):
    return call(
        mixout_kernel, "mixer_output",
        [
            ((ROWS, D), F32, FAR), ((ROWS, D), BF, PINNED), ((ROWS, 1024), BF, PINNED), ((4, 256, 256), BF, PINNED),
            ((4, 256, 256), BF, PINNED),
        ],
        [((ROWS, D), BF), ((ROWS, D), F32), SEMS, SEMS], 18, 5, (tokens, FAR), (gated, PINNED), vecs, w1, w2, after=after,
    )


def select_pair():
    row, col = iota((256, INNER), 0), iota((256, INNER), 1)
    block, q = row >> 6, row & 63
    return ones_where((col == (block & 1) * 96 + q * 2 + (block >> 1)) & (q < 48))


def sections_kernel(normed, cot, g1, u1, d2, own_g1, own_u1, own_d2, *refs):
    gate_o, up_o, grad_o, (g1p, u1p, d2p) = refs[:4], refs[4:8], refs[8:12], refs[12:]

    for i in range(4):
        for out, pair in ((g1p, (g1, own_g1)), (u1p, (u1, own_u1))):
            out[i] = pad_window(pad_sections([w[i, 48 * h : 48 * h + 48] for h in range(2) for w in pair]), i)
        both = jnp.concatenate([w[i].reshape(96, INNER) for w in (d2, own_d2)], axis=0)
        d2p[i] = pad_window(nn(select_pair(), both).astype(BF), i)
    for rows in TILES:
        for x, weights, outs in ((normed, g1p, gate_o), (normed, u1p, up_o), (cot, d2p, grad_o)):
            for out, v in zip(outs, sections(x[rows], weights)):
                out[rows] = v


def glu_sections(normed, cot, own, other):
    return call(
        sections_kernel, "feed_forward_sections", [((ROWS, 256), BF, PINNED)] * 12 + [((4, 256, 256), BF, PINNED)] * 3, [], 8, 4,
        (normed, PINNED), cot, other[0], other[2], other[5], own[0], own[2], own[5],
    )


def glu_kernel(
    h, normed, cot, gate_sect, up_sect, grad_sect, g2, u2, d1, sect_o, gate_grad_o, up_grad_o, grads_o,
    g2p, u2p, d1p, hidden_s, gate_s, up_s
):
    g2p[...] = nn(select_rows(), g2[h].reshape(INNER, D)).astype(BF)
    u2p[...] = nn(select_rows(), u2[h].reshape(INNER, D)).astype(BF)
    d1p[...] = pad_sections([d1[h, 48 * m : 48 * m + 48] for m in range(4)])

    def body(rows, start):
        gate = nn(gate_sect[rows], g2p[...])
        up = nn(up_sect[rows], u2p[...])
        sig = jax.nn.sigmoid(gate)
        act = gate * sig
        hidden = (act * up).astype(BF)
        sect_o[rows] = nt(hidden, d1p[...]).astype(BF)
        grad_hidden = nn(grad_sect[rows], d1p[...])
        grad_gate = (grad_hidden * up * (sig * (1.0 + gate * (1.0 - sig)))).astype(BF)
        grad_up = (grad_hidden * act).astype(BF)
        gate_grad_o[rows] = nt(grad_gate, g2p[...]).astype(BF)
        up_grad_o[rows] = nt(grad_up, u2p[...]).astype(BF)
        hidden_s[rows] = hidden
        gate_s[rows] = grad_gate
        up_s[rows] = grad_up

    tiles(body)
    for i, (a, b, width) in enumerate(((grad_sect, hidden_s, 48), (gate_sect, gate_s, 4), (up_sect, up_s, 4))):
        term = block_grads(width, a[...], b[...])
        for c in range(6):
            start = (i * 6 + c) * INNER
            grads_o[start : start + INNER] = term[:, c * 128 : (c + 1) * 128].astype(BF)

    def diagonal(left, right):
        full = tn(left[...], right[...])
        pieces = [full[64 * k : 64 * k + 48, s : s + 256] for k, s in enumerate(window_starts(INNER))]
        return [pair_columns(*pieces[:2]), pair_columns(*pieces[2:])]

    for i, a in enumerate((gate_grad_o, up_grad_o)):
        one = jnp.concatenate(diagonal(a, normed), axis=1).astype(BF)
        for c in range(6):
            start = GLU_ONE + 96 * c + 48 * i
            grads_o[start : start + 48] = one[:, c * 128 : (c + 1) * 128]
    for i, two in enumerate(diagonal(sect_o, cot)):
        for c in range(3):
            start = GLU_TWO + 48 * (3 * i + c)
            grads_o[start : start + 48] = two[:, c * 128 : (c + 1) * 128].astype(BF)
    grads_o[GLU_TWO + 288 :] = jnp.zeros((32, 128), BF)


def glu_block(h, normed, cot, sects, weights, after=()):
    return call(
        functools.partial(glu_kernel, h), "feed_forward", [((ROWS, 256), BF, PINNED)] * 3 + [((GLU_ROWS, 128), BF)],
        [((256, D), BF)] * 3 + [((ROWS, D), BF)] * 3, 26, 9, (normed, PINNED), cot, *[(v, PINNED) for v in sects],
        weights[1], weights[3], weights[4], after=after,
    )


def column_sums(pair):
    rows = [jnp.sum(v, axis=0, keepdims=True) for v in pair]
    return jnp.concatenate(rows + [jnp.zeros((6, D), F32)], axis=0)


def slot_of(mp, half):
    return jnp.where(mp[0] == half, 0, 1)


def middle_back_kernel(mp, middle_h, cot, gated, sect, vecs, w1p, w2p, *refs):
    glu, (g1p, u1p), outs = [refs[i : i + 4] for i in (0, 4)], refs[8:10], refs[10:]
    (grad_middle_o, grad_gated_o, grads_o, small_o, branch_s, grad_sect_s, middle, in_sems) = outs
    loads = start_all(copies(middle_h, middle, in_sems, ROW_CUTS))
    starts = window_starts(INNER)
    small = jnp.zeros((8, D), F32)
    for i, rows in enumerate(TILES):
        gates, ups = [exchange([v[rows] for v in group]) for group in glu]
        grad = join([nn(gates[k], g1p[k]) + nn(ups[k], u1p[k]) for k in range(4)])
        loads[i].wait()
        mid = middle[rows]
        xhat, rstd = norm_parts(mid)
        small = small + column_sums((grad * xhat, grad))
        grad_middle = cot[rows].astype(F32) + norm_back(grad, xhat, rstd, vecs[2:3])
        grad_middle_o[rows] = grad_middle
        branch = grad_middle.astype(BF)
        branch_s[rows] = branch
        grad_sect = exchange([nt(branch[:, s : s + 256], w2p[m]) for m, s in enumerate(starts)])
        for k in range(4):
            grad_sect_s[rows, k * 256 : (k + 1) * 256] = grad_sect[k]
        grad_gated_o[rows] = join([nn(grad_sect[k], w1p[k]) for k in range(4)]).astype(BF)
    small_o[...] = small
    part = lambda i: slice(i * 256, (i + 1) * 256)
    for half in range(2):
        slot = slot_of(mp, half)
        pair = (2 * half, 2 * half + 1)
        one = pair_columns(*[block_grads(48, grad_sect_s[:, part(k)], gated[:, starts[k] : starts[k] + 256]) for k in pair])
        two = pair_columns(*[block_grads(4, sect[:, part(m)], branch_s[:, starts[m] : starts[m] + 256]) for m in pair])
        for i, v in enumerate((one, two)):
            for c in range(3):
                at = (3 * i + c) * INNER
                grads_o[slot, at : at + INNER] = v[:, c * 128 : (c + 1) * 128].astype(BF)


def result_kernel(middle_h, *refs):
    sects, (d2p, result_h, mark, middle, result_s, in_sems, out_sems) = refs[:4], refs[4:]
    mark[...] = jnp.zeros((8, 128), F32)
    loads = start_all(copies(middle_h, middle, in_sems, ROW_CUTS))
    stores = copies(result_s, result_h, out_sems, ROW_CUTS)
    for i, rows in enumerate(TILES):
        out = join([nn(v, d2p[m]) for m, v in enumerate(exchange([v[rows] for v in sects]))])
        loads[i].wait()
        result_s[rows] = (middle[rows] + out).astype(BF)
        stores[i].start()
    wait_all(stores)


def make_result(middle, sects, d2p, after):
    return call(
        result_kernel, "result", [((ROWS, D), BF, FAR), ((8, 128), F32)],
        [((ROWS, D), F32), ((ROWS, D), BF), SEMS, SEMS], 18, 1, (middle, FAR), *sects, d2p, after=after,
    )


def middle_back(mp, middle, cot, gated, sect, vecs, w1p, w2p, glu, after):
    return call(
        middle_back_kernel, "middle_back",
        [((ROWS, D), F32, PINNED), ((ROWS, D), BF, PINNED), ((2, 6 * INNER, 128), BF), ((8, D), F32)],
        [((ROWS, D), BF), ((ROWS, 1024), BF), ((ROWS, D), F32), SEMS], 26, 9,
        mp, (middle, FAR), cot, (gated, PINNED), (sect, PINNED), vecs, (w1p, PINNED), (w2p, PINNED),
        *[(v, PINNED) for v in glu], after=after,
    )


def mixed_window(grads, start, rows):
    out, width = [], 640
    while width:
        j, at = start // D, start % D
        c, at = at // CHUNK, at % CHUNK
        n = min(width, CHUNK - at)
        out.append(grads[c][j, rows, at : at + n])
        start, width = start + n, width - n
    return jnp.concatenate(out, axis=1)


def mixin_back_kernel(
    tokens_h, m0, m1, m2, vecs, w1, w2, grad_o, norm1, normed_o, grad_sect_o, w1p, w2p, tokens, in_sems
):
    loads = start_all(copies(tokens_h, tokens, in_sems, ROW_CUTS))
    mixer_weights(w1, w2, w1p, w2p, 576)
    small = jnp.zeros((8, D), F32)
    for i, rows in enumerate(TILES):
        windows = [mixed_window((m0, m1, m2), s, rows) for s in window_starts(576)]
        grad_sect = exchange([nt(v, w2p[m]) for m, v in enumerate(windows)])
        for k in range(4):
            grad_sect_o[rows, k * 256 : (k + 1) * 256] = grad_sect[k]
        grad = join([nn(grad_sect[k], w1p[k]) for k in range(4)])
        loads[i].wait()
        xhat, _ = norm_parts(tokens[rows].astype(F32))
        normed_o[rows] = (xhat * vecs[0:1] + vecs[1:2]).astype(BF)
        small = small + column_sums((grad * xhat, grad))
        grad_o[rows] = grad
    norm1[...] = small


def mixin_back(tokens, grads, vecs, w1, w2, after):
    return call(
        mixin_back_kernel, "mixer_input_back",
        [((ROWS, D), F32, PINNED), ((8, D), F32), ((ROWS, D), BF, PINNED), ((ROWS, 1024), BF, PINNED)],
        [((4, 256, 256), BF), ((4, 256, 640), BF), ((ROWS, D), BF), SEMS], 26, 7,
        (tokens, FAR), *[(g, PINNED) for g in grads], vecs, w1, w2, after=after,
    )


def tokens_kernel(tokens_h, grad, grad_middle, vecs, out_h, mark, tokens, out_s, in_sems, out_sems):
    mark[...] = jnp.zeros((8, 128), F32)
    loads = start_all(copies(tokens_h, tokens, in_sems, ROW_CUTS))
    stores = copies(out_s, out_h, out_sems, ROW_CUTS)
    for i, rows in enumerate(TILES):
        loads[i].wait()
        xhat, rstd = norm_parts(tokens[rows].astype(F32))
        out_s[rows] = (grad_middle[rows] + norm_back(grad[rows], xhat, rstd, vecs[0:1])).astype(BF)
        stores[i].start()
    wait_all(stores)


def make_tokens_grad(tokens, grad, grad_middle, vecs, after):
    return call(
        tokens_kernel, "tokens_grad", [((ROWS, D), BF, FAR), ((8, 128), F32)],
        [((ROWS, D), BF), ((ROWS, D), BF), SEMS, SEMS], 18, 1,
        (tokens, FAR), (grad, PINNED), (grad_middle, PINNED), vecs, after=after,
    )


def mixin_grads_kernel(
    own, mp, m0, m1, m2, sect_h, normed, grad_sect, mixout_grads, norm1, norm2, c0, c1, c2, p0, p1, p2, pos, out, sect, sem
):
    part = lambda i: slice(i * 256, (i + 1) * 256)

    def work(half):
        load = pltpu.make_async_copy(sect_h.at[:, half * 512 : half * 512 + 512], sect, sem.at[0])
        load.start()
        pair = (2 * half, 2 * half + 1)
        starts = window_starts(INNER)
        one = pair_columns(*[block_grads(48, grad_sect[:, part(k)], normed[:, starts[k] : starts[k] + 256]) for k in pair])
        load.wait()
        starts = window_starts(576)
        two = pair_columns(
            *[block_grads(4, sect[:, part(m % 2)], mixed_window((m0, m1, m2), starts[m], slice(None))) for m in pair]
        )
        for at, v in ((MIX_IN, one), (MIX_IN + 3 * INNER, two)):
            for c in range(v.shape[1] // 128):
                out[at + c * INNER : at + (c + 1) * INNER] = v[:, c * 128 : (c + 1) * 128].astype(BF)
        cut = lambda v, r, col: v[r : r + 1, col : col + 128]
        conv = lambda r, col: (c0, c1, c2)[col // CHUNK][r : r + 1, col % CHUNK : col % CHUNK + 128]
        small = []
        for v, r in ((norm1, 0), (norm1, 1), (norm2, 0), (norm2, 1)):
            small += [cut(v, r, half * 384 + 128 * i) for i in range(3)]
        small += [conv(9, half * 384 + 128 * i) for i in range(3)]
        for tap in range(3):
            for i in range(9):
                col = half * 1152 + 128 * i
                small.append(conv(3 * (col // D) + tap, col % D))
        small.append(jnp.zeros((6, 128), F32))
        out[MIX_SMALL : MIX_SMALL + 48] = jnp.concatenate(small, axis=0).astype(BF)
        for i in range(3):
            col = half * 384 + 128 * i
            at = MIX_OUT + 128 * i
            out[at : at + 128] = (p0, p1, p2)[col // CHUNK][:, col % CHUNK : col % CHUNK + 128].astype(BF)

    for half in range(2):
        pl.when(mp[0] == (half if own else 1 - half))(functools.partial(work, half))
    out[:MIX_IN] = mixout_grads[0 if own else 1]
    out[MIX_POS : MIX_POS + 16] = jnp.concatenate([pos[...], jnp.zeros((8, 128), F32)], axis=0).astype(BF)
    out[MIX_OUT + 384 :] = jnp.zeros((MIX_ROWS - MIX_OUT - 384, 128), BF)


def mixin_grads(own, mp, grads, sect, normed, grad_sect, extra, after):
    return call(
        functools.partial(mixin_grads_kernel, own), "mixer_input_grads", [((MIX_ROWS, 128), BF)],
        [((ROWS, 512), BF), pltpu.SemaphoreType.DMA((1,))], 20, 0.5, mp, *[(g, PINNED) for g in grads],
        (sect, FAR), (normed, PINNED), (grad_sect, PINNED), *extra, after=after,
    )[0]


def swap_pair(v):
    n = lax.axis_size("mp")
    return lax.ppermute(v, "mp", [(i, (i + 1) % n) for i in range(n)])


def swap_bit(v, bit):
    n = lax.axis_size("dp")
    return lax.ppermute(v, "dp", [(i, i ^ (1 << bit)) for i in range(n)])


def sum_of(a, b):
    return (a.astype(F32) + b.astype(F32)).astype(BF)


def bit_of(place, bit):
    return (place[0] >> bit) & 1


def part_of(ref, bit, half):
    return ref[pl.ds(pl.multiple_of(bit * half, 16), half)]


def split_kernel(bits, place, *refs):
    n = len(bits)
    for i in range(n):
        keep, got = refs[2 * i], refs[2 * i + 1]
        send_o, keep_o = refs[2 * n + 2 * i], refs[2 * n + 2 * i + 1]
        half, bit = send_o.shape[0], bit_of(place, bits[i])
        send_o[...] = sum_of(part_of(keep, 1 - bit, half), part_of(got, 1 - bit, half))
        keep_o[...] = sum_of(part_of(keep, bit, half), part_of(got, bit, half))


def split(place, bits, pairs, after=()):
    outs = [((p[0].shape[0] // 2, 128), BF) for p in pairs for _ in range(2)]
    flat = [v for p in pairs for v in p]
    got = call(functools.partial(split_kernel, bits), "split", outs, [], 8, 0.1, place, *flat, after=after)
    return [(got[2 * i], got[2 * i + 1]) for i in range(len(pairs))]


def sum_kernel(mine, got, out):
    out[...] = sum_of(mine[...], got[...])


def total(mine, got, after=()):
    return call(sum_kernel, "sum", [(mine.shape, BF)], [], 8, 0.1, mine, got, after=after)[0]


def merge_kernel(bits, place, *refs):
    n = len(bits)
    for i in range(n):
        mine, got, out = refs[2 * i], refs[2 * i + 1], refs[2 * n + i]
        half, bit = mine.shape[0], bit_of(place, bits[i])
        out[pl.ds(pl.multiple_of(bit * half, 16), half)] = mine[...]
        out[pl.ds(pl.multiple_of((1 - bit) * half, 16), half)] = got[...]


def merge(place, bits, pairs, after=()):
    outs = [((2 * p[0].shape[0], 128), BF) for p in pairs]
    flat = [v for p in pairs for v in p]
    return call(functools.partial(merge_kernel, bits), "merge", outs, [], 8, 0.1, place, *flat, after=after)


def second_kernel(place, ka, ra, kb, rb, send_a, send_b, keep):
    for i, (mine, got, send, bit) in enumerate(((ka, ra, send_a, bit_of(place, 1)), (kb, rb, send_b, bit_of(place, 0)))):
        half = send.shape[0]
        send[...] = sum_of(part_of(mine, 1 - bit, half), part_of(got, 1 - bit, half))
        keep[i * half : (i + 1) * half] = sum_of(part_of(mine, bit, half), part_of(got, bit, half))


def third_kernel(place, keep, ra, rb, send_o, keep_o):
    size = ra.shape[0]
    half, bit = size // 2, bit_of(place, 2)
    for i, got in enumerate((ra, rb)):
        base = i * size
        for out, b in ((send_o, 1 - bit), (keep_o, bit)):
            rows = pl.ds(pl.multiple_of(base + b * half, 16), half)
            out[i * half : (i + 1) * half] = sum_of(keep[rows], part_of(got, b, half))


def fifth_kernel(place, mine, got, a, b):
    half, bit = mine.shape[0] // 2, bit_of(place, 2)
    for i, out in enumerate((a, b)):
        rows = slice(i * half, (i + 1) * half)
        out[pl.ds(pl.multiple_of(bit * half, 16), half)] = mine[rows]
        out[pl.ds(pl.multiple_of((1 - bit) * half, 16), half)] = got[rows]


def joint_steps(place, ka, ra, kb, rb, rest):
    rows = lambda n: ((n, 128), BF)
    size = ka.shape[0]
    after = yield None
    sa, sb, keep = call(
        second_kernel, "second_split", [rows(size // 2)] * 2 + [rows(size)], [], 8, 0.1, place, ka, ra, kb, rb, after=after
    )
    ra, rb = swap_bit(sa, 1), swap_bit(sb, 0)
    after = yield keep, (ra, rb), None
    send, keep = call(third_kernel, "third_split", [rows(size // 2)] * 2, [], 8, 0.1, place, keep, ra, rb, after=after)
    got = swap_bit(send, 2)
    after = yield keep, (got,), None
    out = total(keep, got, after)
    for bit in rest:
        got = swap_bit(out, bit)
        after = yield out, (got,), None
        out = total(out, got, after)
    got = swap_bit(out, 2)
    after = yield out, (got,), None
    a, b = call(fifth_kernel, "first_merge", [rows(size // 2)] * 2, [], 8, 0.1, place, out, got, after=after)
    ra, rb = swap_bit(a, 1), swap_bit(b, 0)
    after = yield a, (ra, rb), None
    a, b = merge(place, (1, 0), [(a, ra), (b, rb)], after)
    ra, rb = swap_bit(a, 0), swap_bit(b, 1)
    yield a, (ra, rb), (a, ra, b, rb)


class Joint:
    def __init__(self, *args):
        self.run = joint_steps(*args)
        next(self.run)
        self.halves = None

    def step(self, *after):
        token, self.coming, self.halves = self.run.send(after)
        return token


def rows_at(mine, got, bit, start, count):
    half = mine.shape[0]
    out, at = [], start
    while at < start + count:
        n = min(count - (at - start), half - at % half)
        local, lower = at % half, at < half
        a, b = mine[local : local + n], got[local : local + n]
        first = bit == 0 if lower else bit == 1
        out.append(jnp.where(first, a, b))
        at += n
    return out[0] if len(out) == 1 else jnp.concatenate(out, axis=0)


def unpack_glu_kernel(place, a0, b0, a1, b1, down_one, gate_two, up_two, gate_one, up_one, down_two, mark):
    mark[...] = jnp.zeros((8, 128), F32)
    for h, (mine, got) in enumerate(((a0, b0), (a1, b1))):
        take = lambda start, count: rows_at(mine, got, bit_of(place, h), start, count).astype(F32)
        wide = lambda start, rows: jnp.concatenate([take(start + c * rows, rows) for c in range(6)], axis=1)
        down_one[h] = wide(0, INNER)
        gate_two[h] = wide(6 * INNER, INNER).reshape(48, 4, D)
        up_two[h] = wide(12 * INNER, INNER).reshape(48, 4, D)
        ones = wide(GLU_ONE, 96)
        for k in range(4):
            gate_one[k, h] = ones[:48, k * INNER : (k + 1) * INNER]
            up_one[k, h] = ones[48:, k * INNER : (k + 1) * INNER]
        for i in range(2):
            two = jnp.concatenate([take(GLU_TWO + 48 * (3 * i + c), 48) for c in range(3)], axis=1)
            for m in range(2):
                down_two[2 * i + m, :, h, :] = two[:, m * INNER : (m + 1) * INNER]


def unpack_glu(place, parts, after=()):
    outs = [
        ((2, INNER, D), F32), ((2, 48, 4, D), F32), ((2, 48, 4, D), F32), ((4, 2, 48, INNER), F32), ((4, 2, 48, INNER), F32),
        ((4, 48, 2, INNER), F32), ((8, 128), F32),
    ]
    return call(unpack_glu_kernel, "unpack_feed_forward", outs, [], 24, 0.1, place, *parts, after=after)


def unpack_mixer_kernel(place, mp, a0, b0, a1, b1, mixout_one, mixout_two, mixin_one, mixin_two, *refs):
    vecs, (taps, pos_in, pos_bias, pos_out) = refs[:5], refs[5:]
    size = MIX_ROWS // 2

    def take(start, count):
        out, at = [], start
        while at < start + count:
            g = at // size
            n = min(start + count, (g + 1) * size) - at
            mine, got = ((a0, b0), (a1, b1))[g]
            out.append(rows_at(mine, got, bit_of(place, g), at - g * size, n).astype(F32))
            at += n
        return out[0] if len(out) == 1 else jnp.concatenate(out, axis=0)

    wide = lambda start, rows, n: jnp.concatenate([take(start + c * rows, rows) for c in range(n)], axis=1)
    for base, one, two, e in ((0, mixout_one, mixout_two, INNER), (MIX_IN, mixin_one, mixin_two, 576)):
        ones = wide(base, INNER, 3)
        twos = wide(base + 3 * INNER, INNER, 2 * e // 128)
        for i in range(2):
            one[i] = ones[:, i * INNER : (i + 1) * INNER]
            two[i] = twos[:, i * e : (i + 1) * e].reshape(48, 4, e)
    small = take(MIX_SMALL, 48)
    for i in range(5):
        vecs[i][...] = jnp.concatenate([small[3 * i + c : 3 * i + c + 1] for c in range(3)], axis=1).reshape(384)
    for i in range(3):
        taps[i : i + 1] = jnp.concatenate([small[15 + 9 * i + c : 16 + 9 * i + c] for c in range(9)], axis=1)
    pos = take(MIX_POS, 16)
    pos = jnp.where(mp[0] == 0, pos[:8], pltpu.roll(pos[:8], 64, 1))[:, :64]
    pos_in[...] = pos[:5]
    pos_bias[...] = pos[7:8].reshape(64)
    pos_out[...] = wide(MIX_OUT, 128, 3)


def unpack_mixer(place, mp, parts, after):
    outs = [
        ((2, INNER, INNER), F32), ((2, 48, 4, INNER), F32), ((2, INNER, INNER), F32), ((2, 48, 4, 576), F32),
        *[((384,), F32)] * 5, ((3, 1152), F32), ((5, 64), F32), ((64,), F32), ((128, 384), F32),
    ]
    return call(unpack_mixer_kernel, "unpack_mixer", outs, [], 24, 3, place, mp, *parts, after=after)


def local(
    tokens, short_lengths, long_lengths, cotangent, norm1_gain, norm1_bias, mixin_one, mixin_two, conv_taps, skip_gain,
    pos_in, pos_bias, pos_out, mixout_one, mixout_two, norm2_gain, norm2_bias, gate_one, gate_two, up_one, up_two,
    down_one, down_two,
):
    mp_index = lax.axis_index("mp")
    dp_index = lax.axis_index("dp")
    total_bits = (lax.axis_size("dp") - 1).bit_length()
    mp = mp_index.astype(jnp.int32).reshape(1)
    place = dp_index.astype(jnp.int32).reshape(1)
    const = tables()
    rows_first = lambda w: w.transpose(0, 2, 3, 1).reshape(w.shape[0], -1, w.shape[1])
    glu_own = (rows_first(gate_one), gate_two, rows_first(up_one), up_two, rows_first(down_one), down_two)
    glu_other = tuple(swap_pair(w) for w in glu_own)

    vecs, taps = small_params(norm1_gain, norm1_bias, norm2_gain, norm2_bias, skip_gain, conv_taps)
    mixed, sect_in = mixin_forward(
        short_lengths, long_lengths, tokens, vecs, rows_first(mixin_one), mixin_two, (mp, place)
    )
    sin_h, cos_h, kr, ks = make_filter(const, pos_in, pos_bias.reshape(1, -1), pos_out, (mixed,))
    gated, spread, xr, xs, parts, mixed_saved = conv_forward(const, mixed, taps, vecs, kr, ks)
    middle, normed_two, sect_out, w1p_out, w2p_out = mixout_forward(
        tokens, gated, vecs, rows_first(mixout_one), mixout_two, glu_other
    )

    *sects, g1p, u1p, d2p = glu_sections(normed_two, cotangent, glu_own, glu_other)
    glu_parts = []

    def block(i, after=()):
        weights = glu_own if i % 2 else glu_other
        *parts, grads = glu_block(i // 2, normed_two, cotangent, sects[i::4], weights, after)
        glu_parts.append(parts)
        return grads

    other = block(0)
    own = block(1)
    ((send, keep_a),) = split(place, (0,), [(own, swap_pair(other))])
    got_a = swap_bit(send, 0)
    other = block(2, (keep_a,))
    own = block(3)
    ((send, keep_b),) = split(place, (1,), [(own, swap_pair(other))])
    rest = tuple(range(3, total_bits))
    glu_sum = Joint(place, keep_a, got_a, keep_b, swap_bit(send, 1), rest)
    grad_middle, grad_gated, mixout_grads, norm2_small = middle_back(
        mp, middle, cotangent, gated, sect_out, vecs, w1p_out, w2p_out,
        [parts[i] for i in (1, 2) for parts in glu_parts] + [g1p, u1p], (keep_b,),
    )
    saved = (mixed_saved, parts, xr, xs, spread)
    result, last = make_result(middle, [v[0] for v in glu_parts], d2p, (norm2_small,))
    grads, smalls, outs, hidden = [], [], [], []
    for c in range(D // CHUNK):
        g, small, pos_o, hid = conv_back(
            c, const, short_lengths, long_lengths, saved, taps, vecs, kr, ks, grad_gated, sin_h, cos_h, pos_out,
            hidden if c == D // CHUNK - 1 else [], (glu_sum.step(last),),
        )
        last = small
        grads.append(g)
        smalls.append(small)
        outs.append(pos_o)
        hidden.append(hid)
    grad_normed, norm1_small, normed, grad_sect = mixin_back(
        tokens, grads, vecs, rows_first(mixin_one), mixin_two, (glu_sum.step(last),)
    )
    extra = (mixout_grads, norm1_small, norm2_small, *smalls, *outs, hidden[-1])
    other = mixin_grads(False, mp, grads, sect_in, normed, grad_sect, extra, ())
    own = mixin_grads(True, mp, grads, sect_in, normed, grad_sect, extra, (other,))
    got = swap_pair(other)
    size = MIX_ROWS // 2
    (send_a, keep_a), (send_b, keep_b) = split(place, (0, 1), [(own[:size], got[:size]), (own[size:], got[size:])])
    mix_sum = Joint(place, keep_a, swap_bit(send_a, 0), keep_b, swap_bit(send_b, 1), rest)
    tokens_grad, token = make_tokens_grad(tokens, grad_normed, grad_middle, vecs, (keep_b,))
    for which in (mix_sum, mix_sum, glu_sum, mix_sum, mix_sum, glu_sum):
        token = which.step(token)
    for which in (glu_sum, mix_sum):
        while which.halves is None:
            token = which.step(token)
    down_one_g, gate_two_g, up_two_g, gate_one_g, up_one_g, down_two_g, mark = unpack_glu(place, glu_sum.halves, (token,))
    mixout_one_g, mixout_two_g, mixin_one_g, mixin_two_g, *vecs_g, taps_g, pos_in_g, pos_bias_g, pos_out_g = unpack_mixer(
        place, mp, mix_sum.halves, (mark,)
    )

    natural = lambda v: v.transpose(0, 3, 1, 2)
    one = lambda v: natural(v.reshape(2, 4, 48, INNER))
    return (
        result, tokens_grad, vecs_g[0], vecs_g[1], one(mixin_one_g), mixin_two_g, taps_g, vecs_g[4], pos_in_g, pos_bias_g,
        pos_out_g, one(mixout_one_g), mixout_two_g, vecs_g[2], vecs_g[3], natural(gate_one_g), gate_two_g, natural(up_one_g),
        up_two_g, natural(down_one_g.reshape(2, 4, 48, D)), down_two_g,
    )


def solution(mesh):
    return jax.shard_map(
        local,
        mesh=mesh,
        in_specs=(
            P(("dp", "mp"), None),
            P(("dp", "mp")),
            P(("dp", "mp")),
            P(("dp", "mp"), None),
            *[P()] * 13,
            P(None, None, "mp", None),
            P("mp", None, None, None),
            P(None, None, "mp", None),
            P("mp", None, None, None),
            P("mp", None, None, None),
            P(None, None, "mp", None),
        ),
        out_specs=(
            P(("dp", "mp"), None),
            P(("dp", "mp"), None),
            P("mp"),
            P("mp"),
            P("mp", None, None, None),
            P("mp", None, None, None),
            P(None, "mp"),
            P("mp"),
            P(None, "mp"),
            P("mp"),
            P(None, "mp"),
            P("mp", None, None, None),
            P("mp", None, None, None),
            P("mp"),
            P("mp"),
            P(None, None, "mp", None),
            P("mp", None, None, None),
            P(None, None, "mp", None),
            P("mp", None, None, None),
            P("mp", None, None, None),
            P(None, None, "mp", None),
        ),
        check_vma=False,
    )
```

```python
import functools
import math

import jax
import jax.numpy as jnp
import numpy as np
from jax import lax
from jax.experimental import pallas as pl
from jax.experimental.pallas import tpu as pltpu
from jax.sharding import PartitionSpec as P

BF, F32 = jnp.bfloat16, jnp.float32
SHORT, LONG = 128, 1024
ROWS = SHORT + LONG
D = 768
INNER = 192
EPS = 1e-05
SLOWEST = math.log(100.0) / 1.5
FASTEST = math.log(100.0) / 0.3
TILE = 384
CHUNK = 256
MIB = 1024 * 1024
GLU_ONE, GLU_TWO, GLU_ROWS = 18 * INNER, 21 * INNER, 4352
MIX_IN, MIX_SMALL, MIX_POS, MIX_OUT, MIX_ROWS = 6 * INNER, 18 * INNER, 18 * INNER + 48, 18 * INNER + 64, 4096


def nn(a, b):
    return jnp.dot(a, b, preferred_element_type=F32)


def tn(a, b):
    return lax.dot_general(a, b, (((0,), (0,)), ((), ())), preferred_element_type=F32)


def nt(a, b):
    return lax.dot_general(a, b, (((1,), (1,)), ((), ())), preferred_element_type=F32)


def iota(shape, dim):
    return lax.broadcasted_iota(jnp.int32, shape, dim)


def block_of(index, width, count):
    out = jnp.zeros_like(index)
    for i in range(1, count):
        out = out + (index >= width * i).astype(jnp.int32)
    return out


def ones_where(cond):
    return jnp.where(cond, 1.0, 0.0).astype(BF)


def window_starts(e):
    return [2 * e * (m // 2) + (e // 128 * 128) * (m % 2) for m in range(4)]


def select_rows():
    row, col = iota((256, INNER), 0), iota((256, INNER), 1)
    a, q = row >> 6, row & 63
    return ones_where((col == q * 4 + a) & (q < 48))


def pad_sections(pieces):
    zeros = jnp.zeros((16, pieces[0].shape[1]), pieces[0].dtype)
    return jnp.concatenate([v for p in pieces for v in (p, zeros)], axis=0)


def pad_window(v, k):
    zeros = jnp.zeros((v.shape[0], 64), v.dtype)
    return jnp.concatenate([zeros, v] if k % 2 else [v, zeros], axis=1)


def mixer_weights(w1, w2, w1p, w2p, e):
    for i in range(4):
        w1p[i] = pad_window(pad_sections([w1[i, 48 * m : 48 * m + 48] for m in range(4)]), i)
        w2p[i] = pad_window(nn(select_rows(), w2[i].reshape(INNER, e)).astype(BF), i)


def exchange(blocks):
    blocks = [b.astype(BF) for b in blocks]
    return [jnp.concatenate([b[:, 64 * m : 64 * m + 64] for b in blocks], axis=1) for m in range(4)]


def join(windows):
    out = []
    for a, b in (windows[:2], windows[2:]):
        n = a.shape[1] - 128
        out += [a[:, :n], a[:, n:] + b[:, :128], b[:, 128:]]
    return jnp.concatenate(out, axis=1)


def sections(x, w1p):
    return exchange([nt(x[:, s : s + 256], w1p[k]) for k, s in enumerate(window_starts(INNER))])


def pair_columns(a, b):
    n = a.shape[1] - 128
    lane = iota((a.shape[0], 128), 1)
    return jnp.concatenate([a[:, :n], jnp.where(lane < 64, a[:, n:], b[:, :128]), b[:, 128:]], axis=1)


def block_grads(width, left, right):
    full = tn(left, right)
    if width == 48:
        return jnp.concatenate([full[64 * m : 64 * m + 48] for m in range(4)], axis=0)
    return tn(select_rows(), full.astype(BF))


def norm_parts(x):
    centred = x - jnp.mean(x, axis=-1, keepdims=True)
    rstd = lax.rsqrt(jnp.mean(centred * centred, axis=-1, keepdims=True) + EPS)
    return centred * rstd, rstd


def norm_back(grad, xhat, rstd, gain):
    scaled = grad * gain
    first = jnp.mean(scaled, axis=-1, keepdims=True)
    second = jnp.mean(scaled * xhat, axis=-1, keepdims=True)
    return rstd * (scaled - first - xhat * second)


LIMITS = {"mixer_input": 20, "filters": 14, "conv_forward": 22, "mixer_output": 12, "feed_forward": 18, "feed_forward_sections": 12, "middle_back": 22, "conv_back": 21, "mixer_input_back": 18, "mixer_input_grads": 14, "result": 10, "tokens_grad": 10}
WHOLE, PINNED, FAR = "whole", "pinned", "far"


def by_rows(*shape):
    dim = len(shape) - 2
    block = shape[:dim] + (TILE,) + shape[dim + 1 :]
    return pl.BlockSpec(block, lambda i: (0,) * dim + (i, 0))


def by_columns(*shape):
    lead = len(shape) - 1
    return pl.BlockSpec(shape[:-1] + (CHUNK,), lambda i: (0,) * lead + (i,))


def call(kernel, name, outs, scratch, limit, us, *args, grid=None, aliases=None, after=()):
    inner = kernel
    count, skip = len(args), len(after)
    if skip:
        kernel = lambda *refs: inner(*refs[:count], *refs[count + skip :])
    in_specs, operands, out_specs, out_shape = [], [], [], []
    for arg in args:
        arg, mode = arg if isinstance(arg, tuple) else (arg, WHOLE)
        if arg.dtype == jnp.int32:
            in_specs.append(pl.BlockSpec(memory_space=pltpu.SMEM))
        elif mode == FAR:
            arg = pltpu.with_memory_space_constraint(arg, pltpu.HBM)
            in_specs.append(pl.BlockSpec(memory_space=pl.ANY))
        elif isinstance(mode, pl.BlockSpec):
            arg = pltpu.with_memory_space_constraint(arg, pltpu.HBM)
            in_specs.append(mode)
        else:
            if mode == PINNED:
                arg = pltpu.with_memory_space_constraint(arg, pltpu.VMEM)
            in_specs.append(pl.BlockSpec(memory_space=pltpu.VMEM))
        operands.append(arg)
    for arg in after:
        in_specs.append(pl.BlockSpec(memory_space=pl.ANY))
        operands.append(arg)
    for shape, dtype, *mode in outs:
        mode = mode[0] if mode else WHOLE
        if mode == FAR or isinstance(mode, pl.BlockSpec):
            out_specs.append(pl.BlockSpec(memory_space=pl.ANY) if mode == FAR else mode)
            out_shape.append(pltpu.HBM(shape, dtype))
        else:
            out_specs.append(pl.BlockSpec(memory_space=pltpu.VMEM))
            out_shape.append(pltpu.VMEM(shape, dtype) if mode == PINNED else jax.ShapeDtypeStruct(shape, dtype))
    return pl.pallas_call(
        kernel,
        out_shape=out_shape,
        in_specs=in_specs,
        out_specs=out_specs,
        grid=(grid,) if grid else (),
        scratch_shapes=[pltpu.VMEM(*v) if isinstance(v, tuple) else v for v in scratch],
        input_output_aliases=aliases or {},
        cost_estimate=pl.CostEstimate(flops=int(us * 1.0e9), bytes_accessed=0, transcendentals=0),
        compiler_params=pltpu.CompilerParams(vmem_limit_bytes=LIMITS.get(name, 6) * MIB),
        name=name,
    )(*operands)


TILES = [slice(start, start + TILE) for start in range(0, ROWS, TILE)]
CHUNKS = [slice(start, start + CHUNK) for start in range(0, D, CHUNK)]
ROW_CUTS = [(rows,) for rows in TILES]
COLUMN_CUTS = [(Ellipsis, cols) for cols in CHUNKS]
SEMS = pltpu.SemaphoreType.DMA((3,))


def copies(source, target, sems, cuts):
    return [pltpu.make_async_copy(source.at[cut], target.at[cut], sems.at[i]) for i, cut in enumerate(cuts)]


def start_all(moves):
    for move in moves:
        move.start()
    return moves


def wait_all(*groups):
    for moves in groups:
        for move in moves:
            move.wait()


def first_step(body):
    pl.when(pl.program_id(0) == 0)(body)


def last_step(body):
    pl.when(pl.program_id(0) == pl.num_programs(0) - 1)(body)


def grid_part(size):
    start = pl.multiple_of(pl.program_id(0) * size, size)
    return pl.ds(start, size), start


def tables():
    def phases(n, f, t):
        whole = ((2 * f[:, None] + 1) * (2 * t[None, :] + 1)) % (8 * n)
        angle = whole.astype(np.float64) * (math.pi / (4 * n))
        return np.cos(angle), np.sin(angle)

    half = LONG // 2
    low = np.arange(half, dtype=np.int64)
    short = np.concatenate(phases(SHORT, np.arange(SHORT), np.arange(SHORT)), axis=1)
    parts = [np.concatenate(phases(LONG, low, 2 * low + odd), axis=0) for odd in (0, 1)]
    fraction = np.concatenate([np.arange(SHORT) / SHORT, np.arange(LONG) / LONG])
    order = np.concatenate([low, LONG - 1 - low])
    shift = np.concatenate(
        [(2 * f + 1) * (math.pi / (4 * n)) for f, n in ((np.arange(SHORT), SHORT), (order, LONG))]
    )
    aux = np.zeros((ROWS, 8), np.float32)
    aux[:, 0] = fraction
    for i, band in enumerate((1, 2)):
        aux[:, 1 + i] = np.cos(2.0 * math.pi * band * fraction)
        aux[:, 3 + i] = np.sin(2.0 * math.pi * band * fraction)
    aux[:, 5] = np.cos(shift)
    aux[:, 6] = np.sin(shift)
    aux[:, 7] = 1.0
    rates = SLOWEST + (FASTEST - SLOWEST) * np.arange(D) / (D - 1)
    low_type = lambda t: jnp.asarray(t.astype(np.float32), BF)
    return (
        (low_type(short), *[low_type(p) for p in parts], *[low_type(np.ascontiguousarray(p.T)) for p in parts]),
        jnp.asarray(aux),
        low_type(np.ascontiguousarray(aux.T)),
        jnp.asarray(rates[None].astype(np.float32)),
    )


def scale_rows(shape):
    return jnp.where(iota(shape, 0) < SHORT, 1.0 / SHORT, 1.0 / LONG)


def parity(odd):
    return pl.ds(odd, LONG // 2, stride=2)


LANES = [slice(i, i + 128) for i in range(0, CHUNK, 128)]


def transform(v, tabs, room):
    ts, fe, fo, _, _ = tabs
    head = v[:SHORT].astype(BF)
    for i, lanes in enumerate(LANES):
        room[i] = v[SHORT:, lanes]
    even, odd = [jnp.concatenate([room[i, parity(p)] for i in range(2)], axis=1).astype(BF) for p in (0, 1)]
    e, o = nn(fe[...], even), nn(fo[...], odd)
    h = LONG // 2
    real = jnp.concatenate([nn(ts[:, :SHORT], head), e[:h] + o[:h], e[h:] - o[h:]], axis=0)
    imag = jnp.concatenate([nn(ts[:, SHORT:], head), e[h:] + o[h:], e[:h] - o[:h]], axis=0)
    return real, imag


def restore(real, imag, tabs, room):
    ts, _, _, ie, io = tabs
    h = SHORT + LONG // 2
    head = nn(ts[...], jnp.concatenate([real[:SHORT], imag[:SHORT]], axis=0).astype(BF))
    r0, r1, i0, i1 = real[SHORT:h], real[h:], imag[SHORT:h], imag[h:]
    even = nn(ie[...], jnp.concatenate([r0 + i1, i0 + r1], axis=0).astype(BF))
    odd = nn(io[...], jnp.concatenate([r0 - i1, i0 - r1], axis=0).astype(BF))
    for i, lanes in enumerate(LANES):
        room[i, parity(0)] = even[:, lanes]
        room[i, parity(1)] = odd[:, lanes]
    return jnp.concatenate([head, jnp.concatenate([room[0], room[1]], axis=1)], axis=0)


ROOM = ((2, LONG, 128), F32)


def chunks(body):
    for c in range(D // CHUNK):
        body(slice(c * CHUNK, (c + 1) * CHUNK))


def tiles(body):
    for start in range(0, ROWS, TILE):
        body(slice(start, start + TILE), start)


def small_kernel(*refs):
    far, (vecs_o, taps_o), near, sems = refs[:6], refs[6:8], refs[8:14], refs[14]
    copies = [pltpu.make_async_copy(f, n, sems.at[i]) for i, (f, n) in enumerate(zip(far, near))]
    for copy in copies:
        copy.start()
    for copy in copies:
        copy.wait()
    vecs_o[...] = jnp.concatenate([v[...].reshape(1, D) for v in near[:5]] + [jnp.zeros((3, D), F32)], axis=0)
    taps = [near[5][i : i + 1, j * D : (j + 1) * D] for j in range(3) for i in range(3)]
    taps_o[...] = jnp.concatenate(taps + [jnp.zeros((7, D), F32)], axis=0)


def small_params(*args):
    return call(
        small_kernel, "small_parameters", [((8, D), F32), ((16, D), F32)],
        [((D,), F32)] * 5 + [((3, 3 * D), F32), pltpu.SemaphoreType.DMA((6,))], 8, 1, *[(v, FAR) for v in args],
    )


def sin_cos(x):
    turns = jnp.floor(x * (2.0 / math.pi) + 0.5)
    r = ((x - turns * 1.5703125) - turns * 4.837512969970703125e-4) - turns * 7.54978995489188216e-8
    z = r * r
    s = r + r * z * (-1.6666654611e-1 + z * (8.3321608736e-3 - 1.9515295891e-4 * z))
    c = 1.0 - 0.5 * z + z * z * (4.166664568298827e-2 + z * (-1.388731625493765e-3 + 2.443315711809948e-5 * z))
    quarter = turns.astype(jnp.int32) & 3
    odd = (quarter & 1) == 1
    sine = jnp.where(odd, c, s)
    cosine = jnp.where(odd, s, c)
    return jnp.where(quarter >= 2, -sine, sine), jnp.where((quarter == 1) | (quarter == 2), -cosine, cosine)


def filter_kernel(aux, pos_in, pos_bias, pos_out, rates, *refs):
    *tabs, sin_o, cos_o, kr_o, ks_o, room = refs
    pre = jnp.broadcast_to(pos_bias[...], (ROWS, 128))
    for i in range(5):
        pre = pre + aux[:, i : i + 1] * pos_in[i : i + 1, :]
    sin_o[...], cos_o[...] = sin_cos(pre)

    for c, cols in enumerate(CHUNKS):
        hidden = sin_o[...]
        high = hidden.astype(BF)
        low = (hidden - high.astype(F32)).astype(BF)
        w = pos_out[:, cols]
        w_high = w.astype(BF)
        w_low = (w - w_high.astype(F32)).astype(BF)
        shaped = nn(high, w_high) + nn(high, w_low) + nn(low, w_high)
        kern = shaped * jnp.exp(-aux[:, 0:1] * rates[:, cols])
        a, b = transform(kern, tabs, room.at[c])
        cos_h, sin_h = aux[:, 5:6], aux[:, 6:7]
        scale = scale_rows((ROWS, 1))
        kr_o[:, cols] = ((cos_h * a + sin_h * b) * scale).astype(BF)
        ks_o[:, cols] = ((cos_h * b - sin_h * a) * scale).astype(BF)


def make_filter(const, pos_in, pos_bias, pos_out, after):
    tabs, aux, _, rates = const
    return call(
        filter_kernel, "filters", [((ROWS, 128), F32, PINNED)] * 2 + [((ROWS, D), BF, PINNED)] * 2, [((3, *ROOM[0]), F32)], 10, 6,
        aux, pos_in, pos_bias, pos_out, rates, *tabs, after=after,
    )


def row_valid(short_len, long_len, start, rows):
    row = iota((rows, 1), 0) + start
    limit = jnp.where(row < SHORT, short_len[0], long_len[0] + SHORT)
    return row < limit


def mixin_kernel(
    short_len, long_len, tokens_h, vecs, w1, w2, mixed_o, sect_h, w1p, w2p, tokens, sect_s, in_sems, out_sems
):
    loads = start_all(copies(tokens_h, tokens, in_sems, ROW_CUTS))
    stores = copies(sect_s, sect_h, out_sems, ROW_CUTS)
    mixer_weights(w1, w2, w1p, w2p, 576)
    for i, rows in enumerate(TILES):
        loads[i].wait()
        xhat, _ = norm_parts(tokens[rows].astype(F32))
        normed = (xhat * vecs[0:1] + vecs[1:2]).astype(BF)
        sect = sections(normed, w1p)
        for m in range(4):
            sect_s[rows, m * 256 : (m + 1) * 256] = sect[m]
        stores[i].start()
        valid = row_valid(short_len, long_len, rows.start, TILE)
        full = jnp.where(valid, join([nn(sect[m], w2p[m]) for m in range(4)]), 0.0).astype(BF)
        for j in range(3):
            mixed_o[j, rows] = full[:, j * D : (j + 1) * D]
    wait_all(stores)


def mixin_forward(short_len, long_len, tokens, vecs, w1, w2, after):
    return call(
        mixin_kernel, "mixer_input", [((3, ROWS, D), BF, PINNED), ((ROWS, 1024), BF, FAR)],
        [((4, 256, 256), BF), ((4, 256, 640), BF), ((ROWS, D), BF), ((ROWS, 1024), BF), SEMS, SEMS], 22, 6,
        short_len, long_len, (tokens, FAR), vecs, w1, w2, after=after,
    )


def edges(shape):
    row = iota(shape, 0)
    first = (row == 0) | (row == SHORT)
    last = (row == SHORT - 1) | (row == ROWS - 1)
    return first, last


def before(v, first):
    return jnp.where(first, 0.0, pltpu.roll(v, 1, 0))


def after(v, last):
    return jnp.where(last, 0.0, pltpu.roll(v, ROWS - 1, 0))


def tap_rows(taps, cols, j):
    return [taps[3 * j + i : 3 * j + i + 1, cols] for i in range(3)]


def conv_forward_kernel(mixed, taps, vecs, kr, ks, *refs):
    tabs, gated_o, far, near, (mixed_h, room), sems = refs[:5], refs[5], refs[6:10], refs[11:15], (refs[10], refs[15]), refs[16]
    save = pltpu.make_async_copy(mixed, mixed_h, sems.at[4, 0])
    save.start()
    stores = [copies(v, f, sems.at[i], COLUMN_CUTS) for i, (v, f) in enumerate(zip(near, far))]
    spread_s, xr_s, xs_s, parts_s = near
    first, last = edges((ROWS, CHUNK))
    for c, cols in enumerate(CHUNKS):
        parts = []
        for j in range(3):
            m = mixed[j, :, cols].astype(F32)
            t0, t1, t2 = tap_rows(taps, cols, j)
            parts.append(t0 * before(m, first) + t1 * m + t2 * after(m, last))
            parts_s[j, :, cols] = parts[j].astype(BF)
        stores[3][c].start()
        product = parts[0] * parts[2]
        real, imag = transform(product, tabs, room.at[c])
        xr_s[:, cols] = real.astype(BF)
        xs_s[:, cols] = imag.astype(BF)
        stores[1][c].start()
        stores[2][c].start()
        a, b = kr[:, cols].astype(F32), ks[:, cols].astype(F32)
        spread = restore(real * a - imag * b, real * b + imag * a, tabs, room.at[c])
        spread = spread + vecs[4:5, cols] * product
        spread_s[:, cols] = spread.astype(BF)
        gated_o[:, cols] = (spread * parts[1]).astype(BF)
        stores[0][c].start()
    wait_all([save], *stores)


def conv_forward(const, mixed, taps, vecs, kr, ks):
    one, three = ((ROWS, D), BF), ((3, ROWS, D), BF)
    return call(
        conv_forward_kernel, "conv_forward",
        [(*one, PINNED), (*one, FAR), (*one, FAR), (*one, FAR), (*three, FAR), (*three, FAR)],
        [one, one, one, three, ((3, *ROOM[0]), F32), pltpu.SemaphoreType.DMA((5, 3))], 22, 9,
        (mixed, PINNED), taps, vecs, (kr, PINNED), (ks, PINNED), *const[0],
    )


def conv_back_kernel(
    c, short_len, long_len, mixed_h, parts_h, taps, vecs, kr, ks, xr_h, xs_h, spread_h, grad_gated, sin_h, cos_h, aux, features, pos_out,
    rates, *rest
):
    tabs = rest[:5]
    *earlier, grad_o, small_o, pos_out_o, hidden_o, mixed, parts, xr, xs, spread, sems, room = rest[5:]
    cols = slice(c * CHUNK, (c + 1) * CHUNK)
    moves = [(parts_h.at[1, :, cols], parts.at[1]), (xr_h.at[:, cols], xr), (xs_h.at[:, cols], xs)]
    moves += [(spread_h.at[:, cols], spread), (mixed_h.at[:, :, cols], mixed)]
    moves += [(parts_h.at[j, :, cols], parts.at[j]) for j in (0, 2)]
    loads = start_all([pltpu.make_async_copy(far, near, sems.at[i]) for i, (far, near) in enumerate(moves)])
    first, last = edges((ROWS, CHUNK))
    gg = grad_gated[:, cols].astype(F32)
    loads[0].wait()
    grad_spread = gg * parts[1].astype(F32)
    real, imag = transform(grad_spread, tabs, room)
    a, b = kr[:, cols].astype(F32), ks[:, cols].astype(F32)
    grad_product = restore(a * real + b * imag, a * imag - b * real, tabs, room)
    grad_product = grad_product + vecs[4:5, cols] * grad_spread
    wait_all(loads[1:3])
    x_real, x_imag = xr[...].astype(F32), xs[...].astype(F32)
    z_real = x_real * real + x_imag * imag
    z_imag = x_real * imag - x_imag * real
    cos_p, sin_p = aux[:, 5:6], aux[:, 6:7]
    grad_kernel = restore(cos_p * z_real - sin_p * z_imag, cos_p * z_imag + sin_p * z_real, tabs, room)
    shaped_grad = (grad_kernel * (scale_rows((ROWS, 1)) * jnp.exp(-aux[:, 0:1] * rates[:, cols]))).astype(BF)
    pos_out_o[...] = tn(sin_h[...].astype(BF), shaped_grad)
    hidden = nt(shaped_grad, pos_out[:, cols].astype(BF))
    wait_all(loads[3:])
    front = parts[0].astype(F32)
    value = parts[2].astype(F32)
    grads = (grad_product * value, gg * spread[...].astype(F32), grad_product * front)
    valid = row_valid(short_len, long_len, 0, ROWS)
    small = []
    for j in range(3):
        m = mixed[j].astype(F32)
        g = grads[j]
        up, down = after(g, last), before(g, first)
        t0, t1, t2 = tap_rows(taps, cols, j)
        small += [jnp.sum(v * m, axis=0, keepdims=True) for v in (up, g, down)]
        grad_o[j] = jnp.where(valid, t0 * up + t1 * g + t2 * down, 0.0).astype(BF)
    small.append(jnp.sum(grad_spread * front * value, axis=0, keepdims=True))
    small.append(jnp.zeros((6, CHUNK), F32))
    small_o[...] = jnp.concatenate(small, axis=0)
    if not earlier:
        hidden_o[...] = hidden
    else:
        pre = (hidden + earlier[0][...] + earlier[1][...]) * cos_h[...]
        hidden_o[...] = nn(features[...], pre.astype(BF))


def conv_back(c, const, short_len, long_len, saved, taps, vecs, kr, ks, grad_gated, sin_h, cos_h, pos_out, earlier, after):
    tabs, aux, features, rates = const
    mixed, parts, xr, xs, spread = saved
    final = len(earlier) > 0
    one = ((ROWS, CHUNK), BF)
    three = ((3, ROWS, CHUNK), BF)
    return call(
        functools.partial(conv_back_kernel, c), "conv_back",
        [(*three, PINNED), ((16, CHUNK), F32), ((128, CHUNK), F32)] + ([((8, 128), F32)] if final else [((ROWS, 128), F32, PINNED)]),
        [three, three, one, one, one, pltpu.SemaphoreType.DMA((7,)), ROOM], 30, 8,
        short_len, long_len, (mixed, FAR), (parts, FAR), taps, vecs, (kr, PINNED), (ks, PINNED), (xr, FAR), (xs, FAR),
        (spread, FAR), (grad_gated, PINNED), (sin_h, PINNED), (cos_h, PINNED), aux, features, pos_out, rates, *tabs,
        *[(v, PINNED) for v in earlier], after=after,
    )


def mixout_kernel(
    tokens_h, gated, vecs, w1, w2, middle_h, normed_o, sect_o, w1p, w2p, tokens, middle_s, in_sems, out_sems
):
    loads = start_all(copies(tokens_h, tokens, in_sems, ROW_CUTS))
    stores = copies(middle_s, middle_h, out_sems, ROW_CUTS)
    mixer_weights(w1, w2, w1p, w2p, INNER)
    for i, rows in enumerate(TILES):
        sect = sections(gated[rows], w1p)
        for m in range(4):
            sect_o[rows, m * 256 : (m + 1) * 256] = sect[m]
        loads[i].wait()
        middle = tokens[rows].astype(F32) + join([nn(sect[m], w2p[m]) for m in range(4)])
        middle_s[rows] = middle
        stores[i].start()
        xhat, _ = norm_parts(middle)
        normed_o[rows] = (xhat * vecs[2:3] + vecs[3:4]).astype(BF)
    wait_all(stores)


def mixout_forward(tokens, gated, vecs, w1, w2, after):
    return call(
        mixout_kernel, "mixer_output",
        [
            ((ROWS, D), F32, FAR), ((ROWS, D), BF, PINNED), ((ROWS, 1024), BF, PINNED), ((4, 256, 256), BF, PINNED),
            ((4, 256, 256), BF, PINNED),
        ],
        [((ROWS, D), BF), ((ROWS, D), F32), SEMS, SEMS], 18, 5, (tokens, FAR), (gated, PINNED), vecs, w1, w2, after=after,
    )


def select_pair():
    row, col = iota((256, INNER), 0), iota((256, INNER), 1)
    block, q = row >> 6, row & 63
    return ones_where((col == (block & 1) * 96 + q * 2 + (block >> 1)) & (q < 48))


def sections_kernel(normed, cot, g1, u1, d2, own_g1, own_u1, own_d2, *refs):
    gate_o, up_o, grad_o, (g1p, u1p, d2p) = refs[:4], refs[4:8], refs[8:12], refs[12:]

    for i in range(4):
        for out, pair in ((g1p, (g1, own_g1)), (u1p, (u1, own_u1))):
            out[i] = pad_window(pad_sections([w[i, 48 * h : 48 * h + 48] for h in range(2) for w in pair]), i)
        both = jnp.concatenate([w[i].reshape(96, INNER) for w in (d2, own_d2)], axis=0)
        d2p[i] = pad_window(nn(select_pair(), both).astype(BF), i)
    for rows in TILES:
        for x, weights, outs in ((normed, g1p, gate_o), (normed, u1p, up_o), (cot, d2p, grad_o)):
            for out, v in zip(outs, sections(x[rows], weights)):
                out[rows] = v


def glu_sections(normed, cot, own, other):
    return call(
        sections_kernel, "feed_forward_sections", [((ROWS, 256), BF, PINNED)] * 12 + [((4, 256, 256), BF, PINNED)] * 3, [], 8, 4,
        (normed, PINNED), cot, other[0], other[2], other[5], own[0], own[2], own[5],
    )


def glu_kernel(
    h, normed, cot, gate_sect, up_sect, grad_sect, g2, u2, d1, sect_o, gate_grad_o, up_grad_o, grads_o,
    g2p, u2p, d1p, hidden_s, gate_s, up_s
):
    g2p[...] = nn(select_rows(), g2[h].reshape(INNER, D)).astype(BF)
    u2p[...] = nn(select_rows(), u2[h].reshape(INNER, D)).astype(BF)
    d1p[...] = pad_sections([d1[h, 48 * m : 48 * m + 48] for m in range(4)])

    def body(rows, start):
        gate = nn(gate_sect[rows], g2p[...])
        up = nn(up_sect[rows], u2p[...])
        sig = jax.nn.sigmoid(gate)
        act = gate * sig
        hidden = (act * up).astype(BF)
        sect_o[rows] = nt(hidden, d1p[...]).astype(BF)
        grad_hidden = nn(grad_sect[rows], d1p[...])
        grad_gate = (grad_hidden * up * (sig * (1.0 + gate * (1.0 - sig)))).astype(BF)
        grad_up = (grad_hidden * act).astype(BF)
        gate_grad_o[rows] = nt(grad_gate, g2p[...]).astype(BF)
        up_grad_o[rows] = nt(grad_up, u2p[...]).astype(BF)
        hidden_s[rows] = hidden
        gate_s[rows] = grad_gate
        up_s[rows] = grad_up

    tiles(body)
    for i, (a, b, width) in enumerate(((grad_sect, hidden_s, 48), (gate_sect, gate_s, 4), (up_sect, up_s, 4))):
        term = block_grads(width, a[...], b[...])
        for c in range(6):
            start = (i * 6 + c) * INNER
            grads_o[start : start + INNER] = term[:, c * 128 : (c + 1) * 128].astype(BF)

    def diagonal(left, right):
        full = tn(left[...], right[...])
        pieces = [full[64 * k : 64 * k + 48, s : s + 256] for k, s in enumerate(window_starts(INNER))]
        return [pair_columns(*pieces[:2]), pair_columns(*pieces[2:])]

    for i, a in enumerate((gate_grad_o, up_grad_o)):
        one = jnp.concatenate(diagonal(a, normed), axis=1).astype(BF)
        for c in range(6):
            start = GLU_ONE + 96 * c + 48 * i
            grads_o[start : start + 48] = one[:, c * 128 : (c + 1) * 128]
    for i, two in enumerate(diagonal(sect_o, cot)):
        for c in range(3):
            start = GLU_TWO + 48 * (3 * i + c)
            grads_o[start : start + 48] = two[:, c * 128 : (c + 1) * 128].astype(BF)
    grads_o[GLU_TWO + 288 :] = jnp.zeros((32, 128), BF)


def glu_block(h, normed, cot, sects, weights, after=()):
    return call(
        functools.partial(glu_kernel, h), "feed_forward", [((ROWS, 256), BF, PINNED)] * 3 + [((GLU_ROWS, 128), BF)],
        [((256, D), BF)] * 3 + [((ROWS, D), BF)] * 3, 26, 9, (normed, PINNED), cot, *[(v, PINNED) for v in sects],
        weights[1], weights[3], weights[4], after=after,
    )


def column_sums(pair):
    rows = [jnp.sum(v, axis=0, keepdims=True) for v in pair]
    return jnp.concatenate(rows + [jnp.zeros((6, D), F32)], axis=0)


def slot_of(mp, half):
    return jnp.where(mp[0] == half, 0, 1)


def middle_back_kernel(mp, middle_h, cot, gated, sect, vecs, w1p, w2p, *refs):
    glu, (g1p, u1p), outs = [refs[i : i + 4] for i in (0, 4)], refs[8:10], refs[10:]
    (grad_middle_o, grad_gated_o, grads_o, small_o, branch_s, grad_sect_s, middle, in_sems) = outs
    loads = start_all(copies(middle_h, middle, in_sems, ROW_CUTS))
    starts = window_starts(INNER)
    small = jnp.zeros((8, D), F32)
    for i, rows in enumerate(TILES):
        gates, ups = [exchange([v[rows] for v in group]) for group in glu]
        grad = join([nn(gates[k], g1p[k]) + nn(ups[k], u1p[k]) for k in range(4)])
        loads[i].wait()
        mid = middle[rows]
        xhat, rstd = norm_parts(mid)
        small = small + column_sums((grad * xhat, grad))
        grad_middle = cot[rows].astype(F32) + norm_back(grad, xhat, rstd, vecs[2:3])
        grad_middle_o[rows] = grad_middle
        branch = grad_middle.astype(BF)
        branch_s[rows] = branch
        grad_sect = exchange([nt(branch[:, s : s + 256], w2p[m]) for m, s in enumerate(starts)])
        for k in range(4):
            grad_sect_s[rows, k * 256 : (k + 1) * 256] = grad_sect[k]
        grad_gated_o[rows] = join([nn(grad_sect[k], w1p[k]) for k in range(4)]).astype(BF)
    small_o[...] = small
    part = lambda i: slice(i * 256, (i + 1) * 256)
    for half in range(2):
        slot = slot_of(mp, half)
        pair = (2 * half, 2 * half + 1)
        one = pair_columns(*[block_grads(48, grad_sect_s[:, part(k)], gated[:, starts[k] : starts[k] + 256]) for k in pair])
        two = pair_columns(*[block_grads(4, sect[:, part(m)], branch_s[:, starts[m] : starts[m] + 256]) for m in pair])
        for i, v in enumerate((one, two)):
            for c in range(3):
                at = (3 * i + c) * INNER
                grads_o[slot, at : at + INNER] = v[:, c * 128 : (c + 1) * 128].astype(BF)


def result_kernel(middle_h, *refs):
    sects, (d2p, result_h, mark, middle, result_s, in_sems, out_sems) = refs[:4], refs[4:]
    mark[...] = jnp.zeros((8, 128), F32)
    loads = start_all(copies(middle_h, middle, in_sems, ROW_CUTS))
    stores = copies(result_s, result_h, out_sems, ROW_CUTS)
    for i, rows in enumerate(TILES):
        out = join([nn(v, d2p[m]) for m, v in enumerate(exchange([v[rows] for v in sects]))])
        loads[i].wait()
        result_s[rows] = (middle[rows] + out).astype(BF)
        stores[i].start()
    wait_all(stores)


def make_result(middle, sects, d2p, after):
    return call(
        result_kernel, "result", [((ROWS, D), BF, FAR), ((8, 128), F32)],
        [((ROWS, D), F32), ((ROWS, D), BF), SEMS, SEMS], 18, 1, (middle, FAR), *sects, d2p, after=after,
    )


def middle_back(mp, middle, cot, gated, sect, vecs, w1p, w2p, glu, after):
    return call(
        middle_back_kernel, "middle_back",
        [((ROWS, D), F32, PINNED), ((ROWS, D), BF, PINNED), ((2, 6 * INNER, 128), BF), ((8, D), F32)],
        [((ROWS, D), BF), ((ROWS, 1024), BF), ((ROWS, D), F32), SEMS], 26, 9,
        mp, (middle, FAR), cot, (gated, PINNED), (sect, PINNED), vecs, (w1p, PINNED), (w2p, PINNED),
        *[(v, PINNED) for v in glu], after=after,
    )


def mixed_window(grads, start, rows):
    out, width = [], 640
    while width:
        j, at = start // D, start % D
        c, at = at // CHUNK, at % CHUNK
        n = min(width, CHUNK - at)
        out.append(grads[c][j, rows, at : at + n])
        start, width = start + n, width - n
    return jnp.concatenate(out, axis=1)


def mixin_back_kernel(
    tokens_h, m0, m1, m2, vecs, w1, w2, grad_o, norm1, normed_o, grad_sect_o, w1p, w2p, tokens, in_sems
):
    loads = start_all(copies(tokens_h, tokens, in_sems, ROW_CUTS))
    mixer_weights(w1, w2, w1p, w2p, 576)
    small = jnp.zeros((8, D), F32)
    for i, rows in enumerate(TILES):
        windows = [mixed_window((m0, m1, m2), s, rows) for s in window_starts(576)]
        grad_sect = exchange([nt(v, w2p[m]) for m, v in enumerate(windows)])
        for k in range(4):
            grad_sect_o[rows, k * 256 : (k + 1) * 256] = grad_sect[k]
        grad = join([nn(grad_sect[k], w1p[k]) for k in range(4)])
        loads[i].wait()
        xhat, _ = norm_parts(tokens[rows].astype(F32))
        normed_o[rows] = (xhat * vecs[0:1] + vecs[1:2]).astype(BF)
        small = small + column_sums((grad * xhat, grad))
        grad_o[rows] = grad
    norm1[...] = small


def mixin_back(tokens, grads, vecs, w1, w2, after):
    return call(
        mixin_back_kernel, "mixer_input_back",
        [((ROWS, D), F32, PINNED), ((8, D), F32), ((ROWS, D), BF, PINNED), ((ROWS, 1024), BF, PINNED)],
        [((4, 256, 256), BF), ((4, 256, 640), BF), ((ROWS, D), BF), SEMS], 26, 7,
        (tokens, FAR), *[(g, PINNED) for g in grads], vecs, w1, w2, after=after,
    )


def tokens_kernel(tokens_h, grad, grad_middle, vecs, out_h, mark, tokens, out_s, in_sems, out_sems):
    mark[...] = jnp.zeros((8, 128), F32)
    loads = start_all(copies(tokens_h, tokens, in_sems, ROW_CUTS))
    stores = copies(out_s, out_h, out_sems, ROW_CUTS)
    for i, rows in enumerate(TILES):
        loads[i].wait()
        xhat, rstd = norm_parts(tokens[rows].astype(F32))
        out_s[rows] = (grad_middle[rows] + norm_back(grad[rows], xhat, rstd, vecs[0:1])).astype(BF)
        stores[i].start()
    wait_all(stores)


def make_tokens_grad(tokens, grad, grad_middle, vecs, after):
    return call(
        tokens_kernel, "tokens_grad", [((ROWS, D), BF, FAR), ((8, 128), F32)],
        [((ROWS, D), BF), ((ROWS, D), BF), SEMS, SEMS], 18, 1,
        (tokens, FAR), (grad, PINNED), (grad_middle, PINNED), vecs, after=after,
    )


def mixin_grads_kernel(
    own, mp, m0, m1, m2, sect_h, normed, grad_sect, mixout_grads, norm1, norm2, c0, c1, c2, p0, p1, p2, pos, out, sect, sem
):
    part = lambda i: slice(i * 256, (i + 1) * 256)

    def work(half):
        load = pltpu.make_async_copy(sect_h.at[:, half * 512 : half * 512 + 512], sect, sem.at[0])
        load.start()
        pair = (2 * half, 2 * half + 1)
        starts = window_starts(INNER)
        one = pair_columns(*[block_grads(48, grad_sect[:, part(k)], normed[:, starts[k] : starts[k] + 256]) for k in pair])
        load.wait()
        starts = window_starts(576)
        two = pair_columns(
            *[block_grads(4, sect[:, part(m % 2)], mixed_window((m0, m1, m2), starts[m], slice(None))) for m in pair]
        )
        for at, v in ((MIX_IN, one), (MIX_IN + 3 * INNER, two)):
            for c in range(v.shape[1] // 128):
                out[at + c * INNER : at + (c + 1) * INNER] = v[:, c * 128 : (c + 1) * 128].astype(BF)
        cut = lambda v, r, col: v[r : r + 1, col : col + 128]
        conv = lambda r, col: (c0, c1, c2)[col // CHUNK][r : r + 1, col % CHUNK : col % CHUNK + 128]
        small = []
        for v, r in ((norm1, 0), (norm1, 1), (norm2, 0), (norm2, 1)):
            small += [cut(v, r, half * 384 + 128 * i) for i in range(3)]
        small += [conv(9, half * 384 + 128 * i) for i in range(3)]
        for tap in range(3):
            for i in range(9):
                col = half * 1152 + 128 * i
                small.append(conv(3 * (col // D) + tap, col % D))
        small.append(jnp.zeros((6, 128), F32))
        out[MIX_SMALL : MIX_SMALL + 48] = jnp.concatenate(small, axis=0).astype(BF)
        for i in range(3):
            col = half * 384 + 128 * i
            at = MIX_OUT + 128 * i
            out[at : at + 128] = (p0, p1, p2)[col // CHUNK][:, col % CHUNK : col % CHUNK + 128].astype(BF)

    for half in range(2):
        pl.when(mp[0] == (half if own else 1 - half))(functools.partial(work, half))
    out[:MIX_IN] = mixout_grads[0 if own else 1]
    out[MIX_POS : MIX_POS + 16] = jnp.concatenate([pos[...], jnp.zeros((8, 128), F32)], axis=0).astype(BF)
    out[MIX_OUT + 384 :] = jnp.zeros((MIX_ROWS - MIX_OUT - 384, 128), BF)


def mixin_grads(own, mp, grads, sect, normed, grad_sect, extra, after):
    return call(
        functools.partial(mixin_grads_kernel, own), "mixer_input_grads", [((MIX_ROWS, 128), BF)],
        [((ROWS, 512), BF), pltpu.SemaphoreType.DMA((1,))], 20, 0.5, mp, *[(g, PINNED) for g in grads],
        (sect, FAR), (normed, PINNED), (grad_sect, PINNED), *extra, after=after,
    )[0]


def swap_pair(v):
    n = lax.axis_size("mp")
    return lax.ppermute(v, "mp", [(i, (i + 1) % n) for i in range(n)])


def swap_bit(v, bit):
    n = lax.axis_size("dp")
    return lax.ppermute(v, "dp", [(i, i ^ (1 << bit)) for i in range(n)])


def sum_of(a, b):
    return (a.astype(F32) + b.astype(F32)).astype(BF)


def bit_of(place, bit):
    return (place[0] >> bit) & 1


def part_of(ref, bit, half):
    return ref[pl.ds(pl.multiple_of(bit * half, 16), half)]


def split_kernel(bits, place, *refs):
    n = len(bits)
    for i in range(n):
        keep, got = refs[2 * i], refs[2 * i + 1]
        send_o, keep_o = refs[2 * n + 2 * i], refs[2 * n + 2 * i + 1]
        half, bit = send_o.shape[0], bit_of(place, bits[i])
        send_o[...] = sum_of(part_of(keep, 1 - bit, half), part_of(got, 1 - bit, half))
        keep_o[...] = sum_of(part_of(keep, bit, half), part_of(got, bit, half))


def split(place, bits, pairs, after=()):
    outs = [((p[0].shape[0] // 2, 128), BF) for p in pairs for _ in range(2)]
    flat = [v for p in pairs for v in p]
    got = call(functools.partial(split_kernel, bits), "split", outs, [], 8, 0.1, place, *flat, after=after)
    return [(got[2 * i], got[2 * i + 1]) for i in range(len(pairs))]


def sum_kernel(mine, got, out):
    out[...] = sum_of(mine[...], got[...])


def total(mine, got, after=()):
    return call(sum_kernel, "sum", [(mine.shape, BF)], [], 8, 0.1, mine, got, after=after)[0]


def merge_kernel(bits, place, *refs):
    n = len(bits)
    for i in range(n):
        mine, got, out = refs[2 * i], refs[2 * i + 1], refs[2 * n + i]
        half, bit = mine.shape[0], bit_of(place, bits[i])
        out[pl.ds(pl.multiple_of(bit * half, 16), half)] = mine[...]
        out[pl.ds(pl.multiple_of((1 - bit) * half, 16), half)] = got[...]


def merge(place, bits, pairs, after=()):
    outs = [((2 * p[0].shape[0], 128), BF) for p in pairs]
    flat = [v for p in pairs for v in p]
    return call(functools.partial(merge_kernel, bits), "merge", outs, [], 8, 0.1, place, *flat, after=after)


def second_kernel(place, ka, ra, kb, rb, send_a, send_b, keep):
    for i, (mine, got, send, bit) in enumerate(((ka, ra, send_a, bit_of(place, 1)), (kb, rb, send_b, bit_of(place, 0)))):
        half = send.shape[0]
        send[...] = sum_of(part_of(mine, 1 - bit, half), part_of(got, 1 - bit, half))
        keep[i * half : (i + 1) * half] = sum_of(part_of(mine, bit, half), part_of(got, bit, half))


def third_kernel(place, keep, ra, rb, send_o, keep_o):
    size = ra.shape[0]
    half, bit = size // 2, bit_of(place, 2)
    for i, got in enumerate((ra, rb)):
        base = i * size
        for out, b in ((send_o, 1 - bit), (keep_o, bit)):
            rows = pl.ds(pl.multiple_of(base + b * half, 16), half)
            out[i * half : (i + 1) * half] = sum_of(keep[rows], part_of(got, b, half))


def fifth_kernel(place, mine, got, a, b):
    half, bit = mine.shape[0] // 2, bit_of(place, 2)
    for i, out in enumerate((a, b)):
        rows = slice(i * half, (i + 1) * half)
        out[pl.ds(pl.multiple_of(bit * half, 16), half)] = mine[rows]
        out[pl.ds(pl.multiple_of((1 - bit) * half, 16), half)] = got[rows]


def joint_steps(place, ka, ra, kb, rb, rest):
    rows = lambda n: ((n, 128), BF)
    size = ka.shape[0]
    after = yield None
    sa, sb, keep = call(
        second_kernel, "second_split", [rows(size // 2)] * 2 + [rows(size)], [], 8, 0.1, place, ka, ra, kb, rb, after=after
    )
    ra, rb = swap_bit(sa, 1), swap_bit(sb, 0)
    after = yield keep, (ra, rb), None
    send, keep = call(third_kernel, "third_split", [rows(size // 2)] * 2, [], 8, 0.1, place, keep, ra, rb, after=after)
    got = swap_bit(send, 2)
    after = yield keep, (got,), None
    out = total(keep, got, after)
    for bit in rest:
        got = swap_bit(out, bit)
        after = yield out, (got,), None
        out = total(out, got, after)
    got = swap_bit(out, 2)
    after = yield out, (got,), None
    a, b = call(fifth_kernel, "first_merge", [rows(size // 2)] * 2, [], 8, 0.1, place, out, got, after=after)
    ra, rb = swap_bit(a, 1), swap_bit(b, 0)
    after = yield a, (ra, rb), None
    a, b = merge(place, (1, 0), [(a, ra), (b, rb)], after)
    ra, rb = swap_bit(a, 0), swap_bit(b, 1)
    yield a, (ra, rb), (a, ra, b, rb)


class Joint:
    def __init__(self, *args):
        self.run = joint_steps(*args)
        next(self.run)
        self.halves = None

    def step(self, *after):
        token, self.coming, self.halves = self.run.send(after)
        return token


def rows_at(mine, got, bit, start, count):
    half = mine.shape[0]
    out, at = [], start
    while at < start + count:
        n = min(count - (at - start), half - at % half)
        local, lower = at % half, at < half
        a, b = mine[local : local + n], got[local : local + n]
        first = bit == 0 if lower else bit == 1
        out.append(jnp.where(first, a, b))
        at += n
    return out[0] if len(out) == 1 else jnp.concatenate(out, axis=0)


def unpack_glu_kernel(place, a0, b0, a1, b1, down_one, gate_two, up_two, gate_one, up_one, down_two, mark):
    mark[...] = jnp.zeros((8, 128), F32)
    for h, (mine, got) in enumerate(((a0, b0), (a1, b1))):
        take = lambda start, count: rows_at(mine, got, bit_of(place, h), start, count).astype(F32)
        wide = lambda start, rows: jnp.concatenate([take(start + c * rows, rows) for c in range(6)], axis=1)
        down_one[h] = wide(0, INNER)
        gate_two[h] = wide(6 * INNER, INNER).reshape(48, 4, D)
        up_two[h] = wide(12 * INNER, INNER).reshape(48, 4, D)
        ones = wide(GLU_ONE, 96)
        for k in range(4):
            gate_one[k, h] = ones[:48, k * INNER : (k + 1) * INNER]
            up_one[k, h] = ones[48:, k * INNER : (k + 1) * INNER]
        for i in range(2):
            two = jnp.concatenate([take(GLU_TWO + 48 * (3 * i + c), 48) for c in range(3)], axis=1)
            for m in range(2):
                down_two[2 * i + m, :, h, :] = two[:, m * INNER : (m + 1) * INNER]


def unpack_glu(place, parts, after=()):
    outs = [
        ((2, INNER, D), F32), ((2, 48, 4, D), F32), ((2, 48, 4, D), F32), ((4, 2, 48, INNER), F32), ((4, 2, 48, INNER), F32),
        ((4, 48, 2, INNER), F32), ((8, 128), F32),
    ]
    return call(unpack_glu_kernel, "unpack_feed_forward", outs, [], 24, 0.1, place, *parts, after=after)


def unpack_mixer_kernel(place, mp, a0, b0, a1, b1, mixout_one, mixout_two, mixin_one, mixin_two, *refs):
    vecs, (taps, pos_in, pos_bias, pos_out) = refs[:5], refs[5:]
    size = MIX_ROWS // 2

    def take(start, count):
        out, at = [], start
        while at < start + count:
            g = at // size
            n = min(start + count, (g + 1) * size) - at
            mine, got = ((a0, b0), (a1, b1))[g]
            out.append(rows_at(mine, got, bit_of(place, g), at - g * size, n).astype(F32))
            at += n
        return out[0] if len(out) == 1 else jnp.concatenate(out, axis=0)

    wide = lambda start, rows, n: jnp.concatenate([take(start + c * rows, rows) for c in range(n)], axis=1)
    for base, one, two, e in ((0, mixout_one, mixout_two, INNER), (MIX_IN, mixin_one, mixin_two, 576)):
        ones = wide(base, INNER, 3)
        twos = wide(base + 3 * INNER, INNER, 2 * e // 128)
        for i in range(2):
            one[i] = ones[:, i * INNER : (i + 1) * INNER]
            two[i] = twos[:, i * e : (i + 1) * e].reshape(48, 4, e)
    small = take(MIX_SMALL, 48)
    for i in range(5):
        vecs[i][...] = jnp.concatenate([small[3 * i + c : 3 * i + c + 1] for c in range(3)], axis=1).reshape(384)
    for i in range(3):
        taps[i : i + 1] = jnp.concatenate([small[15 + 9 * i + c : 16 + 9 * i + c] for c in range(9)], axis=1)
    pos = take(MIX_POS, 16)
    pos = jnp.where(mp[0] == 0, pos[:8], pltpu.roll(pos[:8], 64, 1))[:, :64]
    pos_in[...] = pos[:5]
    pos_bias[...] = pos[7:8].reshape(64)
    pos_out[...] = wide(MIX_OUT, 128, 3)


def unpack_mixer(place, mp, parts, after):
    outs = [
        ((2, INNER, INNER), F32), ((2, 48, 4, INNER), F32), ((2, INNER, INNER), F32), ((2, 48, 4, 576), F32),
        *[((384,), F32)] * 5, ((3, 1152), F32), ((5, 64), F32), ((64,), F32), ((128, 384), F32),
    ]
    return call(unpack_mixer_kernel, "unpack_mixer", outs, [], 24, 3, place, mp, *parts, after=after)


def local(
    tokens, short_lengths, long_lengths, cotangent, norm1_gain, norm1_bias, mixin_one, mixin_two, conv_taps, skip_gain,
    pos_in, pos_bias, pos_out, mixout_one, mixout_two, norm2_gain, norm2_bias, gate_one, gate_two, up_one, up_two,
    down_one, down_two,
):
    mp_index = lax.axis_index("mp")
    dp_index = lax.axis_index("dp")
    total_bits = (lax.axis_size("dp") - 1).bit_length()
    mp = mp_index.astype(jnp.int32).reshape(1)
    place = dp_index.astype(jnp.int32).reshape(1)
    const = tables()
    rows_first = lambda w: w.transpose(0, 2, 3, 1).reshape(w.shape[0], -1, w.shape[1])
    glu_own = (rows_first(gate_one), gate_two, rows_first(up_one), up_two, rows_first(down_one), down_two)
    glu_other = tuple(swap_pair(w) for w in glu_own)

    vecs, taps = small_params(norm1_gain, norm1_bias, norm2_gain, norm2_bias, skip_gain, conv_taps)
    mixed, sect_in = mixin_forward(
        short_lengths, long_lengths, tokens, vecs, rows_first(mixin_one), mixin_two, (mp, place)
    )
    sin_h, cos_h, kr, ks = make_filter(const, pos_in, pos_bias.reshape(1, -1), pos_out, (mixed,))
    gated, spread, xr, xs, parts, mixed_saved = conv_forward(const, mixed, taps, vecs, kr, ks)
    middle, normed_two, sect_out, w1p_out, w2p_out = mixout_forward(
        tokens, gated, vecs, rows_first(mixout_one), mixout_two, glu_other
    )

    *sects, g1p, u1p, d2p = glu_sections(normed_two, cotangent, glu_own, glu_other)
    glu_parts = []

    def block(i, after=()):
        weights = glu_own if i % 2 else glu_other
        *parts, grads = glu_block(i // 2, normed_two, cotangent, sects[i::4], weights, after)
        glu_parts.append(parts)
        return grads

    other = block(0)
    own = block(1)
    ((send, keep_a),) = split(place, (0,), [(own, swap_pair(other))])
    got_a = swap_bit(send, 0)
    other = block(2, (keep_a,))
    own = block(3)
    ((send, keep_b),) = split(place, (1,), [(own, swap_pair(other))])
    rest = tuple(range(3, total_bits))
    glu_sum = Joint(place, keep_a, got_a, keep_b, swap_bit(send, 1), rest)
    grad_middle, grad_gated, mixout_grads, norm2_small = middle_back(
        mp, middle, cotangent, gated, sect_out, vecs, w1p_out, w2p_out,
        [parts[i] for i in (1, 2) for parts in glu_parts] + [g1p, u1p], (keep_b,),
    )
    saved = (mixed_saved, parts, xr, xs, spread)
    result, last = make_result(middle, [v[0] for v in glu_parts], d2p, (norm2_small,))
    grads, smalls, outs, hidden = [], [], [], []
    for c in range(D // CHUNK):
        g, small, pos_o, hid = conv_back(
            c, const, short_lengths, long_lengths, saved, taps, vecs, kr, ks, grad_gated, sin_h, cos_h, pos_out,
            hidden if c == D // CHUNK - 1 else [], (glu_sum.step(last),),
        )
        last = small
        grads.append(g)
        smalls.append(small)
        outs.append(pos_o)
        hidden.append(hid)
    grad_normed, norm1_small, normed, grad_sect = mixin_back(
        tokens, grads, vecs, rows_first(mixin_one), mixin_two, (glu_sum.step(last),)
    )
    extra = (mixout_grads, norm1_small, norm2_small, *smalls, *outs, hidden[-1])
    other = mixin_grads(False, mp, grads, sect_in, normed, grad_sect, extra, ())
    own = mixin_grads(True, mp, grads, sect_in, normed, grad_sect, extra, (other,))
    got = swap_pair(other)
    size = MIX_ROWS // 2
    (send_a, keep_a), (send_b, keep_b) = split(place, (0, 1), [(own[:size], got[:size]), (own[size:], got[size:])])
    mix_sum = Joint(place, keep_a, swap_bit(send_a, 0), keep_b, swap_bit(send_b, 1), rest)
    tokens_grad, token = make_tokens_grad(tokens, grad_normed, grad_middle, vecs, (keep_b,))
    for which in (mix_sum, mix_sum, glu_sum, mix_sum, glu_sum, mix_sum):
        token = which.step(token)
    for which in (glu_sum, mix_sum):
        while which.halves is None:
            token = which.step(token)
    down_one_g, gate_two_g, up_two_g, gate_one_g, up_one_g, down_two_g, mark = unpack_glu(place, glu_sum.halves, (token,))
    mixout_one_g, mixout_two_g, mixin_one_g, mixin_two_g, *vecs_g, taps_g, pos_in_g, pos_bias_g, pos_out_g = unpack_mixer(
        place, mp, mix_sum.halves, (mark,)
    )

    natural = lambda v: v.transpose(0, 3, 1, 2)
    one = lambda v: natural(v.reshape(2, 4, 48, INNER))
    return (
        result, tokens_grad, vecs_g[0], vecs_g[1], one(mixin_one_g), mixin_two_g, taps_g, vecs_g[4], pos_in_g, pos_bias_g,
        pos_out_g, one(mixout_one_g), mixout_two_g, vecs_g[2], vecs_g[3], natural(gate_one_g), gate_two_g, natural(up_one_g),
        up_two_g, natural(down_one_g.reshape(2, 4, 48, D)), down_two_g,
    )


def solution(mesh):
    return jax.shard_map(
        local,
        mesh=mesh,
        in_specs=(
            P(("dp", "mp"), None),
            P(("dp", "mp")),
            P(("dp", "mp")),
            P(("dp", "mp"), None),
            *[P()] * 13,
            P(None, None, "mp", None),
            P("mp", None, None, None),
            P(None, None, "mp", None),
            P("mp", None, None, None),
            P("mp", None, None, None),
            P(None, None, "mp", None),
        ),
        out_specs=(
            P(("dp", "mp"), None),
            P(("dp", "mp"), None),
            P("mp"),
            P("mp"),
            P("mp", None, None, None),
            P("mp", None, None, None),
            P(None, "mp"),
            P("mp"),
            P(None, "mp"),
            P("mp"),
            P(None, "mp"),
            P("mp", None, None, None),
            P("mp", None, None, None),
            P("mp"),
            P("mp"),
            P(None, None, "mp", None),
            P("mp", None, None, None),
            P(None, None, "mp", None),
            P("mp", None, None, None),
            P("mp", None, None, None),
            P(None, None, "mp", None),
        ),
        check_vma=False,
    )
```
